32 devices in a mesh: fsdp: 4 (over x, core), branch: 8 (over z, y).
Axes of the slice: x: 2, y: 2, z: 4, core: 2. Of those that a mesh axis runs over, the one named last changes fastest.
Arguments:
- hidden: bfloat16 [24, 128, 8192], P('branch', None, 'fsdp')
- parents: int32 [24], replicated, may hold values from -1 to 22, as said below
- lengths: int32 [24], replicated, may hold values from 32 to 128, as said below
- gain: float32 [8192], replicated, may hold values from 0.1 to 1.9
- w_query: bfloat16 [8192, 4096], P('branch', 'fsdp')
- w_key: bfloat16 [8192, 512], P('branch', 'fsdp')
- w_value: bfloat16 [8192, 512], P('branch', 'fsdp'), may hold values from -0.0625 to 0.0625
- query_bias: float32 [4096], P('fsdp'), may hold values from -4 to 4
- key_bias: float32 [512], P('fsdp'), may hold values from -4 to 4
- value_bias: float32 [512], P('fsdp'), may hold values from -4 to 4
Outputs:
- attended: bfloat16 [24, 128, 4096], P('branch', None, 'fsdp')
The draws below stay inside these ranges and needn't reach their ends.
Inputs may be any that keep to these rules, and one draw needn't show every extreme that they name: parents[j] < j, and only block 0 has -1. Blocks k * 3 to k * 3 + 2 form span k. Block 0 of a span k > 0 hangs under one of the first 2 blocks of an earlier span, block 1 of every span under block 0 of that span, the last block of every span under the block before it, so each span is a chain of its three blocks. No block has more than 6 ancestors outside its span, and some block has exactly 6. `lengths`: blocks 0 and 1 of every span are full.
All inputs are finite; a program needn't handle non-finite values.
Results may differ from the reference program's by a relative error of at most 0.0042.
Values may be sent and summed in bfloat16 or wider, within the bound.
No kernel may reach another device: no remote copies, remote signals or barrier semaphores. Data moves between devices by JAX's collectives and lax.ppermute only.
A program may use at most 128 MiB of HBM per device.

```python
import math
import jax
import jax.numpy as jnp
from jax import lax

D = 8192
HD = 128
GROUP = 8
BLK = 128
BLK_DEV = 3
STEMS = 2
KVH = 4
NBLK = 24
LOGB = 3
ANC = 6


def base_keys(key):
    return jax.random.normal(jax.random.fold_in(key, 7), (D, KVH * HD), jnp.float32) * D ** (-0.5)


def draw_w_key(key, part):
    return base_keys(key).astype(jnp.bfloat16)


def draw_w_query(key, part):
    noise = jax.random.normal(jax.random.fold_in(key, 9), (D, KVH, GROUP, HD), jnp.float32) * D ** (-0.5)
    mixed = noise
    return mixed.reshape(D, KVH * GROUP * HD).astype(jnp.bfloat16)


def draw_hidden(key, part):
    noise_key = jax.random.fold_in(key, 21)
    row_key = jax.random.fold_in(key, 22)
    column_key = jax.random.fold_in(key, 23)
    shape = (NBLK, BLK, D)
    values = jax.random.normal(noise_key, shape, jnp.float32)
    row_scale = jnp.exp(jax.random.uniform(row_key, (NBLK, BLK, 1), jnp.float32, 0.0, math.log(10.0)))
    column_scale = jnp.exp(jax.random.uniform(column_key, (D,), jnp.float32, 0.0, math.log(10.0)))
    return (values * row_scale * column_scale).astype(jnp.bfloat16)


def draw_parents(key, part):
    spans = NBLK // BLK_DEV
    span_ids = jnp.arange(spans, dtype=jnp.int32)
    bit_ids = jnp.arange(LOGB, dtype=jnp.int32)
    powers = (2 ** bit_ids).astype(jnp.int32)
    bits_set = span_ids[:, None] // powers[None, :] % 2 == 1
    scores = jax.random.randint(jax.random.fold_in(key, 1), (1, spans, LOGB), 0, 1 << 20) * LOGB + bit_ids
    chosen = jnp.argmax(jnp.where(bits_set[None], scores, -1), -1).astype(jnp.int32)
    parent_span = span_ids[None, :] - powers[chosen]
    cursor = jnp.full((1,), spans - 1, jnp.int32)
    on_chain = jnp.zeros((1, spans), bool)
    for level in range(LOGB):
        on_chain = on_chain | (span_ids[None, :] == cursor[:, None])
        cursor = jnp.take_along_axis(parent_span, jnp.maximum(cursor, 0)[:, None], 1)[:, 0]
    stem_pick = jax.random.randint(jax.random.fold_in(key, 2), (1, spans), 0, STEMS)
    stem_pick = jnp.where(on_chain, STEMS - 1, stem_pick)
    entry = jnp.where(span_ids[None, :] == 0, -1, parent_span * BLK_DEV + stem_pick)
    local_ids = jnp.arange(BLK_DEV, dtype=jnp.int32)
    low = jnp.where(span_ids == 0, 1, 0)[None, :, None]
    pick = jax.random.randint(jax.random.fold_in(key, 3), (1, spans, BLK_DEV), low, local_ids[None, None, :] + 1)
    pick = jnp.where(local_ids[None, None, :] == BLK_DEV - 1, BLK_DEV - 1, pick)
    span_base = (span_ids * BLK_DEV)[None, :, None]
    later = jnp.where(pick == 0, entry[:, :, None], span_base + pick - 1)
    result = jnp.where(local_ids[None, None, :] == 0, entry[:, :, None], jnp.where(local_ids[None, None, :] == 1, span_base, later))
    return result.reshape(NBLK).astype(jnp.int32)


def draw_lengths(key, part):
    drawn = jax.random.randint(jax.random.fold_in(key, 5), (NBLK,), BLK // 4, BLK + 1)
    stem_block = jnp.arange(NBLK, dtype=jnp.int32) % BLK_DEV < STEMS
    return jnp.where(stem_block, BLK, drawn).astype(jnp.int32)


def level_of(key, extent, cuts, low, largest):
    loudness = 1.0
    for dim, shards_of in cuts:
        steps = jax.random.uniform(jax.random.fold_in(jax.random.fold_in(key, 6), dim), (shards_of,), jnp.float32, low / len(cuts), largest / len(cuts))
        loudness = loudness * jnp.repeat(jnp.exp(steps), extent[dim] // shards_of).reshape((-1,) + (1,) * (len(extent) - 1 - dim))
    return loudness


def normal_values(own_key, extent, deviation, reach, shards=(), kind=jnp.bfloat16):
    array = jax.random.normal(own_key, extent, jnp.float32) * deviation
    if len(shards) > 0:
        array = level_of(own_key, extent, shards, -0.22, 0.18) * array
    return jnp.clip(array, min=-reach, max=reach).astype(kind)


def setup_inputs(seed: int = 0) -> dict:
    seeds = jax.random.split(jax.random.key(seed), 11)
    return {
        "hidden": draw_hidden(jax.random.fold_in(seeds[10], 71), 0),
        "parents": draw_parents(jax.random.fold_in(seeds[10], 71), 0),
        "lengths": draw_lengths(jax.random.fold_in(seeds[10], 71), 0),
        "gain": jnp.clip(1.0 + 0.18 * jax.random.normal(seeds[3], (D,), jnp.float32), 0.1, 1.9),
        "w_query": draw_w_query(jax.random.fold_in(seeds[10], 71), 0),
        "w_key": draw_w_key(jax.random.fold_in(seeds[10], 71), 0),
        "w_value": normal_values(seeds[6], (D, KVH * HD), D ** -0.5, 0.0625, ((0, 8), (1, 4))),
        "query_bias": normal_values(seeds[7], (KVH * GROUP * HD,), 1.0, 4.0, ((0, 4),), jnp.float32),
        "key_bias": normal_values(seeds[8], (KVH * HD,), 1.0, 4.0, ((0, 4),), jnp.float32),
        "value_bias": normal_values(seeds[9], (KVH * HD,), 1.0, 4.0, ((0, 4),), jnp.float32),
    }


def rotate(vectors, position):
    half_size = vectors.shape[-1] // 2
    freq_index = jnp.arange(half_size).astype(vectors.dtype)
    freqs = jnp.exp(freq_index * (-2.0 * math.log(1000000.0) / vectors.shape[-1]))
    angles = position.astype(vectors.dtype)[:, None, None] * freqs[None, None, :]
    cosines = jnp.cos(angles)
    sines = jnp.sin(angles)
    front_half = vectors[..., :half_size]
    back_half = vectors[..., half_size:]
    return jnp.concatenate([front_half * cosines - back_half * sines, back_half * cosines + front_half * sines], -1)

def depth_of(parent_row):

    def visit(depths, block):
        parent = parent_row[block]
        value = jnp.where(parent < 0, 0, depths[jnp.maximum(parent, 0)] + 1).astype(jnp.int32)
        return (depths.at[block].set(value), None)
    depths, unused = lax.scan(visit, jnp.zeros((NBLK,), jnp.int32), jnp.arange(NBLK, dtype=jnp.int32))
    return depths

def reference(hidden, parents, lengths, gain, w_query, w_key, w_value, query_bias, key_bias, value_bias):
    parent_row = parents
    length_row = lengths
    tokens = hidden.reshape(NBLK * BLK, D).astype(jnp.float32)
    normed = (tokens * lax.rsqrt(lax.optimization_barrier(jnp.mean(tokens * tokens, -1, keepdims=True)) + 1e-06) * gain).astype(jnp.bfloat16)
    query = jnp.dot(normed, w_query, preferred_element_type=jnp.float32) + query_bias
    key = jnp.dot(normed, w_key, preferred_element_type=jnp.float32) + key_bias
    value = jnp.dot(normed, w_value, preferred_element_type=jnp.float32) + value_bias
    depths = depth_of(parent_row)
    slot_ids = jnp.arange(BLK, dtype=jnp.int32)
    position = (depths[:, None] * BLK + slot_ids[None, :]).reshape(-1)
    rotated_query = rotate(query.reshape(-1, KVH * GROUP, HD), position).astype(jnp.bfloat16).reshape(NBLK, BLK, KVH, GROUP, HD)
    rotated_key = rotate(key.reshape(-1, KVH, HD), position).astype(jnp.bfloat16).reshape(NBLK, BLK, KVH, HD)
    value_bf16 = value.astype(jnp.bfloat16).reshape(NBLK, BLK, KVH, HD)
    chain_len = ANC + BLK_DEV
    scale = HD ** (-0.5)

    def one_block(block):
        chain_ids = []
        cursor = block
        for level in range(chain_len):
            chain_ids.append(cursor)
            cursor = jnp.where(cursor >= 0, parent_row[jnp.maximum(cursor, 0)], -1)
        chain_ids = jnp.stack(chain_ids).astype(jnp.int32)
        safe_ids = jnp.maximum(chain_ids, 0)
        keys_here = rotated_key[safe_ids].reshape(chain_len * BLK, KVH, HD)
        values_here = value_bf16[safe_ids].reshape(chain_len * BLK, KVH, HD)
        live = (chain_ids >= 0)[:, None] & (slot_ids[None, :] < length_row[safe_ids][:, None])
        first_link = (jnp.arange(chain_len) == 0)[None, :, None]
        causal = jnp.logical_not(first_link) | (slot_ids[None, None, :] <= slot_ids[:, None, None])
        visible = (live[None] & causal).reshape(BLK, chain_len * BLK)
        scores = jnp.einsum('tkgh,skh->kgts', rotated_query[block].astype(jnp.float32), keys_here.astype(jnp.float32)) * scale
        scores = jnp.where(visible[None, None], scores, -1e+30)
        row_max = lax.optimization_barrier(jnp.max(scores, -1, keepdims=True))
        exps = jnp.exp(scores - row_max)
        weights = (exps / lax.optimization_barrier(jnp.sum(exps, -1, keepdims=True))).astype(jnp.bfloat16)
        output = jnp.einsum('kgts,skh->tkgh', weights.astype(jnp.float32), values_here.astype(jnp.float32))
        output = jnp.where((slot_ids < length_row[block])[:, None, None, None], output, 0.0)
        return output.reshape(BLK, KVH * GROUP * HD).astype(jnp.bfloat16)
    return lax.map(one_block, jnp.arange(NBLK, dtype=jnp.int32))
```

```python
import functools
import math

import jax
import jax.numpy as jnp
from jax import lax
from jax.experimental import pallas as pl
from jax.experimental.pallas import tpu as pltpu
from jax.sharding import PartitionSpec as P

HD = 128
STEMS = 2
THETA = 1000000.0
NEG = -1e30


def bits_of(count):
    return count.bit_length() - 1


def far_chain(parents_ref, first_block, far_slots):
    cursor = parents_ref[first_block]
    ids = []
    total = jnp.int32(0)
    for level in range(far_slots):
        ids.append(cursor)
        total = total + jnp.where(cursor >= 0, 1, 0)
        above = parents_ref[jnp.maximum(cursor, 0)]
        cursor = jnp.where(cursor >= 0, above, -1)
    return ids, total


def merge(right_ref, left_ref, own, inverse_ref, bias):
    total = own + right_ref[...].astype(jnp.float32) + left_ref[...].astype(jnp.float32)
    inverse = inverse_ref[...]
    scaled = jnp.where(inverse > 0, total * inverse, 0.0)
    return scaled + bias


def turn(vectors, cos, sin):
    half = vectors.shape[-1] // 2
    return vectors * cos + pltpu.roll(vectors, half, 1) * sin


def kv_kernel(
    far_slots, block_len, meta_ref, parents_ref, right_ref, left_ref, own_ref, inverse_ref,
    bias_ref, kv_ref, cos_ref, sin_ref,
):
    tokens = kv_ref.shape[0]
    blocks = meta_ref[2]
    first_block = meta_ref[1] * blocks
    unused, far_total = far_chain(parents_ref, first_block, far_slots)
    rows = lax.broadcasted_iota(jnp.int32, (tokens, HD), 0)
    lanes = lax.broadcasted_iota(jnp.int32, (tokens, HD), 1)
    front = lanes < HD // 2
    pair = jnp.where(front, lanes, lanes - HD // 2).astype(jnp.float32)
    freqs = jnp.exp(pair * (-2.0 * math.log(THETA) / HD))
    angles = (rows + far_total * block_len).astype(jnp.float32) * freqs
    cos = jnp.cos(angles)
    sin = jnp.sin(angles)
    sin = jnp.where(front, -sin, sin)
    cos_ref[...] = cos
    sin_ref[...] = sin
    inverse = inverse_ref[...]
    total = own_ref[0] + right_ref[...].astype(jnp.float32) + left_ref[...].astype(jnp.float32)
    key = jnp.where(inverse > 0, total[:, :HD] * inverse, 0.0) + bias_ref[:, :HD]
    value = jnp.where(inverse > 0, total[:, HD:] * inverse, 0.0) + bias_ref[:, HD:]
    kv_ref[:, :HD] = turn(key, cos, sin).astype(jnp.bfloat16)
    kv_ref[:, HD:] = value.astype(jnp.bfloat16)


def attend_kernel(
    far_slots, blocks, meta_ref, parents_ref, lengths_ref, right_ref, left_ref, own_ref,
    inverse_ref, bias_ref, cos_ref, sin_ref, kv_ref, stems_ref, out_ref, far_key, far_value,
    far_mask,
):
    tokens = kv_ref.shape[0]
    block_len = tokens // blocks
    device = meta_ref[1]
    first_block = device * blocks

    @pl.when(pl.program_id(0) == 0)
    def _():
        ids, unused = far_chain(parents_ref, first_block, far_slots)
        for level in range(far_slots):
            live = ids[level] >= 0
            safe = jnp.maximum(ids[level], 0)
            owner = lax.div(safe, jnp.int32(blocks))
            inner = lax.rem(safe, jnp.int32(blocks))
            where = lax.bitwise_xor(owner, device)
            start = pl.multiple_of(inner * block_len, block_len)
            here = pl.ds(level * block_len, block_len)
            far_key[here, :] = stems_ref[where, pl.ds(start, block_len), :HD]
            far_value[here, :] = stems_ref[where, pl.ds(start, block_len), HD:]
            far_mask[:, here] = jnp.broadcast_to(jnp.where(live, 0.0, NEG), (8, block_len))

    query = merge(right_ref, left_ref, own_ref[0], inverse_ref, bias_ref[...])
    query = turn(query, cos_ref[...], sin_ref[...]).astype(jnp.bfloat16)
    factor = HD ** (-0.5) * math.log2(math.e)
    contract = (((1,), (1,)), ((), ()))
    row = lax.broadcasted_iota(jnp.int32, (block_len, block_len), 0)
    column = lax.broadcasted_iota(jnp.int32, (block_len, block_len), 1)
    for block in range(blocks):
        here = slice(block * block_len, (block + 1) * block_len)
        query_block = query[here]
        far = lax.dot_general(
            query_block, far_key[...], contract, preferred_element_type=jnp.float32
        )
        far = far + far_mask[0:1, :]
        parts = [far]
        for other in range(block + 1):
            near = lax.dot_general(
                query_block,
                kv_ref[other * block_len : (other + 1) * block_len, :HD],
                contract,
                preferred_element_type=jnp.float32,
            )
            if other == block or other >= STEMS:
                seen = column < lengths_ref[first_block + other]
                if other == block:
                    seen = seen & (column <= row)
                near = jnp.where(seen, near, NEG)
            parts.append(near)
        peak = functools.reduce(jnp.maximum, [jnp.max(part, -1, keepdims=True) for part in parts])
        peak = peak * factor
        exps = [jnp.exp2(part * factor - peak) for part in parts]
        total = functools.reduce(jnp.add, [jnp.sum(part, -1, keepdims=True) for part in exps])
        output = jnp.dot(
            exps[0].astype(jnp.bfloat16), far_value[...], preferred_element_type=jnp.float32
        )
        for other in range(block + 1):
            output += jnp.dot(
                exps[1 + other].astype(jnp.bfloat16),
                kv_ref[other * block_len : (other + 1) * block_len, HD:],
                preferred_element_type=jnp.float32,
            )
        output = output / total
        if block >= STEMS:
            output = jnp.where(row[:, :1] < lengths_ref[first_block + block], output, 0.0)
        out_ref[here, :] = output.astype(jnp.bfloat16)


def shards(
    hidden, parents, lengths, gain, w_query, w_key, w_value, query_bias, key_bias, value_bias
):
    blocks, block_len, feature_part = hidden.shape
    tokens = blocks * block_len
    features = gain.shape[0]
    rows = w_query.shape[0]
    columns = w_query.shape[1]
    head_count = columns // HD
    lines = lax.axis_size("fsdp")
    branches = lax.axis_size("branch")
    groups = branches // lines
    far_slots = STEMS * bits_of(branches)
    part = lax.axis_index("fsdp")
    device = lax.axis_index("branch")
    member = device % groups
    level = device // groups
    bf16 = jnp.bfloat16
    f32 = jnp.float32

    def swap(array, axis, bit):
        size = lax.axis_size(axis)
        return lax.ppermute(array, axis, [(i, i ^ bit) for i in range(size)])

    w_kv = jnp.concatenate([w_key, w_value], 1)
    query_chunks = 2
    width = columns // query_chunks
    w_chunks = [w_kv] + [
        lax.slice_in_dim(w_query, c * width, (c + 1) * width, axis=1) for c in range(query_chunks)
    ]
    w_rows = [
        [chunk] + [swap(chunk, "branch", j) for j in range(1, groups)] for chunk in w_chunks
    ]

    raw = hidden.reshape(tokens, feature_part)
    pieces = []
    for j in range(groups):
        start = (member ^ j) * rows
        gain_here = lax.dynamic_slice_in_dim(gain, part * feature_part + start, rows)
        piece = lax.dynamic_slice_in_dim(raw, start, rows, axis=1).astype(f32) * gain_here
        pieces.append(piece.astype(bf16))
    scaled = jnp.concatenate(pieces, 1)

    half_lines = lines // 2
    shift = bits_of(half_lines)

    def landing(z, feature):
        return ((z ^ feature) & 1) * half_lines + (z >> 1)

    exchange = []
    for z in range(lines):
        for g in range(groups):
            for feature in range(lines):
                source = feature * branches + z * groups + g
                target = landing(z, feature) * branches + feature * groups + g
                exchange.append((source, target))
    halves = 2
    span = tokens // halves
    gathered = []
    for h in range(halves):
        sent = lax.slice_in_dim(scaled, h * span, (h + 1) * span, axis=0)
        held = {0: lax.ppermute(sent, ("fsdp", "branch"), exchange)}
        bit = half_lines
        while bit:
            for j in list(held):
                held[j | bit] = swap(held[j], "fsdp", bit)
            bit //= 2

        order = [None] * lines
        for j in range(lines):
            order[((j & (half_lines - 1)) << 1) | (j >> shift)] = held[j]
        gathered.append(jnp.stack(order))
    base = ((part & (half_lines - 1)) << 1) | ((part >> shift) ^ (level & 1))
    everything = jnp.concatenate(gathered, 1).reshape(lines * tokens, feature_part)

    squares = jnp.sum(jnp.square(raw.astype(f32)), -1).reshape(blocks, block_len)
    bit = 1
    while bit < lines:
        squares = squares + swap(squares, "fsdp", bit)
        bit *= 2
    inverse = lax.rsqrt(squares / features + 1e-06).reshape(tokens)
    inverse = jnp.broadcast_to(inverse[:, None], (tokens, HD))

    def product(chunk):
        total = None
        for j in range(groups):
            term = jnp.dot(
                everything[:, j * rows : (j + 1) * rows], chunk[j], preferred_element_type=f32
            )
            total = term if total is None else total + term
        return total.reshape(lines, tokens, -1)

    up = [[((z * groups + g), (z + 1) * groups + g) for z in range(s + 1) for g in range(groups)]
          for s in range(lines - 1)]
    down = [[((lines - 1 - z) * groups + g, (lines - 2 - z) * groups + g)
             for z in range(s + 1) for g in range(groups)] for s in range(lines - 1)]

    def reduce_line(partial):
        def of(target):
            target = jnp.clip(target, 0, lines - 1)
            return lax.dynamic_index_in_dim(partial, target ^ base, 0, keepdims=False)

        right = left = None
        for s in range(lines - 1):
            ahead = of(level + (lines - 1 - s))
            behind = of(level - (lines - 1 - s))
            if s:
                ahead = ahead + right.astype(f32)
                behind = behind + left.astype(f32)
            right = lax.ppermute(ahead.astype(bf16), "branch", up[s])
            left = lax.ppermute(behind.astype(bf16), "branch", down[s])
        return right, left

    meta = jnp.stack([level ^ base, device, jnp.int32(blocks)]).astype(jnp.int32)

    partial = product(w_rows[0])
    right, left = reduce_line(partial)
    kv_width = 2 * HD
    bias = jnp.concatenate([key_bias, value_bias])[None]
    full = lambda *shape: pl.BlockSpec(shape, lambda *unused: (0,) * len(shape))
    kv, cos, sin = pl.pallas_call(
        functools.partial(kv_kernel, far_slots, block_len),
        grid_spec=pltpu.PrefetchScalarGridSpec(
            num_scalar_prefetch=2,
            grid=(1,),
            in_specs=[
                full(tokens, kv_width),
                full(tokens, kv_width),
                pl.BlockSpec((1, tokens, kv_width), lambda i, meta, parents: (meta[0], 0, 0)),
                full(tokens, HD),
                full(1, kv_width),
            ],
            out_specs=[full(tokens, kv_width), full(tokens, HD), full(tokens, HD)],
        ),
        out_shape=[
            jax.ShapeDtypeStruct((tokens, kv_width), bf16),
            jax.ShapeDtypeStruct((tokens, HD), f32),
            jax.ShapeDtypeStruct((tokens, HD), f32),
        ],
        name="finish_kv",
    )(meta, parents, right, left, partial, inverse, bias)

    stems = kv[None, : STEMS * block_len]
    bit = 1
    while bit < branches:
        stems = jnp.concatenate([stems, swap(stems, "branch", bit)], 0)
        bit *= 2

    output = None
    chunk_heads = head_count // query_chunks
    for c in range(query_chunks):
        partial = product(w_rows[1 + c])
        right, left = reduce_line(partial)
        first_head = c * chunk_heads
        in_specs = [
            pl.BlockSpec((tokens, HD), lambda i, *s: (0, i)),
            pl.BlockSpec((tokens, HD), lambda i, *s: (0, i)),
            pl.BlockSpec((1, tokens, HD), lambda i, meta, *s: (meta[0], 0, i)),
            full(tokens, HD),
            pl.BlockSpec((1, HD), lambda i, *s, first_head=first_head: (0, first_head + i)),
            full(tokens, HD),
            full(tokens, HD),
            full(tokens, kv_width),
            full(branches, STEMS * block_len, kv_width),
        ]
        operands = [
            meta, parents, lengths, right, left, partial, inverse, query_bias[None], cos, sin,
            kv, stems,
        ]
        kernel = functools.partial(attend_kernel, far_slots, blocks)
        aliases = {}
        if output is not None:
            in_specs.append(pl.BlockSpec(memory_space=pl.ANY))
            operands.append(output)
            aliases = {len(operands) - 1: 0}
            kernel = functools.partial(with_output, kernel)
        output = pl.pallas_call(
            kernel,
            grid_spec=pltpu.PrefetchScalarGridSpec(
                num_scalar_prefetch=3,
                grid=(chunk_heads,),
                in_specs=in_specs,
                out_specs=pl.BlockSpec(
                    (tokens, HD), lambda i, *s, first_head=first_head: (0, first_head + i)
                ),
                scratch_shapes=[
                    pltpu.VMEM((far_slots * block_len, HD), bf16),
                    pltpu.VMEM((far_slots * block_len, HD), bf16),
                    pltpu.VMEM((8, far_slots * block_len), f32),
                ],
            ),
            out_shape=jax.ShapeDtypeStruct((tokens, columns), bf16),
            input_output_aliases=aliases,
            compiler_params=pltpu.CompilerParams(vmem_limit_bytes=40 * 2**20),
            name="attend",
        )(*operands)
    return output.reshape(blocks, block_len, columns)


def with_output(kernel, *refs):
    kernel(*refs[:12], *refs[13:])


def solution(mesh):
    return jax.shard_map(
        shards,
        mesh=mesh,
        in_specs=(
            P("branch", None, "fsdp"),
            P(),
            P(),
            P(),
            P("branch", "fsdp"),
            P("branch", "fsdp"),
            P("branch", "fsdp"),
            P("fsdp"),
            P("fsdp"),
            P("fsdp"),
        ),
        out_specs=P("branch", None, "fsdp"),
        check_vma=False,
    )
```

```python
import functools
import math

import jax
import jax.numpy as jnp
from jax import lax
from jax.experimental import pallas as pl
from jax.experimental.pallas import tpu as pltpu
from jax.sharding import PartitionSpec as P

HD = 128
STEMS = 2
THETA = 1000000.0
NEG = -1e30


def bits_of(count):
    return count.bit_length() - 1


def tie(array, *others):
    return lax.optimization_barrier((array,) + others)[0]


def far_chain(parents_ref, first_block, far_slots):
    cursor = parents_ref[first_block]
    ids = []
    total = jnp.int32(0)
    for level in range(far_slots):
        ids.append(cursor)
        total = total + jnp.where(cursor >= 0, 1, 0)
        above = parents_ref[jnp.maximum(cursor, 0)]
        cursor = jnp.where(cursor >= 0, above, -1)
    return ids, total


def merge(right_ref, left_ref, own, inverse_ref, bias):
    total = own + right_ref[...].astype(jnp.float32) + left_ref[...].astype(jnp.float32)
    inverse = inverse_ref[...]
    scaled = jnp.where(inverse > 0, total * inverse, 0.0)
    return scaled + bias


def turn(vectors, cos, sin):
    half = vectors.shape[-1] // 2
    return vectors * cos + pltpu.roll(vectors, half, 1) * sin


def kv_kernel(
    far_slots, block_len, meta_ref, parents_ref, right_ref, left_ref, own_ref, inverse_ref,
    bias_ref, kv_ref, cos_ref, sin_ref,
):
    tokens = kv_ref.shape[0]
    blocks = meta_ref[2]
    first_block = meta_ref[1] * blocks
    unused, far_total = far_chain(parents_ref, first_block, far_slots)
    rows = lax.broadcasted_iota(jnp.int32, (tokens, HD), 0)
    lanes = lax.broadcasted_iota(jnp.int32, (tokens, HD), 1)
    front = lanes < HD // 2
    pair = jnp.where(front, lanes, lanes - HD // 2).astype(jnp.float32)
    freqs = jnp.exp(pair * (-2.0 * math.log(THETA) / HD))
    angles = (rows + far_total * block_len).astype(jnp.float32) * freqs
    cos = jnp.cos(angles)
    sin = jnp.sin(angles)
    sin = jnp.where(front, -sin, sin)
    cos_ref[...] = cos
    sin_ref[...] = sin
    inverse = inverse_ref[...]
    total = own_ref[0] + right_ref[...].astype(jnp.float32) + left_ref[...].astype(jnp.float32)
    key = jnp.where(inverse > 0, total[:, :HD] * inverse, 0.0) + bias_ref[:, :HD]
    value = jnp.where(inverse > 0, total[:, HD:] * inverse, 0.0) + bias_ref[:, HD:]
    kv_ref[:, :HD] = turn(key, cos, sin).astype(jnp.bfloat16)
    kv_ref[:, HD:] = value.astype(jnp.bfloat16)


def attend_kernel(
    far_slots, blocks, meta_ref, parents_ref, lengths_ref, right_ref, left_ref, own_ref,
    inverse_ref, bias_ref, cos_ref, sin_ref, kv_ref, stems_ref, out_ref, far_key, far_value,
    far_mask,
):
    tokens = kv_ref.shape[0]
    block_len = tokens // blocks
    device = meta_ref[1]
    first_block = device * blocks

    @pl.when(pl.program_id(0) == 0)
    def _():
        ids, unused = far_chain(parents_ref, first_block, far_slots)
        for level in range(far_slots):
            live = ids[level] >= 0
            safe = jnp.maximum(ids[level], 0)
            owner = lax.div(safe, jnp.int32(blocks))
            inner = lax.rem(safe, jnp.int32(blocks))
            where = lax.bitwise_xor(owner, device)
            start = pl.multiple_of(inner * block_len, block_len)
            here = pl.ds(level * block_len, block_len)
            far_key[here, :] = stems_ref[where, pl.ds(start, block_len), :HD]
            far_value[here, :] = stems_ref[where, pl.ds(start, block_len), HD:]
            far_mask[:, here] = jnp.broadcast_to(jnp.where(live, 0.0, NEG), (8, block_len))

    query = merge(right_ref, left_ref, own_ref[0], inverse_ref, bias_ref[...])
    query = turn(query, cos_ref[...], sin_ref[...]).astype(jnp.bfloat16)
    factor = HD ** (-0.5) * math.log2(math.e)
    contract = (((1,), (1,)), ((), ()))
    row = lax.broadcasted_iota(jnp.int32, (block_len, block_len), 0)
    column = lax.broadcasted_iota(jnp.int32, (block_len, block_len), 1)
    for block in range(blocks):
        here = slice(block * block_len, (block + 1) * block_len)
        query_block = query[here]
        far = lax.dot_general(
            query_block, far_key[...], contract, preferred_element_type=jnp.float32
        )
        far = far + far_mask[0:1, :]
        parts = [far]
        for other in range(block + 1):
            near = lax.dot_general(
                query_block,
                kv_ref[other * block_len : (other + 1) * block_len, :HD],
                contract,
                preferred_element_type=jnp.float32,
            )
            if other == block or other >= STEMS:
                seen = column < lengths_ref[first_block + other]
                if other == block:
                    seen = seen & (column <= row)
                near = jnp.where(seen, near, NEG)
            parts.append(near)
        peak = functools.reduce(jnp.maximum, [jnp.max(part, -1, keepdims=True) for part in parts])
        peak = peak * factor
        exps = [jnp.exp2(part * factor - peak) for part in parts]
        total = functools.reduce(jnp.add, [jnp.sum(part, -1, keepdims=True) for part in exps])
        output = jnp.dot(
            exps[0].astype(jnp.bfloat16), far_value[...], preferred_element_type=jnp.float32
        )
        for other in range(block + 1):
            output += jnp.dot(
                exps[1 + other].astype(jnp.bfloat16),
                kv_ref[other * block_len : (other + 1) * block_len, HD:],
                preferred_element_type=jnp.float32,
            )
        output = output / total
        if block >= STEMS:
            output = jnp.where(row[:, :1] < lengths_ref[first_block + block], output, 0.0)
        out_ref[here, :] = output.astype(jnp.bfloat16)


def shards(
    hidden, parents, lengths, gain, w_query, w_key, w_value, query_bias, key_bias, value_bias
):
    blocks, block_len, feature_part = hidden.shape
    tokens = blocks * block_len
    features = gain.shape[0]
    rows = w_query.shape[0]
    columns = w_query.shape[1]
    head_count = columns // HD
    lines = lax.axis_size("fsdp")
    branches = lax.axis_size("branch")
    groups = branches // lines
    far_slots = STEMS * bits_of(branches)
    part = lax.axis_index("fsdp")
    device = lax.axis_index("branch")
    member = device % groups
    level = device // groups
    bf16 = jnp.bfloat16
    f32 = jnp.float32

    def swap(array, axis, bit):
        size = lax.axis_size(axis)
        return lax.ppermute(array, axis, [(i, i ^ bit) for i in range(size)])

    w_kv = jnp.concatenate([w_key, w_value], 1)
    query_chunks = 2
    width = columns // query_chunks
    w_chunks = [w_kv] + [
        lax.slice_in_dim(w_query, c * width, (c + 1) * width, axis=1) for c in range(query_chunks)
    ]
    w_rows = [
        [chunk] + [swap(chunk, "branch", j) for j in range(1, groups)] for chunk in w_chunks
    ]

    raw = hidden.reshape(tokens, feature_part)
    pieces = []
    for j in range(groups):
        start = (member ^ j) * rows
        gain_here = lax.dynamic_slice_in_dim(gain, part * feature_part + start, rows)
        piece = lax.dynamic_slice_in_dim(raw, start, rows, axis=1).astype(f32) * gain_here
        pieces.append(piece.astype(bf16))
    scaled = jnp.concatenate(pieces, 1)

    squares = jnp.sum(jnp.square(raw.astype(f32)), -1).reshape(blocks, block_len)
    bit = 1
    while bit < lines:
        squares = squares + swap(squares, "fsdp", bit)
        bit *= 2
    inverse = lax.rsqrt(squares / features + 1e-06).reshape(tokens)
    inverse = jnp.broadcast_to(inverse[:, None], (tokens, HD))

    half_lines = lines // 2
    top = bits_of(half_lines)

    def column(z, feature):
        return (z ^ feature) & (half_lines - 1)

    def middle(z, feature):
        return (column(z, feature) << 1) | ((feature >> top) ^ (z & 1))

    def landing(z, feature):
        return (column(z, feature) << 1) | (z >> top)

    first_hop = []
    second_hop = []
    for z in range(lines):
        for g in range(groups):
            for feature in range(lines):
                here = z * groups + g
                there = feature * groups + g
                stop = middle(z, feature) * branches + here
                first_hop.append((feature * branches + here, stop))
                second_hop.append((stop, landing(z, feature) * branches + there))
    axes = ("fsdp", "branch")
    sent = [scaled[h * block_len : (h + 1) * block_len] for h in range(blocks)]
    sent = [lax.ppermute(piece, axes, first_hop) for piece in sent]
    sent[1] = tie(sent[1], w_rows[0][-1])
    sent[2] = tie(sent[2], squares)
    sent = [lax.ppermute(piece, axes, second_hop) for piece in sent]
    held = [{0: piece} for piece in sent]
    held[1][0] = tie(held[1][0], w_rows[1][-1])
    bit = half_lines
    while bit:
        for piece in held:
            for j in list(piece):
                piece[j | bit] = swap(piece[j], "fsdp", bit)
        bit //= 2
        held[-1][0] = tie(held[-1][0], w_rows[-1][-1])
    gathered = []
    for piece in held:
        order = [None] * lines
        for j in range(lines):
            order[((j & 1) << top) | (j >> 1)] = piece[j]
        gathered.append(jnp.stack(order))
    base = ((part & 1) << top) | ((part >> 1) ^ (level & (half_lines - 1)))
    everything = jnp.concatenate(gathered, 1).reshape(lines * tokens, feature_part)

    def product(chunk):
        total = None
        for j in range(groups):
            term = jnp.dot(
                everything[:, j * rows : (j + 1) * rows], chunk[j], preferred_element_type=f32
            )
            total = term if total is None else total + term
        return total.reshape(lines, tokens, -1)

    up = [[((z * groups + g), (z + 1) * groups + g) for z in range(s + 1) for g in range(groups)]
          for s in range(lines - 1)]
    down = [[((lines - 1 - z) * groups + g, (lines - 2 - z) * groups + g)
             for z in range(s + 1) for g in range(groups)] for s in range(lines - 1)]

    def reduce_line(partial):
        def of(target):
            target = jnp.clip(target, 0, lines - 1)
            return lax.dynamic_index_in_dim(partial, target ^ base, 0, keepdims=False)

        right = left = None
        for s in range(lines - 1):
            ahead = of(level + (lines - 1 - s))
            behind = of(level - (lines - 1 - s))
            if s:
                ahead = ahead + right.astype(f32)
                behind = behind + left.astype(f32)
            right = lax.ppermute(ahead.astype(bf16), "branch", up[s])
            left = lax.ppermute(behind.astype(bf16), "branch", down[s])
        return right, left

    meta = jnp.stack([level ^ base, device, jnp.int32(blocks)]).astype(jnp.int32)

    partial = product(w_rows[0])
    right, left = reduce_line(partial)
    kv_width = 2 * HD
    bias = jnp.concatenate([key_bias, value_bias])[None]
    full = lambda *shape: pl.BlockSpec(shape, lambda *unused: (0,) * len(shape))
    kv, cos, sin = pl.pallas_call(
        functools.partial(kv_kernel, far_slots, block_len),
        grid_spec=pltpu.PrefetchScalarGridSpec(
            num_scalar_prefetch=2,
            grid=(1,),
            in_specs=[
                full(tokens, kv_width),
                full(tokens, kv_width),
                pl.BlockSpec((1, tokens, kv_width), lambda i, meta, parents: (meta[0], 0, 0)),
                full(tokens, HD),
                full(1, kv_width),
            ],
            out_specs=[full(tokens, kv_width), full(tokens, HD), full(tokens, HD)],
        ),
        out_shape=[
            jax.ShapeDtypeStruct((tokens, kv_width), bf16),
            jax.ShapeDtypeStruct((tokens, HD), f32),
            jax.ShapeDtypeStruct((tokens, HD), f32),
        ],
        name="finish_kv",
    )(meta, parents, right, left, partial, inverse, bias)

    stems = kv[None, : STEMS * block_len]
    bit = 1
    while bit < branches:
        stems = jnp.concatenate([stems, swap(stems, "branch", bit)], 0)
        bit *= 2

    output = None
    chunk_heads = head_count // query_chunks
    for c in range(query_chunks):
        chunk = w_rows[1 + c]
        chunk[0] = tie(chunk[0], partial)
        partial = product(chunk)
        right, left = reduce_line(partial)
        first_head = c * chunk_heads
        in_specs = [
            pl.BlockSpec((tokens, HD), lambda i, *s: (0, i)),
            pl.BlockSpec((tokens, HD), lambda i, *s: (0, i)),
            pl.BlockSpec((1, tokens, HD), lambda i, meta, *s: (meta[0], 0, i)),
            full(tokens, HD),
            pl.BlockSpec((1, HD), lambda i, *s, first_head=first_head: (0, first_head + i)),
            full(tokens, HD),
            full(tokens, HD),
            full(tokens, kv_width),
            full(branches, STEMS * block_len, kv_width),
        ]
        operands = [
            meta, parents, lengths, right, left, partial, inverse, query_bias[None], cos, sin,
            kv, stems,
        ]
        kernel = functools.partial(attend_kernel, far_slots, blocks)
        aliases = {}
        if output is not None:
            in_specs.append(pl.BlockSpec(memory_space=pl.ANY))
            operands.append(output)
            aliases = {len(operands) - 1: 0}
            kernel = functools.partial(with_output, kernel)
        output = pl.pallas_call(
            kernel,
            grid_spec=pltpu.PrefetchScalarGridSpec(
                num_scalar_prefetch=3,
                grid=(chunk_heads,),
                in_specs=in_specs,
                out_specs=pl.BlockSpec(
                    (tokens, HD), lambda i, *s, first_head=first_head: (0, first_head + i)
                ),
                scratch_shapes=[
                    pltpu.VMEM((far_slots * block_len, HD), bf16),
                    pltpu.VMEM((far_slots * block_len, HD), bf16),
                    pltpu.VMEM((8, far_slots * block_len), f32),
                ],
            ),
            out_shape=jax.ShapeDtypeStruct((tokens, columns), bf16),
            input_output_aliases=aliases,
            compiler_params=pltpu.CompilerParams(vmem_limit_bytes=40 * 2**20),
            name="attend",
        )(*operands)
    return output.reshape(blocks, block_len, columns)


def with_output(kernel, *refs):
    kernel(*refs[:12], *refs[13:])


def solution(mesh):
    return jax.shard_map(
        shards,
        mesh=mesh,
        in_specs=(
            P("branch", None, "fsdp"),
            P(),
            P(),
            P(),
            P("branch", "fsdp"),
            P("branch", "fsdp"),
            P("branch", "fsdp"),
            P("fsdp"),
            P("fsdp"),
            P("fsdp"),
        ),
        out_specs=P("branch", None, "fsdp"),
        check_vma=False,
    )
```

```python
import functools
import math

import jax
import jax.numpy as jnp
from jax import lax
from jax.experimental import pallas as pl
from jax.experimental.pallas import tpu as pltpu
from jax.sharding import PartitionSpec as P

HD = 128
STEMS = 2
THETA = 1000000.0
NEG = -1e30


def bits_of(count):
    return count.bit_length() - 1


def tie(array, *others):
    return lax.optimization_barrier((array,) + others)[0]


def far_chain(parents_ref, first_block, far_slots):
    cursor = parents_ref[first_block]
    ids = []
    total = jnp.int32(0)
    for level in range(far_slots):
        ids.append(cursor)
        total = total + jnp.where(cursor >= 0, 1, 0)
        above = parents_ref[jnp.maximum(cursor, 0)]
        cursor = jnp.where(cursor >= 0, above, -1)
    return ids, total


def add_up(refs, inverse, bias, columns):
    total = refs[0][0, :, columns]
    for ref in refs[1:]:
        total = total + ref[0, :, columns].astype(jnp.float32)
    repeats = total.shape[1] // HD
    inverse = jnp.concatenate([inverse] * repeats, 1)
    return jnp.where(inverse > 0, total * inverse, 0.0) + bias


def turn(vectors, cos, sin):
    half = vectors.shape[-1] // 2
    return vectors * cos + pltpu.roll(vectors, half, 1) * sin


def table_kernel(far_slots, blocks, block_len, device_ref, parents_ref, cos_ref, sin_ref):
    tokens = cos_ref.shape[0]
    unused, far_total = far_chain(parents_ref, device_ref[0] * blocks, far_slots)
    rows = lax.broadcasted_iota(jnp.int32, (tokens, HD), 0)
    lanes = lax.broadcasted_iota(jnp.int32, (tokens, HD), 1)
    front = lanes < HD // 2
    pair = jnp.where(front, lanes, lanes - HD // 2).astype(jnp.float32)
    freqs = jnp.exp(pair * (-2.0 * math.log(THETA) / HD))
    angles = (rows + far_total * block_len).astype(jnp.float32) * freqs
    sin = jnp.sin(angles)
    cos_ref[...] = jnp.cos(angles)
    sin_ref[...] = jnp.where(front, -sin, sin)


def project_kernel(lines, blocks, groups, chunks, place_ref, *refs):
    pieces = refs[: lines * blocks]
    refs = refs[lines * blocks :]
    weights = refs[: groups * chunks]
    send_ref, keep_ref, held, sems = refs[groups * chunks :]
    half = lines // 2
    block_len = held.shape[1] // blocks
    copies = []
    for i in range(lines):
        target = lax.bitwise_xor(jnp.int32(i), place_ref[0])
        slot = jnp.where(target % 2 == 0, half, 0) + target // 2
        for block in range(blocks):
            copy = pltpu.make_async_copy(
                pieces[i * blocks + block],
                held.at[slot, pl.ds(block * block_len, block_len)],
                sems.at[i * blocks + block],
            )
            copy.start()
            copies.append(copy)
    for copy in copies:
        copy.wait()
    rows = weights[0].shape[0]

    def step(slot, carry):
        start = 0
        for chunk in range(chunks):
            total = None
            for g in range(groups):
                term = jnp.dot(
                    held[slot, :, g * rows : (g + 1) * rows],
                    weights[chunk * groups + g][...],
                    preferred_element_type=jnp.float32,
                )
                total = term if total is None else total + term
            stop = start + total.shape[1]

            @pl.when(slot < half)
            def _():
                send_ref[slot, :, start:stop] = total.astype(jnp.bfloat16)

            @pl.when(slot >= half)
            def _():
                keep_ref[slot - half, :, start:stop] = total

            start = stop
        return carry

    lax.fori_loop(0, lines, step, 0)


def kv_kernel(addends, inverse_ref, bias_ref, cos_ref, sin_ref, *refs):
    kv_ref = refs[-1]
    both = add_up(refs[:addends], inverse_ref[...], bias_ref[...], slice(0, 2 * HD))
    kv_ref[:, :HD] = turn(both[:, :HD], cos_ref[...], sin_ref[...]).astype(jnp.bfloat16)
    kv_ref[:, HD:] = both[:, HD:].astype(jnp.bfloat16)


def attend_kernel(
    far_slots, block_len, blocks, heads, first_head, parts, addends, aliased, device_ref,
    parents_ref, lengths_ref, inverse_ref, bias_ref, cos_ref, sin_ref, stems_ref, *refs,
):
    keys = refs[:2]
    refs = refs[2:]
    sums = [refs[p * addends : (p + 1) * addends] for p in range(len(parts))]
    refs = refs[len(parts) * addends + aliased :]
    out_ref, far_key, far_value, far_mask, held, sems = refs
    device = device_ref[0]
    first_block = device * blocks
    ids, unused = far_chain(parents_ref, first_block, far_slots)
    for level in range(far_slots):
        live = ids[level] >= 0
        safe = jnp.maximum(ids[level], 0)
        owner = lax.div(safe, jnp.int32(blocks))
        inner = lax.rem(safe, jnp.int32(blocks))
        where = lax.bitwise_xor(owner, device)
        start = pl.multiple_of(inner * block_len, block_len)
        here = pl.ds(level * block_len, block_len)
        far_key[here, :] = stems_ref[where, pl.ds(start, block_len), :HD]
        far_value[here, :] = stems_ref[where, pl.ds(start, block_len), HD:]
        far_mask[:, here] = jnp.broadcast_to(jnp.where(live, 0.0, NEG), (8, block_len))

    factor = HD ** (-0.5) * math.log2(math.e)
    contract = (((1,), (1,)), ((), ()))
    rows = heads * block_len
    column = lax.broadcasted_iota(jnp.int32, (rows, block_len), 1)
    row = lax.broadcasted_iota(jnp.int32, (rows, block_len), 0) % block_len
    near = [(keys[0], block * block_len) for block in range(STEMS)]
    near += [(keys[1], (block - STEMS) * block_len) for block in range(STEMS, blocks)]
    copies = []
    for p, (first, count, offset) in enumerate(parts):
        for inside in range(count):
            block = first + inside
            here = slice(block * block_len, (block + 1) * block_len)
            mine = slice(inside * block_len, (inside + 1) * block_len)
            total = sums[p][0][0, mine, offset : offset + heads * HD]
            for ref in sums[p][1:]:
                total = total + ref[0, mine, offset : offset + heads * HD].astype(jnp.float32)
            inverse = inverse_ref[here]
            query = []
            for head in range(heads):
                lanes = slice(head * HD, (head + 1) * HD)
                one = jnp.where(inverse > 0, total[:, lanes] * inverse, 0.0)
                one = one + bias_ref[:, lanes]
                query.append(turn(one, cos_ref[here], sin_ref[here]).astype(jnp.bfloat16))
            query = jnp.concatenate(query, 0)
            far = lax.dot_general(
                query, far_key[...], contract, preferred_element_type=jnp.float32
            )
            scores = [far + far_mask[0:1, :]]
            for other in range(block + 1):
                ref, begin = near[other]
                score = lax.dot_general(
                    query,
                    ref[begin : begin + block_len, :HD],
                    contract,
                    preferred_element_type=jnp.float32,
                )
                if other == block or other >= STEMS:
                    seen = column < lengths_ref[first_block + other]
                    if other == block:
                        seen = seen & (column <= row)
                    score = jnp.where(seen, score, NEG)
                scores.append(score)
            peak = functools.reduce(
                jnp.maximum, [jnp.max(score, -1, keepdims=True) for score in scores]
            )
            peak = peak * factor
            exps = [jnp.exp2(score * factor - peak) for score in scores]
            total = functools.reduce(jnp.add, [jnp.sum(e, -1, keepdims=True) for e in exps])
            output = jnp.dot(
                exps[0].astype(jnp.bfloat16), far_value[...], preferred_element_type=jnp.float32
            )
            for other in range(block + 1):
                ref, begin = near[other]
                output += jnp.dot(
                    exps[1 + other].astype(jnp.bfloat16),
                    ref[begin : begin + block_len, HD:],
                    preferred_element_type=jnp.float32,
                )
            output = output / total
            if block >= STEMS:
                output = jnp.where(row < lengths_ref[first_block + block], output, 0.0)
            output = output.astype(jnp.bfloat16)
            for head in range(heads):
                lanes = slice(head * HD, (head + 1) * HD)
                held[here, lanes] = output[head * block_len : (head + 1) * block_len]
            copy = pltpu.make_async_copy(
                held.at[pl.ds(block * block_len, block_len)],
                out_ref.at[pl.ds(block * block_len, block_len), pl.ds(first_head * HD, heads * HD)],
                sems.at[block],
            )
            copy.start()
            copies.append(copy)
    for copy in copies:
        copy.wait()


def shards(
    hidden, parents, lengths, gain, w_query, w_key, w_value, query_bias, key_bias, value_bias
):
    blocks, block_len, feature_part = hidden.shape
    tokens = blocks * block_len
    features = gain.shape[0]
    rows = w_query.shape[0]
    columns = w_query.shape[1]
    head_count = columns // HD
    lines = lax.axis_size("fsdp")
    branches = lax.axis_size("branch")
    groups = branches // lines
    far_slots = STEMS * bits_of(branches)
    part = lax.axis_index("fsdp")
    device = lax.axis_index("branch")
    member = device % groups
    level = device // groups
    bf16 = jnp.bfloat16
    f32 = jnp.float32
    half_lines = lines // 2
    top = bits_of(half_lines)
    kv_width = 2 * HD

    def swap(array, axis, bit):
        size = lax.axis_size(axis)
        return lax.ppermute(array, axis, [(i, i ^ bit) for i in range(size)])

    def spread(index):
        return ((index & 1) << top) | (index >> 1)

    smem = pl.BlockSpec(memory_space=pltpu.SMEM)
    vmem = pl.BlockSpec(memory_space=pltpu.VMEM)
    anywhere = pl.BlockSpec(memory_space=pl.ANY)
    device_id = device.astype(jnp.int32)[None]
    place = spread(part).astype(jnp.int32)[None]

    raw = hidden.reshape(tokens, feature_part)
    pieces = []
    for j in range(groups):
        start = (member ^ j) * rows
        gain_here = lax.dynamic_slice_in_dim(gain, part * feature_part + start, rows)
        piece = lax.dynamic_slice_in_dim(raw, start, rows, axis=1).astype(f32) * gain_here
        pieces.append(piece.astype(bf16))
    scaled = jnp.concatenate(pieces, 1)

    def column(z, feature):
        return (z ^ feature) & (half_lines - 1)

    def middle(z, feature):
        return (column(z, feature) << 1) | ((feature >> top) ^ (z & 1))

    def landing(z, feature):
        return (column(z, feature) << 1) | ((z ^ feature) >> top)

    first_hop = []
    second_hop = []
    for z in range(lines):
        for g in range(groups):
            for feature in range(lines):
                here = z * groups + g
                there = feature * groups + g
                stop = middle(z, feature) * branches + here
                first_hop.append((feature * branches + here, stop))
                second_hop.append((stop, landing(z, feature) * branches + there))
    axes = ("fsdp", "branch")
    sent = [scaled[h * block_len : (h + 1) * block_len] for h in range(blocks)]
    sent = [lax.ppermute(piece, axes, first_hop) for piece in sent]

    head_cuts = [0, (5 * head_count + 7) // 8, head_count]
    w_rows = []
    w_chunks = [jnp.concatenate([w_key, w_value], 1)] + [
        lax.slice_in_dim(w_query, low * HD, high * HD, axis=1)
        for low, high in zip(head_cuts, head_cuts[1:])
    ]
    waits = [None, sent[0], None]
    for chunk, wait in zip(w_chunks, waits):
        outgoing = chunk if wait is None else tie(chunk, wait)
        if len(w_rows) == 2:
            outgoing = tie(chunk, w_rows[0][-1])
        w_rows.append([chunk] + [swap(outgoing, "branch", j) for j in range(1, groups)])

    sent = [lax.ppermute(piece, axes, second_hop) for piece in sent]
    held = [{0: piece} for piece in sent]
    bit = half_lines
    while bit:
        for piece in held:
            for j in list(piece):
                piece[j | bit] = swap(piece[j], "fsdp", bit)
        bit //= 2
    held = [[piece[j] for j in sorted(piece, key=spread)] for piece in held]

    squares = jnp.sum(jnp.square(raw.astype(f32)), -1).reshape(blocks, block_len)
    bit = 1
    while bit < lines:
        squares = squares + swap(squares, "fsdp", bit)
        bit *= 2
    inverse = lax.rsqrt(squares / features + 1e-06).reshape(tokens)
    inverse = jnp.broadcast_to(inverse[:, None], (tokens, HD))

    cos, sin = pl.pallas_call(
        functools.partial(table_kernel, far_slots, blocks, block_len),
        in_specs=[smem, smem],
        out_specs=[vmem, vmem],
        out_shape=[jax.ShapeDtypeStruct((tokens, HD), f32)] * 2,
        name="tables",
    )(device_id, parents)

    order = [None]

    def project(which, chunks):
        count = len(which)
        length = count * block_len
        weights = [w for chunk in chunks for w in w_rows[chunk]]
        width = sum(w_rows[chunk][0].shape[1] for chunk in chunks)
        operands = [held[block][i] for i in range(lines) for block in which]
        if order[0] is not None:
            weights[0] = tie(weights[0], order[0])
        flops = 2 * lines * length * feature_part * width
        send, keep = pl.pallas_call(
            functools.partial(project_kernel, lines, count, groups, len(chunks)),
            in_specs=[smem] + [anywhere] * len(operands) + [vmem] * len(weights),
            out_specs=[vmem, vmem],
            out_shape=[
                jax.ShapeDtypeStruct((half_lines, length, width), bf16),
                jax.ShapeDtypeStruct((half_lines, length, width), f32),
            ],
            scratch_shapes=[
                pltpu.VMEM((lines, length, feature_part), bf16),
                pltpu.SemaphoreType.DMA((len(operands),)),
            ],
            compiler_params=pltpu.CompilerParams(vmem_limit_bytes=32 * 2**20),
            cost_estimate=pl.CostEstimate(
                flops=flops, bytes_accessed=2 * lines * length * feature_part, transcendentals=0
            ),
            name="project",
        )(place, *operands, *weights)
        order[0] = send
        return send, keep

    def halve(send, keep):
        addends = [keep]
        total = keep
        bit = 1
        while bit < lines:
            came = swap(send, "branch", bit * groups)
            addends.append(came)
            bit *= 2
            if bit < lines:
                total = total + came.astype(f32)
                send = total[1::2].astype(bf16)
                total = total[0::2]
        return addends

    addend_count = 1 + bits_of(lines)

    def lead(array):
        return pl.BlockSpec((1,) + array.shape[1:], lambda i: (0, 0, 0))

    def whole(array):
        return pl.BlockSpec(array.shape, lambda i: (0,) * array.ndim)

    kv_bias = jnp.concatenate([key_bias, value_bias])[None]

    def finish_kv(addends, first, count):
        low, high = first * block_len, (first + count) * block_len
        operands = [inverse[low:high], kv_bias, cos[low:high], sin[low:high]]
        return pl.pallas_call(
            functools.partial(kv_kernel, addend_count),
            grid=(1,),
            in_specs=[whole(x) for x in operands] + [lead(x) for x in addends],
            out_specs=pl.BlockSpec((high - low, kv_width), lambda i: (0, 0)),
            out_shape=jax.ShapeDtypeStruct((high - low, kv_width), bf16),
            compiler_params=pltpu.CompilerParams(vmem_limit_bytes=16 * 2**20),
            name="finish_kv",
        )(*operands, *addends)

    early = list(range(STEMS))
    late = list(range(STEMS, blocks))
    first_sums = project(early, [0])
    second_sums = project(early, [1])
    first_sums = halve(*first_sums)
    stem_kv = finish_kv(first_sums, 0, STEMS)
    second_sums = halve(*second_sums)
    third_sums = halve(*project(late, [0, 1]))
    late_kv = finish_kv(third_sums, STEMS, blocks - STEMS)
    fourth_sums = halve(*project(early + late, [2]))

    stems = stem_kv[None]
    bit = 1
    while bit < branches:
        stems = jnp.concatenate([stems, swap(stems, "branch", bit)], 0)
        bit *= 2

    def attend(heads, first_head, parts, sums, output):
        operands = [
            inverse, query_bias[None, first_head * HD : (first_head + heads) * HD], cos, sin,
            stems, stem_kv, late_kv,
        ]
        in_specs = [smem] * 3 + [whole(x) for x in operands]
        for addends in sums:
            operands += addends
            in_specs += [lead(x) for x in addends]
        aliases = {}
        if output is not None:
            aliases = {3 + len(operands): 0}
            operands.append(output)
            in_specs.append(anywhere)
        kernel = functools.partial(
            attend_kernel, far_slots, block_len, blocks, heads, first_head, parts, addend_count,
            len(aliases),
        )
        keys = (far_slots * len(parts) + blocks) * block_len
        return pl.pallas_call(
            kernel,
            grid=(1,),
            in_specs=in_specs,
            out_specs=anywhere,
            scratch_shapes=[
                pltpu.VMEM((far_slots * block_len, HD), bf16),
                pltpu.VMEM((far_slots * block_len, HD), bf16),
                pltpu.VMEM((8, far_slots * block_len), f32),
                pltpu.VMEM((tokens, heads * HD), bf16),
                pltpu.SemaphoreType.DMA((blocks,)),
            ],
            out_shape=jax.ShapeDtypeStruct((tokens, columns), bf16),
            input_output_aliases=aliases,
            compiler_params=pltpu.CompilerParams(vmem_limit_bytes=40 * 2**20),
            cost_estimate=pl.CostEstimate(
                flops=4 * tokens * heads * keys * HD,
                bytes_accessed=2 * tokens * heads * HD,
                transcendentals=tokens * heads * keys,
            ),
            name="attend",
        )(device_id, parents, lengths, *operands)

    output = attend(
        head_cuts[1], 0, [(0, STEMS, 0), (STEMS, blocks - STEMS, kv_width)],
        [second_sums, third_sums], None,
    )
    output = attend(
        head_count - head_cuts[1], head_cuts[1], [(0, blocks, 0)], [fourth_sums], output
    )
    return output.reshape(blocks, block_len, columns)


def solution(mesh):
    return jax.shard_map(
        shards,
        mesh=mesh,
        in_specs=(
            P("branch", None, "fsdp"),
            P(),
            P(),
            P(),
            P("branch", "fsdp"),
            P("branch", "fsdp"),
            P("branch", "fsdp"),
            P("fsdp"),
            P("fsdp"),
            P("fsdp"),
        ),
        out_specs=P("branch", None, "fsdp"),
        check_vma=False,
    )
```

```python
import functools
import math

import jax
import jax.numpy as jnp
from jax import lax
from jax.experimental import pallas as pl
from jax.experimental.pallas import tpu as pltpu
from jax.sharding import PartitionSpec as P

HD = 128
STEMS = 2
THETA = 1000000.0
NEG = -1e30


def bits_of(count):
    return count.bit_length() - 1


def tie(array, *others):
    return lax.optimization_barrier((array,) + others)[0]


def far_chain(parents_ref, first_block, far_slots):
    cursor = parents_ref[first_block]
    ids = []
    total = jnp.int32(0)
    for level in range(far_slots):
        ids.append(cursor)
        total = total + jnp.where(cursor >= 0, 1, 0)
        above = parents_ref[jnp.maximum(cursor, 0)]
        cursor = jnp.where(cursor >= 0, above, -1)
    return ids, total


def add_up(refs, inverse, bias, columns):
    total = refs[0][0, :, columns]
    for ref in refs[1:]:
        total = total + ref[0, :, columns].astype(jnp.float32)
    repeats = total.shape[1] // HD
    inverse = jnp.concatenate([inverse] * repeats, 1)
    return jnp.where(inverse > 0, total * inverse, 0.0) + bias


def turn(vectors, cos, sin):
    half = vectors.shape[-1] // 2
    return vectors * cos + pltpu.roll(vectors, half, 1) * sin


def table_kernel(far_slots, blocks, block_len, device_ref, parents_ref, cos_ref, sin_ref):
    tokens = cos_ref.shape[0]
    unused, far_total = far_chain(parents_ref, device_ref[0] * blocks, far_slots)
    rows = lax.broadcasted_iota(jnp.int32, (tokens, HD), 0)
    lanes = lax.broadcasted_iota(jnp.int32, (tokens, HD), 1)
    front = lanes < HD // 2
    pair = jnp.where(front, lanes, lanes - HD // 2).astype(jnp.float32)
    freqs = jnp.exp(pair * (-2.0 * math.log(THETA) / HD))
    angles = (rows + far_total * block_len).astype(jnp.float32) * freqs
    sin = jnp.sin(angles)
    cos_ref[...] = jnp.cos(angles)
    sin_ref[...] = jnp.where(front, -sin, sin)


def project_kernel(lines, blocks, chunks, place_ref, *refs):
    pieces = refs[: lines * blocks]
    weights = refs[lines * blocks : lines * blocks + chunks]
    send_ref, keep_ref, held, sems = refs[lines * blocks + chunks :]
    half = lines // 2
    block_len = pieces[0].shape[0]
    copies = []
    for i in range(lines):
        target = lax.bitwise_xor(jnp.int32(i), place_ref[0])
        slot = jnp.where(target % 2 == 0, half, 0) + target // 2
        for block in range(blocks):
            start = pl.multiple_of((slot * blocks + block) * block_len, block_len)
            copy = pltpu.make_async_copy(
                pieces[i * blocks + block],
                held.at[pl.ds(start, block_len)],
                sems.at[i * blocks + block],
            )
            copy.start()
            copies.append(copy)
    for copy in copies:
        copy.wait()
    middle = held.shape[0] // 2
    start = 0
    for weight in weights:
        stop = start + weight.shape[1]
        send_ref[:, start:stop] = jnp.dot(
            held[:middle], weight[...], preferred_element_type=jnp.float32
        ).astype(jnp.bfloat16)
        keep_ref[:, start:stop] = jnp.dot(
            held[middle:], weight[...], preferred_element_type=jnp.float32
        )
        start = stop


def kv_kernel(addends, inverse_ref, bias_ref, cos_ref, sin_ref, *refs):
    kv_ref = refs[-1]
    both = add_up(refs[:addends], inverse_ref[...], bias_ref[...], slice(0, 2 * HD))
    kv_ref[:, :HD] = turn(both[:, :HD], cos_ref[...], sin_ref[...]).astype(jnp.bfloat16)
    kv_ref[:, HD:] = both[:, HD:].astype(jnp.bfloat16)


def attend_kernel(
    far_slots, block_len, blocks, heads, first_head, parts, addends, aliased, device_ref,
    parents_ref, lengths_ref, inverse_ref, bias_ref, cos_ref, sin_ref, stems_ref, *refs,
):
    keys = refs[:2]
    refs = refs[2:]
    sums = [refs[p * addends : (p + 1) * addends] for p in range(len(parts))]
    refs = refs[len(parts) * addends + aliased :]
    out_ref, far_key, far_value, far_mask, held, sems = refs
    device = device_ref[0]
    first_block = device * blocks
    ids, unused = far_chain(parents_ref, first_block, far_slots)
    for level in range(far_slots):
        live = ids[level] >= 0
        safe = jnp.maximum(ids[level], 0)
        owner = lax.div(safe, jnp.int32(blocks))
        inner = lax.rem(safe, jnp.int32(blocks))
        where = lax.bitwise_xor(owner, device)
        start = pl.multiple_of(inner * block_len, block_len)
        here = pl.ds(level * block_len, block_len)
        far_key[here, :] = stems_ref[where, pl.ds(start, block_len), :HD]
        far_value[here, :] = stems_ref[where, pl.ds(start, block_len), HD:]
        far_mask[:, here] = jnp.broadcast_to(jnp.where(live, 0.0, NEG), (8, block_len))

    factor = HD ** (-0.5) * math.log2(math.e)
    contract = (((1,), (1,)), ((), ()))
    rows = heads * block_len
    column = lax.broadcasted_iota(jnp.int32, (rows, block_len), 1)
    row = lax.broadcasted_iota(jnp.int32, (rows, block_len), 0) % block_len
    near = [(keys[0], block * block_len) for block in range(STEMS)]
    near += [(keys[1], (block - STEMS) * block_len) for block in range(STEMS, blocks)]
    copies = []
    for p, (first, count, offset) in enumerate(parts):
        for inside in range(count):
            block = first + inside
            here = slice(block * block_len, (block + 1) * block_len)
            mine = slice(inside * block_len, (inside + 1) * block_len)
            total = sums[p][0][0, mine, offset : offset + heads * HD]
            for ref in sums[p][1:]:
                total = total + ref[0, mine, offset : offset + heads * HD].astype(jnp.float32)
            inverse = inverse_ref[here]
            query = []
            for head in range(heads):
                lanes = slice(head * HD, (head + 1) * HD)
                one = jnp.where(inverse > 0, total[:, lanes] * inverse, 0.0)
                one = one + bias_ref[:, lanes]
                query.append(turn(one, cos_ref[here], sin_ref[here]).astype(jnp.bfloat16))
            query = jnp.concatenate(query, 0)
            far = lax.dot_general(
                query, far_key[...], contract, preferred_element_type=jnp.float32
            )
            scores = [far + far_mask[0:1, :]]
            for other in range(block + 1):
                ref, begin = near[other]
                score = lax.dot_general(
                    query,
                    ref[begin : begin + block_len, :HD],
                    contract,
                    preferred_element_type=jnp.float32,
                )
                if other == block or other >= STEMS:
                    seen = column < lengths_ref[first_block + other]
                    if other == block:
                        seen = seen & (column <= row)
                    score = jnp.where(seen, score, NEG)
                scores.append(score)
            peak = functools.reduce(
                jnp.maximum, [jnp.max(score, -1, keepdims=True) for score in scores]
            )
            peak = peak * factor
            exps = [jnp.exp2(score * factor - peak) for score in scores]
            total = functools.reduce(jnp.add, [jnp.sum(e, -1, keepdims=True) for e in exps])
            output = jnp.dot(
                exps[0].astype(jnp.bfloat16), far_value[...], preferred_element_type=jnp.float32
            )
            for other in range(block + 1):
                ref, begin = near[other]
                output += jnp.dot(
                    exps[1 + other].astype(jnp.bfloat16),
                    ref[begin : begin + block_len, HD:],
                    preferred_element_type=jnp.float32,
                )
            output = output / total
            if block >= STEMS:
                output = jnp.where(row < lengths_ref[first_block + block], output, 0.0)
            output = output.astype(jnp.bfloat16)
            for head in range(heads):
                lanes = slice(head * HD, (head + 1) * HD)
                held[here, lanes] = output[head * block_len : (head + 1) * block_len]
            copy = pltpu.make_async_copy(
                held.at[pl.ds(block * block_len, block_len)],
                out_ref.at[pl.ds(block * block_len, block_len), pl.ds(first_head * HD, heads * HD)],
                sems.at[block],
            )
            copy.start()
            copies.append(copy)
    for copy in copies:
        copy.wait()


def shards(
    hidden, parents, lengths, gain, w_query, w_key, w_value, query_bias, key_bias, value_bias
):
    blocks, block_len, feature_part = hidden.shape
    tokens = blocks * block_len
    features = gain.shape[0]
    rows = w_query.shape[0]
    columns = w_query.shape[1]
    head_count = columns // HD
    lines = lax.axis_size("fsdp")
    branches = lax.axis_size("branch")
    groups = branches // lines
    far_slots = STEMS * bits_of(branches)
    part = lax.axis_index("fsdp")
    device = lax.axis_index("branch")
    bf16 = jnp.bfloat16
    f32 = jnp.float32
    half_lines = lines // 2
    top = bits_of(half_lines)
    kv_width = 2 * HD

    def swap(array, axis, bit):
        size = lax.axis_size(axis)
        return lax.ppermute(array, axis, [(i, i ^ bit) for i in range(size)])

    def spread(index):
        return ((index & 1) << top) | (index >> 1)

    smem = pl.BlockSpec(memory_space=pltpu.SMEM)
    vmem = pl.BlockSpec(memory_space=pltpu.VMEM)
    anywhere = pl.BlockSpec(memory_space=pl.ANY)
    device_id = device.astype(jnp.int32)[None]
    place = spread(part).astype(jnp.int32)[None]

    raw = hidden.reshape(tokens, feature_part)
    gain_part = lax.dynamic_slice_in_dim(gain, part * feature_part, feature_part)

    def column(z, feature):
        return (z ^ feature) & (half_lines - 1)

    def middle(z, feature):
        return (column(z, feature) << 1) | ((feature >> top) ^ (z & 1))

    def landing(z, feature):
        return (column(z, feature) << 1) | ((z ^ feature) >> top)

    first_hop = []
    second_hop = []
    for z in range(lines):
        for g in range(groups):
            for feature in range(lines):
                here = z * groups + g
                there = feature * groups + g
                stop = middle(z, feature) * branches + here
                first_hop.append((feature * branches + here, stop))
                second_hop.append((stop, landing(z, feature) * branches + there))
    axes = ("fsdp", "branch")
    first_sent = (raw[:block_len].astype(f32) * gain_part).astype(bf16)
    rest_sent = tie(raw, first_sent)[block_len:]
    rest_sent = (rest_sent.astype(f32) * gain_part).astype(bf16)
    first_sent = lax.ppermute(first_sent, axes, first_hop)
    rest_sent = lax.ppermute(rest_sent, axes, first_hop)
    sent = [first_sent] + [
        rest_sent[i * block_len : (i + 1) * block_len] for i in range(blocks - 1)
    ]

    head_cuts = [0, (5 * head_count + 7) // 8, head_count]
    w_chunks = [jnp.concatenate([w_key, w_value], 1)] + [
        lax.slice_in_dim(w_query, low * HD, high * HD, axis=1)
        for low, high in zip(head_cuts, head_cuts[1:])
    ]
    teams = [[z * groups + g for g in range(groups)] for z in range(lines)]
    w_rows = [
        lax.all_gather(chunk, "branch", axis_index_groups=teams, axis=0, tiled=True)
        for chunk in w_chunks
    ]

    squares = jnp.sum(jnp.square(raw.astype(f32)), -1).reshape(blocks, block_len)
    bit = 1
    while bit < lines:
        squares = squares + swap(squares, "fsdp", bit)
        bit *= 2
    inverse = lax.rsqrt(squares / features + 1e-06).reshape(tokens)
    inverse = jnp.broadcast_to(inverse[:, None], (tokens, HD))

    cos, sin = pl.pallas_call(
        functools.partial(table_kernel, far_slots, blocks, block_len),
        in_specs=[smem, smem],
        out_specs=[vmem, vmem],
        out_shape=[jax.ShapeDtypeStruct((tokens, HD), f32)] * 2,
        name="tables",
    )(device_id, parents)

    sent[0] = tie(sent[0], cos, sin, *w_chunks)
    sent = [lax.ppermute(piece, axes, second_hop) for piece in sent]
    held = [{0: piece} for piece in sent]
    bit = half_lines
    while bit:
        for piece in held:
            for j in list(piece):
                piece[j | bit] = swap(piece[j], "fsdp", bit)
        bit //= 2
    held = [[piece[j] for j in sorted(piece, key=spread)] for piece in held]

    order = [None]

    def project(which, chunks):
        count = len(which)
        length = count * block_len
        weights = [w_rows[chunk] for chunk in chunks]
        width = sum(w.shape[1] for w in weights)
        operands = [held[block][i] for i in range(lines) for block in which]
        if order[0] is not None:
            weights[0] = tie(weights[0], order[0])
        flops = 2 * lines * length * feature_part * width
        send, keep = pl.pallas_call(
            functools.partial(project_kernel, lines, count, len(chunks)),
            in_specs=[smem] + [anywhere] * len(operands) + [vmem] * len(weights),
            out_specs=[vmem, vmem],
            out_shape=[
                jax.ShapeDtypeStruct((half_lines * length, width), bf16),
                jax.ShapeDtypeStruct((half_lines * length, width), f32),
            ],
            scratch_shapes=[
                pltpu.VMEM((lines * length, feature_part), bf16),
                pltpu.SemaphoreType.DMA((len(operands),)),
            ],
            compiler_params=pltpu.CompilerParams(vmem_limit_bytes=32 * 2**20),
            cost_estimate=pl.CostEstimate(
                flops=flops, bytes_accessed=2 * lines * length * feature_part, transcendentals=0
            ),
            name="project",
        )(place, *operands, *weights)
        order[0] = send
        return send.reshape(half_lines, length, width), keep.reshape(half_lines, length, width)

    def halve(send, keep):
        addends = [keep]
        total = keep
        bit = 1
        while bit < lines:
            came = swap(send, "branch", bit * groups)
            addends.append(came)
            bit *= 2
            if bit < lines:
                total = total + came.astype(f32)
                send = total[1::2].astype(bf16)
                total = total[0::2]
        return addends

    addend_count = 1 + bits_of(lines)

    def lead(array):
        return pl.BlockSpec((1,) + array.shape[1:], lambda i: (0, 0, 0))

    def whole(array):
        return pl.BlockSpec(array.shape, lambda i: (0,) * array.ndim)

    kv_bias = jnp.concatenate([key_bias, value_bias])[None]

    def finish_kv(addends, first, count):
        low, high = first * block_len, (first + count) * block_len
        operands = [inverse[low:high], kv_bias, cos[low:high], sin[low:high]]
        return pl.pallas_call(
            functools.partial(kv_kernel, addend_count),
            grid=(1,),
            in_specs=[whole(x) for x in operands] + [lead(x) for x in addends],
            out_specs=pl.BlockSpec((high - low, kv_width), lambda i: (0, 0)),
            out_shape=jax.ShapeDtypeStruct((high - low, kv_width), bf16),
            compiler_params=pltpu.CompilerParams(vmem_limit_bytes=16 * 2**20),
            name="finish_kv",
        )(*operands, *addends)

    early = list(range(STEMS))
    late = list(range(STEMS, blocks))
    first_sums = project(early, [0])
    second_sums = project(early, [1])
    first_sums = halve(*first_sums)
    stem_kv = finish_kv(first_sums, 0, STEMS)
    second_sums = halve(*second_sums)
    third_sums = halve(*project(late, [0, 1]))
    late_kv = finish_kv(third_sums, STEMS, blocks - STEMS)
    fourth_sums = halve(*project(early + late, [2]))

    stems = stem_kv[None]
    bit = 1
    while bit < branches:
        stems = jnp.concatenate([stems, swap(stems, "branch", bit)], 0)
        bit *= 2

    def attend(heads, first_head, parts, sums, output):
        operands = [
            inverse, query_bias[None, first_head * HD : (first_head + heads) * HD], cos, sin,
            stems, stem_kv, late_kv,
        ]
        in_specs = [smem] * 3 + [whole(x) for x in operands]
        for addends in sums:
            operands += addends
            in_specs += [lead(x) for x in addends]
        aliases = {}
        if output is not None:
            aliases = {3 + len(operands): 0}
            operands.append(output)
            in_specs.append(anywhere)
        kernel = functools.partial(
            attend_kernel, far_slots, block_len, blocks, heads, first_head, parts, addend_count,
            len(aliases),
        )
        keys = (far_slots * len(parts) + blocks) * block_len
        return pl.pallas_call(
            kernel,
            grid=(1,),
            in_specs=in_specs,
            out_specs=anywhere,
            scratch_shapes=[
                pltpu.VMEM((far_slots * block_len, HD), bf16),
                pltpu.VMEM((far_slots * block_len, HD), bf16),
                pltpu.VMEM((8, far_slots * block_len), f32),
                pltpu.VMEM((tokens, heads * HD), bf16),
                pltpu.SemaphoreType.DMA((blocks,)),
            ],
            out_shape=jax.ShapeDtypeStruct((tokens, columns), bf16),
            input_output_aliases=aliases,
            compiler_params=pltpu.CompilerParams(vmem_limit_bytes=40 * 2**20),
            cost_estimate=pl.CostEstimate(
                flops=4 * tokens * heads * keys * HD,
                bytes_accessed=2 * tokens * heads * HD,
                transcendentals=tokens * heads * keys,
            ),
            name="attend",
        )(device_id, parents, lengths, *operands)

    output = attend(
        head_cuts[1], 0, [(0, STEMS, 0), (STEMS, blocks - STEMS, kv_width)],
        [second_sums, third_sums], None,
    )
    output = attend(
        head_count - head_cuts[1], head_cuts[1], [(0, blocks, 0)], [fourth_sums], output
    )
    return output.reshape(blocks, block_len, columns)


def solution(mesh):
    return jax.shard_map(
        shards,
        mesh=mesh,
        in_specs=(
            P("branch", None, "fsdp"),
            P(),
            P(),
            P(),
            P("branch", "fsdp"),
            P("branch", "fsdp"),
            P("branch", "fsdp"),
            P("fsdp"),
            P("fsdp"),
            P("fsdp"),
        ),
        out_specs=P("branch", None, "fsdp"),
        check_vma=False,
    )
```

```python
import functools
import math

import jax
import jax.numpy as jnp
from jax import lax
from jax.experimental import pallas as pl
from jax.experimental.pallas import tpu as pltpu
from jax.sharding import PartitionSpec as P

HD = 128
STEMS = 2
THETA = 1000000.0
NEG = -1e30


def bits_of(count):
    return count.bit_length() - 1


def tie(array, *others):
    return lax.optimization_barrier((array,) + others)[0]


def far_chain(parents_ref, first_block, far_slots):
    cursor = parents_ref[first_block]
    ids = []
    total = jnp.int32(0)
    for level in range(far_slots):
        ids.append(cursor)
        total = total + jnp.where(cursor >= 0, 1, 0)
        above = parents_ref[jnp.maximum(cursor, 0)]
        cursor = jnp.where(cursor >= 0, above, -1)
    return ids, total


def add_up(refs, inverse, bias, columns):
    total = refs[0][0, :, columns]
    for ref in refs[1:]:
        total = total + ref[0, :, columns].astype(jnp.float32)
    repeats = total.shape[1] // HD
    inverse = jnp.concatenate([inverse] * repeats, 1)
    return jnp.where(inverse > 0, total * inverse, 0.0) + bias


def turn(vectors, cos, sin):
    half = vectors.shape[-1] // 2
    return vectors * cos + pltpu.roll(vectors, half, 1) * sin


def table_kernel(far_slots, blocks, block_len, device_ref, parents_ref, cos_ref, sin_ref):
    tokens = cos_ref.shape[0]
    unused, far_total = far_chain(parents_ref, device_ref[0] * blocks, far_slots)
    rows = lax.broadcasted_iota(jnp.int32, (tokens, HD), 0)
    lanes = lax.broadcasted_iota(jnp.int32, (tokens, HD), 1)
    front = lanes < HD // 2
    pair = jnp.where(front, lanes, lanes - HD // 2).astype(jnp.float32)
    freqs = jnp.exp(pair * (-2.0 * math.log(THETA) / HD))
    angles = (rows + far_total * block_len).astype(jnp.float32) * freqs
    sin = jnp.sin(angles)
    cos_ref[...] = jnp.cos(angles)
    sin_ref[...] = jnp.where(front, -sin, sin)


def project_kernel(lines, blocks, groups, place_ref, *refs):
    pieces = refs[: lines * blocks]
    send_ref, keep_ref, held, weight, sems = refs[-5:]
    weights = refs[lines * blocks : -5]
    half = lines // 2
    block_len = pieces[0].shape[0]
    rows = weights[0].shape[0]
    copies = []
    start = 0
    for w, ref in enumerate(weights):
        member = lax.bitwise_xor(place_ref[1], jnp.int32(w % groups))
        width = ref.shape[1]
        there = weight.at[pl.ds(pl.multiple_of(member * rows, rows), rows), pl.ds(start, width)]
        copies.append(pltpu.make_async_copy(ref, there, sems.at[w]))
        if w % groups == groups - 1:
            start += width
    for i in range(lines):
        target = lax.bitwise_xor(jnp.int32(i), place_ref[0])
        slot = jnp.where(target % 2 == 0, half, 0) + target // 2
        for block in range(blocks):
            begin = pl.multiple_of((slot * blocks + block) * block_len, block_len)
            n = i * blocks + block
            there = held.at[pl.ds(begin, block_len)]
            copies.append(pltpu.make_async_copy(pieces[n], there, sems.at[len(weights) + n]))
    for copy in copies:
        copy.start()
    for copy in copies:
        copy.wait()
    middle = held.shape[0] // 2
    send_ref[...] = jnp.dot(
        held[:middle], weight[...], preferred_element_type=jnp.float32
    ).astype(jnp.bfloat16)
    keep_ref[...] = jnp.dot(held[middle:], weight[...], preferred_element_type=jnp.float32)


def kv_kernel(addends, inverse_ref, bias_ref, cos_ref, sin_ref, *refs):
    kv_ref = refs[-1]
    both = add_up(refs[:addends], inverse_ref[...], bias_ref[...], slice(0, 2 * HD))
    kv_ref[:, :HD] = turn(both[:, :HD], cos_ref[...], sin_ref[...]).astype(jnp.bfloat16)
    kv_ref[:, HD:] = both[:, HD:].astype(jnp.bfloat16)


def attend_kernel(
    far_slots, block_len, blocks, heads, first_head, parts, addends, aliased, tour, device_ref,
    parents_ref, lengths_ref, inverse_ref, bias_ref, cos_ref, sin_ref, stems_ref, *refs,
):
    keys = refs[:2]
    refs = refs[2:]
    sums = [refs[p * addends : (p + 1) * addends] for p in range(len(parts))]
    refs = refs[len(parts) * addends + aliased :]
    out_ref, far_key, far_value, far_mask, held, sems = refs
    device = device_ref[0]
    first_block = device * blocks
    ids, unused = far_chain(parents_ref, first_block, far_slots)
    for level in range(far_slots):
        live = ids[level] >= 0
        safe = jnp.maximum(ids[level], 0)
        owner = lax.div(safe, jnp.int32(blocks))
        inner = lax.rem(safe, jnp.int32(blocks))
        apart = lax.bitwise_xor(owner, device)
        where = jnp.int32(0)
        for step, bit in enumerate(tour):
            where = where + jnp.where(lax.bitwise_and(apart, bit) != 0, 1 << step, 0)
        start = pl.multiple_of(inner * block_len, block_len)
        here = pl.ds(level * block_len, block_len)
        far_key[here, :] = stems_ref[where, pl.ds(start, block_len), :HD]
        far_value[here, :] = stems_ref[where, pl.ds(start, block_len), HD:]
        far_mask[:, here] = jnp.broadcast_to(jnp.where(live, 0.0, NEG), (8, block_len))

    factor = HD ** (-0.5) * math.log2(math.e)
    contract = (((1,), (1,)), ((), ()))
    rows = heads * block_len
    column = lax.broadcasted_iota(jnp.int32, (rows, block_len), 1)
    row = lax.broadcasted_iota(jnp.int32, (rows, block_len), 0) % block_len
    near = [(keys[0], block * block_len) for block in range(STEMS)]
    near += [(keys[1], (block - STEMS) * block_len) for block in range(STEMS, blocks)]
    copies = []
    for p, (first, count, offset) in enumerate(parts):
        for inside in range(count):
            block = first + inside
            here = slice(block * block_len, (block + 1) * block_len)
            mine = slice(inside * block_len, (inside + 1) * block_len)
            total = sums[p][0][0, mine, offset : offset + heads * HD]
            for ref in sums[p][1:]:
                total = total + ref[0, mine, offset : offset + heads * HD].astype(jnp.float32)
            inverse = inverse_ref[here]
            query = []
            for head in range(heads):
                lanes = slice(head * HD, (head + 1) * HD)
                one = jnp.where(inverse > 0, total[:, lanes] * inverse, 0.0)
                one = one + bias_ref[:, lanes]
                query.append(turn(one, cos_ref[here], sin_ref[here]).astype(jnp.bfloat16))
            query = jnp.concatenate(query, 0)
            far = lax.dot_general(
                query, far_key[...], contract, preferred_element_type=jnp.float32
            )
            scores = [far + far_mask[0:1, :]]
            for other in range(block + 1):
                ref, begin = near[other]
                score = lax.dot_general(
                    query,
                    ref[begin : begin + block_len, :HD],
                    contract,
                    preferred_element_type=jnp.float32,
                )
                if other == block or other >= STEMS:
                    seen = column < lengths_ref[first_block + other]
                    if other == block:
                        seen = seen & (column <= row)
                    score = jnp.where(seen, score, NEG)
                scores.append(score)
            peak = functools.reduce(
                jnp.maximum, [jnp.max(score, -1, keepdims=True) for score in scores]
            )
            peak = peak * factor
            exps = [jnp.exp2(score * factor - peak) for score in scores]
            total = functools.reduce(jnp.add, [jnp.sum(e, -1, keepdims=True) for e in exps])
            output = jnp.dot(
                exps[0].astype(jnp.bfloat16), far_value[...], preferred_element_type=jnp.float32
            )
            for other in range(block + 1):
                ref, begin = near[other]
                output += jnp.dot(
                    exps[1 + other].astype(jnp.bfloat16),
                    ref[begin : begin + block_len, HD:],
                    preferred_element_type=jnp.float32,
                )
            output = output / total
            if block >= STEMS:
                output = jnp.where(row < lengths_ref[first_block + block], output, 0.0)
            output = output.astype(jnp.bfloat16)
            for head in range(heads):
                lanes = slice(head * HD, (head + 1) * HD)
                held[here, lanes] = output[head * block_len : (head + 1) * block_len]
            copy = pltpu.make_async_copy(
                held.at[pl.ds(block * block_len, block_len)],
                out_ref.at[pl.ds(block * block_len, block_len), pl.ds(first_head * HD, heads * HD)],
                sems.at[block],
            )
            copy.start()
            copies.append(copy)
    for copy in copies:
        copy.wait()


def shards(
    hidden, parents, lengths, gain, w_query, w_key, w_value, query_bias, key_bias, value_bias
):
    blocks, block_len, feature_part = hidden.shape
    tokens = blocks * block_len
    features = gain.shape[0]
    rows = w_query.shape[0]
    columns = w_query.shape[1]
    head_count = columns // HD
    lines = lax.axis_size("fsdp")
    branches = lax.axis_size("branch")
    groups = branches // lines
    far_slots = STEMS * bits_of(branches)
    part = lax.axis_index("fsdp")
    device = lax.axis_index("branch")
    bf16 = jnp.bfloat16
    f32 = jnp.float32
    half_lines = lines // 2
    top = bits_of(half_lines)
    kv_width = 2 * HD

    def swap(array, axis, bit):
        size = lax.axis_size(axis)
        return lax.ppermute(array, axis, [(i, i ^ bit) for i in range(size)])

    def spread(index):
        return ((index & 1) << top) | (index >> 1)

    smem = pl.BlockSpec(memory_space=pltpu.SMEM)
    vmem = pl.BlockSpec(memory_space=pltpu.VMEM)
    anywhere = pl.BlockSpec(memory_space=pl.ANY)
    device_id = device.astype(jnp.int32)[None]
    place = jnp.stack([spread(part), device % groups]).astype(jnp.int32)

    raw = hidden.reshape(tokens, feature_part)
    gain_part = lax.dynamic_slice_in_dim(gain, part * feature_part, feature_part)

    def column(z, feature):
        return (z ^ feature) & (half_lines - 1)

    def middle(z, feature):
        return (column(z, feature) << 1) | ((feature >> top) ^ (z & 1))

    def landing(z, feature):
        return (column(z, feature) << 1) | ((z ^ feature) >> top)

    first_hop = []
    second_hop = []
    for z in range(lines):
        for g in range(groups):
            for feature in range(lines):
                here = z * groups + g
                there = feature * groups + g
                stop = middle(z, feature) * branches + here
                first_hop.append((feature * branches + here, stop))
                second_hop.append((stop, landing(z, feature) * branches + there))
    axes = ("fsdp", "branch")
    head_cuts = [0, (5 * head_count + 7) // 8, head_count]
    w_chunks = [jnp.concatenate([w_key, w_value], 1)] + [
        lax.slice_in_dim(w_query, low * HD, high * HD, axis=1)
        for low, high in zip(head_cuts, head_cuts[1:])
    ]
    squares = jnp.sum(jnp.square(raw.astype(f32)), -1).reshape(blocks, block_len)
    scaled = (raw.astype(f32) * gain_part).astype(bf16)
    cut = STEMS * block_len
    sent = [lax.ppermute(piece, axes, first_hop) for piece in (scaled[:cut], scaled[cut:])]
    squares = tie(squares, sent[0])
    bit = 1
    while bit < lines:
        squares = squares + swap(squares, "fsdp", bit)
        bit *= 2
    inverse = lax.rsqrt(squares / features + 1e-06).reshape(tokens)
    inverse = jnp.broadcast_to(inverse[:, None], (tokens, HD))
    sent = [piece[i : i + block_len] for piece in sent for i in range(0, len(piece), block_len)]

    head_cuts = [0, (5 * head_count + 7) // 8, head_count]
    w_chunks = [jnp.concatenate([w_key, w_value], 1)] + [
        lax.slice_in_dim(w_query, low * HD, high * HD, axis=1)
        for low, high in zip(head_cuts, head_cuts[1:])
    ]
    w_rows = []
    for chunk in w_chunks:
        outgoing = tie(chunk, w_rows[-1][-1]) if w_rows else chunk
        w_rows.append([chunk] + [swap(outgoing, "branch", j) for j in range(1, groups)])

    cos, sin = pl.pallas_call(
        functools.partial(table_kernel, far_slots, blocks, block_len),
        in_specs=[smem, smem],
        out_specs=[vmem, vmem],
        out_shape=[jax.ShapeDtypeStruct((tokens, HD), f32)] * 2,
        name="tables",
    )(device_id, parents)
    sent[0] = tie(sent[0], cos, sin, *w_chunks)
    sent[1] = tie(sent[1], w_rows[0][-1])
    sent[2] = tie(sent[2], squares)

    sent = [lax.ppermute(piece, axes, second_hop) for piece in sent]
    held = [{0: piece} for piece in sent]
    held[-1][0] = tie(held[-1][0], w_rows[1][-1])
    bit = half_lines
    while bit:
        for piece in held:
            for j in list(piece):
                piece[j | bit] = swap(piece[j], "fsdp", bit)
        bit //= 2
    held = [[piece[j] for j in sorted(piece, key=spread)] for piece in held]

    def project(which, chunks, *after):
        count = len(which)
        length = count * block_len
        weights = [w for chunk in chunks for w in w_rows[chunk]]
        width = sum(w_chunks[chunk].shape[1] for chunk in chunks)
        operands = [held[block][i] for i in range(lines) for block in which]
        operands[0] = tie(operands[0], *after) if after else operands[0]
        flops = 2 * lines * length * feature_part * width
        send, keep = pl.pallas_call(
            functools.partial(project_kernel, lines, count, groups),
            in_specs=[smem] + [anywhere] * (len(operands) + len(weights)),
            out_specs=[vmem, vmem],
            out_shape=[
                jax.ShapeDtypeStruct((half_lines * length, width), bf16),
                jax.ShapeDtypeStruct((half_lines * length, width), f32),
            ],
            scratch_shapes=[
                pltpu.VMEM((lines * length, feature_part), bf16),
                pltpu.VMEM((feature_part, width), bf16),
                pltpu.SemaphoreType.DMA((len(operands) + len(weights),)),
            ],
            compiler_params=pltpu.CompilerParams(vmem_limit_bytes=32 * 2**20),
            cost_estimate=pl.CostEstimate(
                flops=flops, bytes_accessed=2 * lines * length * feature_part, transcendentals=0
            ),
            name="project",
        )(place, *operands, *weights)
        return send.reshape(half_lines, length, width), keep.reshape(half_lines, length, width)

    class Halving:
        def __init__(self, partial):
            self.send, self.total = partial
            self.addends = [self.total]
            self.bit = 1

        def step(self, *after):
            send = tie(self.send, *after) if after else self.send
            self.came = swap(send, "branch", self.bit * groups)
            self.addends.append(self.came)
            self.bit *= 2

        def add(self):
            total = self.total + self.came.astype(f32)
            self.send = total[1::2].astype(bf16)
            self.total = total[0::2]

        def rest(self, *after):
            while self.bit < lines:
                self.add()
                self.step(*after)

    addend_count = 1 + bits_of(lines)

    def lead(array):
        return pl.BlockSpec((1,) + array.shape[1:], lambda i: (0, 0, 0))

    def whole(array):
        return pl.BlockSpec(array.shape, lambda i: (0,) * array.ndim)

    kv_bias = jnp.concatenate([key_bias, value_bias])[None]

    def finish_kv(addends, first, count):
        low, high = first * block_len, (first + count) * block_len
        operands = [inverse[low:high], kv_bias, cos[low:high], sin[low:high]]
        return pl.pallas_call(
            functools.partial(kv_kernel, addend_count),
            grid=(1,),
            in_specs=[whole(x) for x in operands] + [lead(x) for x in addends],
            out_specs=pl.BlockSpec((high - low, kv_width), lambda i: (0, 0)),
            out_shape=jax.ShapeDtypeStruct((high - low, kv_width), bf16),
            compiler_params=pltpu.CompilerParams(vmem_limit_bytes=16 * 2**20),
            name="finish_kv",
        )(*operands, *addends)

    early = list(range(STEMS))
    late = list(range(STEMS, blocks))
    first = Halving(project(early, [0]))
    first.step()
    second = Halving(project(early, [1], first.send))
    second.step()
    first.rest(second.send)
    third = Halving(project(late, [0, 1], second.send, first.send))
    stem_kv = finish_kv(first.addends, 0, STEMS)

    tour = [1 << i for i in range(bits_of(groups))]
    tour += [groups << i for i in reversed(range(bits_of(lines)))]
    stems = stem_kv[None]

    def tour_step(stems, bit, *after):
        came = swap(tie(stems, *after) if after else stems, "branch", bit)
        return jnp.concatenate([stems, came], 0)

    for bit in tour[: bits_of(groups)]:
        stems = tour_step(stems, bit)
    third.step(stem_kv)
    far_tour = tour[bits_of(groups) :]
    stems = tour_step(stems, far_tour[0])
    fourth = Halving(project(early + late, [2], third.send))
    second.rest(stems if len(far_tour) == 0 else third.send)
    fourth.step(second.came)
    third.rest()
    for bit in far_tour[1:]:
        stems = tour_step(stems, bit)
    fourth.rest(third.send)
    third.addends[-1] = tie(third.addends[-1], fourth.send)
    late_kv = finish_kv(third.addends, STEMS, blocks - STEMS)
    second_sums, third_sums, fourth_sums = second.addends, third.addends, fourth.addends

    def attend(heads, first_head, parts, sums, output):
        operands = [
            inverse, query_bias[None, first_head * HD : (first_head + heads) * HD], cos, sin,
            stems, stem_kv, late_kv,
        ]
        in_specs = [smem] * 3 + [whole(x) for x in operands]
        for addends in sums:
            operands += addends
            in_specs += [lead(x) for x in addends]
        aliases = {}
        if output is not None:
            aliases = {3 + len(operands): 0}
            operands.append(output)
            in_specs.append(anywhere)
        kernel = functools.partial(
            attend_kernel, far_slots, block_len, blocks, heads, first_head, parts, addend_count,
            len(aliases), tour,
        )
        keys = (far_slots * len(parts) + blocks) * block_len
        return pl.pallas_call(
            kernel,
            grid=(1,),
            in_specs=in_specs,
            out_specs=anywhere,
            scratch_shapes=[
                pltpu.VMEM((far_slots * block_len, HD), bf16),
                pltpu.VMEM((far_slots * block_len, HD), bf16),
                pltpu.VMEM((8, far_slots * block_len), f32),
                pltpu.VMEM((tokens, heads * HD), bf16),
                pltpu.SemaphoreType.DMA((blocks,)),
            ],
            out_shape=jax.ShapeDtypeStruct((tokens, columns), bf16),
            input_output_aliases=aliases,
            compiler_params=pltpu.CompilerParams(vmem_limit_bytes=40 * 2**20),
            cost_estimate=pl.CostEstimate(
                flops=4 * tokens * heads * keys * HD,
                bytes_accessed=2 * tokens * heads * HD,
                transcendentals=tokens * heads * keys,
            ),
            name="attend",
        )(device_id, parents, lengths, *operands)

    output = attend(
        head_cuts[1], 0, [(0, STEMS, 0), (STEMS, blocks - STEMS, kv_width)],
        [second_sums, third_sums], None,
    )
    output = attend(
        head_count - head_cuts[1], head_cuts[1], [(0, blocks, 0)], [fourth_sums], output
    )
    return output.reshape(blocks, block_len, columns)


def solution(mesh):
    return jax.shard_map(
        shards,
        mesh=mesh,
        in_specs=(
            P("branch", None, "fsdp"),
            P(),
            P(),
            P(),
            P("branch", "fsdp"),
            P("branch", "fsdp"),
            P("branch", "fsdp"),
            P("fsdp"),
            P("fsdp"),
            P("fsdp"),
        ),
        out_specs=P("branch", None, "fsdp"),
        check_vma=False,
    )
```

```python
import functools
import math

import jax
import jax.numpy as jnp
from jax import lax
from jax.experimental import pallas as pl
from jax.experimental.pallas import tpu as pltpu
from jax.sharding import PartitionSpec as P

HD = 128
STEMS = 2
THETA = 1000000.0
NEG = -1e30


def bits_of(count):
    return count.bit_length() - 1


def tie(array, *others):
    return lax.optimization_barrier((array,) + others)[0]


def far_chain(parents_ref, first_block, far_slots):
    cursor = parents_ref[first_block]
    ids = []
    total = jnp.int32(0)
    for level in range(far_slots):
        ids.append(cursor)
        total = total + jnp.where(cursor >= 0, 1, 0)
        above = parents_ref[jnp.maximum(cursor, 0)]
        cursor = jnp.where(cursor >= 0, above, -1)
    return ids, total


def add_up(refs, inverse, bias, columns):
    total = refs[0][0, :, columns]
    for ref in refs[1:]:
        total = total + ref[0, :, columns].astype(jnp.float32)
    repeats = total.shape[1] // HD
    inverse = jnp.concatenate([inverse] * repeats, 1)
    return jnp.where(inverse > 0, total * inverse, 0.0) + bias


def turn(vectors, cos, sin):
    half = vectors.shape[-1] // 2
    return vectors * cos + pltpu.roll(vectors, half, 1) * sin


def table_kernel(far_slots, blocks, block_len, device_ref, parents_ref, cos_ref, sin_ref):
    tokens = cos_ref.shape[0]
    unused, far_total = far_chain(parents_ref, device_ref[0] * blocks, far_slots)
    rows = lax.broadcasted_iota(jnp.int32, (tokens, HD), 0)
    lanes = lax.broadcasted_iota(jnp.int32, (tokens, HD), 1)
    front = lanes < HD // 2
    pair = jnp.where(front, lanes, lanes - HD // 2).astype(jnp.float32)
    freqs = jnp.exp(pair * (-2.0 * math.log(THETA) / HD))
    angles = (rows + far_total * block_len).astype(jnp.float32) * freqs
    sin = jnp.sin(angles)
    cos_ref[...] = jnp.cos(angles)
    sin_ref[...] = jnp.where(front, -sin, sin)


def assemble(lines, blocks, place_ref, pieces, held, sems):
    half = lines // 2
    block_len = pieces[0].shape[0]
    copies = []
    for i in range(lines):
        target = lax.bitwise_xor(jnp.int32(i), place_ref[0])
        slot = jnp.where(target % 2 == 0, half, 0) + target // 2
        for block in range(blocks):
            begin = pl.multiple_of((slot * blocks + block) * block_len, block_len)
            n = i * blocks + block
            there = held.at[pl.ds(begin, block_len)]
            copies.append(pltpu.make_async_copy(pieces[n], there, sems.at[n]))
    for copy in copies:
        copy.start()
    return copies


def project_kernel(lines, groups, chunks, counts, fresh, place_ref, *refs):
    fresh_count = lines * counts[-1] if fresh else 0
    whole_count = len(counts) - (1 if fresh else 0)
    wholes = list(refs[:whole_count])
    pieces = refs[whole_count : whole_count + fresh_count]
    refs = refs[whole_count + fresh_count :]
    weights = refs[: groups * chunks]
    outs = refs[groups * chunks :]
    send_ref, keep_ref = outs[:2]
    if fresh:
        held, sems = outs[2:]
        for copy in assemble(lines, counts[-1], place_ref, pieces, held, sems):
            copy.wait()
        wholes.append(held)
    half = lines // 2
    rows = weights[0].shape[0]
    length = send_ref.shape[1]
    begin = 0
    for held, count in zip(wholes, counts):
        share = held.shape[0] // lines
        middle = half * share
        start = 0
        for chunk in range(chunks):
            width = weights[chunk * groups].shape[1]
            for out_ref, low in ((send_ref, 0), (keep_ref, middle)):
                total = None
                for g in range(groups):
                    member = lax.bitwise_xor(place_ref[1], jnp.int32(g))
                    lanes = pl.ds(pl.multiple_of(member * rows, rows), rows)
                    term = jnp.dot(
                        held[low : low + middle, lanes],
                        weights[chunk * groups + g][...],
                        preferred_element_type=jnp.float32,
                    )
                    total = term if total is None else total + term
                total = total.astype(out_ref.dtype).reshape(half, share, width)
                out_ref[:, begin : begin + share, start : start + width] = total
            start += width
        begin += share


def kv_kernel(addends, inverse_ref, bias_ref, cos_ref, sin_ref, *refs):
    kv_ref = refs[-1]
    both = add_up(refs[:addends], inverse_ref[...], bias_ref[...], slice(0, 2 * HD))
    kv_ref[:, :HD] = turn(both[:, :HD], cos_ref[...], sin_ref[...]).astype(jnp.bfloat16)
    kv_ref[:, HD:] = both[:, HD:].astype(jnp.bfloat16)


def attend_kernel(
    far_slots, block_len, blocks, heads, first_head, parts, addends, aliased, tour, device_ref,
    parents_ref, lengths_ref, inverse_ref, bias_ref, cos_ref, sin_ref, stems_ref, *refs,
):
    keys = refs[:2]
    refs = refs[2:]
    sums = [refs[p * addends : (p + 1) * addends] for p in range(len(parts))]
    refs = refs[len(parts) * addends + aliased :]
    out_ref, far_key, far_value, far_mask, held, sems = refs
    device = device_ref[0]
    first_block = device * blocks
    ids, unused = far_chain(parents_ref, first_block, far_slots)
    for level in range(far_slots):
        live = ids[level] >= 0
        safe = jnp.maximum(ids[level], 0)
        owner = lax.div(safe, jnp.int32(blocks))
        inner = lax.rem(safe, jnp.int32(blocks))
        apart = lax.bitwise_xor(owner, device)
        where = jnp.int32(0)
        for step, bit in enumerate(tour):
            where = where + jnp.where(lax.bitwise_and(apart, bit) != 0, 1 << step, 0)
        start = pl.multiple_of(inner * block_len, block_len)
        here = pl.ds(level * block_len, block_len)
        far_key[here, :] = stems_ref[where, pl.ds(start, block_len), :HD]
        far_value[here, :] = stems_ref[where, pl.ds(start, block_len), HD:]
        far_mask[:, here] = jnp.broadcast_to(jnp.where(live, 0.0, NEG), (8, block_len))

    factor = HD ** (-0.5) * math.log2(math.e)
    contract = (((1,), (1,)), ((), ()))
    rows = heads * block_len
    column = lax.broadcasted_iota(jnp.int32, (rows, block_len), 1)
    row = lax.broadcasted_iota(jnp.int32, (rows, block_len), 0) % block_len
    near = [(keys[0], block * block_len) for block in range(STEMS)]
    near += [(keys[1], (block - STEMS) * block_len) for block in range(STEMS, blocks)]
    copies = []
    for p, (first, count, offset) in enumerate(parts):
        for inside in range(count):
            block = first + inside
            here = slice(block * block_len, (block + 1) * block_len)
            mine = slice(inside * block_len, (inside + 1) * block_len)
            total = sums[p][0][0, mine, offset : offset + heads * HD]
            for ref in sums[p][1:]:
                total = total + ref[0, mine, offset : offset + heads * HD].astype(jnp.float32)
            inverse = inverse_ref[here]
            query = []
            for head in range(heads):
                lanes = slice(head * HD, (head + 1) * HD)
                one = jnp.where(inverse > 0, total[:, lanes] * inverse, 0.0)
                one = one + bias_ref[:, lanes]
                query.append(turn(one, cos_ref[here], sin_ref[here]).astype(jnp.bfloat16))
            query = jnp.concatenate(query, 0)
            far = lax.dot_general(
                query, far_key[...], contract, preferred_element_type=jnp.float32
            )
            scores = [far + far_mask[0:1, :]]
            for other in range(block + 1):
                ref, begin = near[other]
                score = lax.dot_general(
                    query,
                    ref[begin : begin + block_len, :HD],
                    contract,
                    preferred_element_type=jnp.float32,
                )
                if other == block or other >= STEMS:
                    seen = column < lengths_ref[first_block + other]
                    if other == block:
                        seen = seen & (column <= row)
                    score = jnp.where(seen, score, NEG)
                scores.append(score)
            peak = functools.reduce(
                jnp.maximum, [jnp.max(score, -1, keepdims=True) for score in scores]
            )
            peak = peak * factor
            exps = [jnp.exp2(score * factor - peak) for score in scores]
            total = functools.reduce(jnp.add, [jnp.sum(e, -1, keepdims=True) for e in exps])
            output = jnp.dot(
                exps[0].astype(jnp.bfloat16), far_value[...], preferred_element_type=jnp.float32
            )
            for other in range(block + 1):
                ref, begin = near[other]
                output += jnp.dot(
                    exps[1 + other].astype(jnp.bfloat16),
                    ref[begin : begin + block_len, HD:],
                    preferred_element_type=jnp.float32,
                )
            output = output / total
            if block >= STEMS:
                output = jnp.where(row < lengths_ref[first_block + block], output, 0.0)
            output = output.astype(jnp.bfloat16)
            for head in range(heads):
                lanes = slice(head * HD, (head + 1) * HD)
                held[here, lanes] = output[head * block_len : (head + 1) * block_len]
            copy = pltpu.make_async_copy(
                held.at[pl.ds(block * block_len, block_len)],
                out_ref.at[pl.ds(block * block_len, block_len), pl.ds(first_head * HD, heads * HD)],
                sems.at[block],
            )
            copy.start()
            copies.append(copy)
    for copy in copies:
        copy.wait()


def shards(
    hidden, parents, lengths, gain, w_query, w_key, w_value, query_bias, key_bias, value_bias
):
    blocks, block_len, feature_part = hidden.shape
    tokens = blocks * block_len
    features = gain.shape[0]
    rows = w_query.shape[0]
    columns = w_query.shape[1]
    head_count = columns // HD
    lines = lax.axis_size("fsdp")
    branches = lax.axis_size("branch")
    groups = branches // lines
    far_slots = STEMS * bits_of(branches)
    part = lax.axis_index("fsdp")
    device = lax.axis_index("branch")
    bf16 = jnp.bfloat16
    f32 = jnp.float32
    half_lines = lines // 2
    top = bits_of(half_lines)
    kv_width = 2 * HD

    def swap(array, axis, bit):
        size = lax.axis_size(axis)
        return lax.ppermute(array, axis, [(i, i ^ bit) for i in range(size)])

    def spread(index):
        return ((index & 1) << top) | (index >> 1)

    smem = pl.BlockSpec(memory_space=pltpu.SMEM)
    vmem = pl.BlockSpec(memory_space=pltpu.VMEM)
    anywhere = pl.BlockSpec(memory_space=pl.ANY)
    device_id = device.astype(jnp.int32)[None]
    place = jnp.stack([spread(part), device % groups]).astype(jnp.int32)

    raw = hidden.reshape(tokens, feature_part)
    gain_part = lax.dynamic_slice_in_dim(gain, part * feature_part, feature_part)

    def column(z, feature):
        return (z ^ feature) & (half_lines - 1)

    def middle(z, feature):
        return (column(z, feature) << 1) | ((feature >> top) ^ (z & 1))

    def landing(z, feature):
        return (column(z, feature) << 1) | ((z ^ feature) >> top)

    first_hop = []
    second_hop = []
    for z in range(lines):
        for g in range(groups):
            for feature in range(lines):
                here = z * groups + g
                there = feature * groups + g
                stop = middle(z, feature) * branches + here
                first_hop.append((feature * branches + here, stop))
                second_hop.append((stop, landing(z, feature) * branches + there))
    axes = ("fsdp", "branch")
    head_cuts = [0, (5 * head_count + 7) // 8, head_count]
    w_chunks = [jnp.concatenate([w_key, w_value], 1)] + [
        lax.slice_in_dim(w_query, low * HD, high * HD, axis=1)
        for low, high in zip(head_cuts, head_cuts[1:])
    ]
    squares = jnp.sum(jnp.square(raw.astype(f32)), -1).reshape(blocks, block_len)
    bit = 1
    while bit < lines:
        squares = squares + swap(squares, "fsdp", bit)
        bit *= 2
    inverse = lax.rsqrt(squares / features + 1e-06).reshape(tokens)
    inverse = jnp.broadcast_to(inverse[:, None], (tokens, HD))
    sent = []
    for block in range(blocks):
        piece = (hidden[block].astype(f32) * gain_part).astype(bf16)
        if block == 1:
            piece = tie(piece, sent[-1], squares)
        elif block:
            piece = tie(piece, sent[-1])
        sent.append(lax.ppermute(piece, axes, first_hop))

    head_cuts = [0, (5 * head_count + 7) // 8, head_count]
    w_chunks = [jnp.concatenate([w_key, w_value], 1)] + [
        lax.slice_in_dim(w_query, low * HD, high * HD, axis=1)
        for low, high in zip(head_cuts, head_cuts[1:])
    ]
    w_rows = []
    for chunk in w_chunks:
        outgoing = tie(chunk, w_rows[-1][-1]) if w_rows else chunk
        w_rows.append([chunk] + [swap(outgoing, "branch", j) for j in range(1, groups)])

    cos, sin = pl.pallas_call(
        functools.partial(table_kernel, far_slots, blocks, block_len),
        in_specs=[smem, smem],
        out_specs=[vmem, vmem],
        out_shape=[jax.ShapeDtypeStruct((tokens, HD), f32)] * 2,
        name="tables",
    )(device_id, parents)
    sent[0] = tie(sent[0], cos, sin, *w_chunks)
    sent[1] = tie(sent[1], w_rows[0][-1])

    sent = [lax.ppermute(piece, axes, second_hop) for piece in sent]
    held = [{0: piece} for piece in sent]
    bit = half_lines
    while bit > 1:
        for piece in held:
            for j in list(piece):
                piece[j | bit] = swap(piece[j], "fsdp", bit)
        bit //= 2

    def last_bit(piece):
        for j in list(piece):
            piece[j | 1] = swap(piece[j], "fsdp", 1)
        return [piece[j] for j in sorted(piece, key=spread)]

    held = [last_bit(piece) for piece in held[:STEMS]] + held[STEMS:]

    assembled = {}

    def project(spans, chunks, *after):
        weights = [w for chunk in chunks for w in w_rows[chunk]]
        width = sum(w_chunks[chunk].shape[1] for chunk in chunks)
        fresh = spans[-1] not in assembled
        counts = [high - low for low, high in spans]
        wholes = [assembled[span] for span in spans if span in assembled]
        pieces = []
        if fresh:
            pieces = [held[block][i] for i in range(lines) for block in range(*spans[-1])]
        operands = wholes + pieces
        operands[0] = tie(operands[0], *after) if after else operands[0]
        length = sum(counts) * block_len
        out_specs = [vmem, vmem]
        out_shape = [
            jax.ShapeDtypeStruct((half_lines, length, width), bf16),
            jax.ShapeDtypeStruct((half_lines, length, width), f32),
        ]
        scratch = []
        if fresh:
            out_specs.append(vmem)
            out_shape.append(
                jax.ShapeDtypeStruct((lines * counts[-1] * block_len, feature_part), bf16)
            )
            scratch.append(pltpu.SemaphoreType.DMA((len(pieces),)))
        results = pl.pallas_call(
            functools.partial(project_kernel, lines, groups, len(chunks), counts, fresh),
            in_specs=[smem] + [vmem] * len(wholes) + [anywhere] * len(pieces)
            + [vmem] * len(weights),
            out_specs=out_specs,
            out_shape=out_shape,
            scratch_shapes=scratch,
            compiler_params=pltpu.CompilerParams(vmem_limit_bytes=24 * 2**20),
            cost_estimate=pl.CostEstimate(
                flops=2 * lines * length * feature_part * width,
                bytes_accessed=2 * lines * length * feature_part,
                transcendentals=0,
            ),
            name="project",
        )(place, *operands, *weights)
        if fresh:
            assembled[spans[-1]] = results[2]
        return results[0], results[1]

    class Halving:
        def __init__(self, partial):
            self.send, self.total = partial
            self.addends = [self.total]
            self.bit = 1

        def step(self, *after):
            send = tie(self.send, *after) if after else self.send
            self.came = swap(send, "branch", self.bit * groups)
            self.addends.append(self.came)
            self.bit *= 2

        def add(self, *after):
            self.came = tie(self.came, *after) if after else self.came
            self.addends[-1] = self.came
            total = self.total + self.came.astype(f32)
            self.send = total[1::2].astype(bf16)
            self.total = total[0::2]

        def rest(self, *after):
            while self.bit < lines:
                self.add(*after)
                self.step()

    addend_count = 1 + bits_of(lines)

    def lead(array):
        return pl.BlockSpec((1,) + array.shape[1:], lambda i: (0, 0, 0))

    def whole(array):
        return pl.BlockSpec(array.shape, lambda i: (0,) * array.ndim)

    kv_bias = jnp.concatenate([key_bias, value_bias])[None]

    def finish_kv(addends, first, count):
        low, high = first * block_len, (first + count) * block_len
        operands = [inverse[low:high], kv_bias, cos[low:high], sin[low:high]]
        return pl.pallas_call(
            functools.partial(kv_kernel, addend_count),
            grid=(1,),
            in_specs=[whole(x) for x in operands] + [lead(x) for x in addends],
            out_specs=pl.BlockSpec((high - low, kv_width), lambda i: (0, 0)),
            out_shape=jax.ShapeDtypeStruct((high - low, kv_width), bf16),
            compiler_params=pltpu.CompilerParams(vmem_limit_bytes=16 * 2**20),
            name="finish_kv",
        )(*operands, *addends)

    early = (0, STEMS)
    late = (STEMS, blocks)
    first = Halving(project([early], [0], w_rows[1][-1]))
    first.step()
    second = Halving(project([early], [1], first.send))
    second.step()
    for block in range(*late):
        held[block][0] = tie(held[block][0], second.send)
        held[block] = last_bit(held[block])
    first.rest(second.send)
    third = Halving(project([late], [0, 1], first.send))
    third.step()
    first.addends[-1] = tie(first.addends[-1], third.send)
    stem_kv = finish_kv(first.addends, 0, STEMS)

    tour = [1 << i for i in range(bits_of(groups))]
    tour += [groups << i for i in reversed(range(bits_of(lines)))]
    stems = stem_kv[None]
    came = swap(stems, "branch", tour[0])
    second.rest(stem_kv, w_rows[2][-1])
    last = second
    for step, bit in enumerate(tour[1:]):
        stems = jnp.concatenate([stems, tie(came, last.send)], 0)
        came = swap(stems, "branch", bit)
        if step == 0:
            fourth = Halving(project([early, late], [2], stems))
            fourth.step()
            third.rest(fourth.send)
            last = third
    fourth.rest(stems, second.came)
    stems = jnp.concatenate([stems, came], 0)
    third.addends[-1] = tie(third.addends[-1], fourth.send)
    late_kv = finish_kv(third.addends, STEMS, blocks - STEMS)
    second_sums, third_sums, fourth_sums = second.addends, third.addends, fourth.addends

    def attend(heads, first_head, parts, sums, output):
        operands = [
            inverse, query_bias[None, first_head * HD : (first_head + heads) * HD], cos, sin,
            stems, stem_kv, late_kv,
        ]
        in_specs = [smem] * 3 + [whole(x) for x in operands]
        for addends in sums:
            operands += addends
            in_specs += [lead(x) for x in addends]
        aliases = {}
        if output is not None:
            aliases = {3 + len(operands): 0}
            operands.append(output)
            in_specs.append(anywhere)
        kernel = functools.partial(
            attend_kernel, far_slots, block_len, blocks, heads, first_head, parts, addend_count,
            len(aliases), tour,
        )
        keys = (far_slots * len(parts) + blocks) * block_len
        return pl.pallas_call(
            kernel,
            grid=(1,),
            in_specs=in_specs,
            out_specs=anywhere,
            scratch_shapes=[
                pltpu.VMEM((far_slots * block_len, HD), bf16),
                pltpu.VMEM((far_slots * block_len, HD), bf16),
                pltpu.VMEM((8, far_slots * block_len), f32),
                pltpu.VMEM((tokens, heads * HD), bf16),
                pltpu.SemaphoreType.DMA((blocks,)),
            ],
            out_shape=jax.ShapeDtypeStruct((tokens, columns), bf16),
            input_output_aliases=aliases,
            compiler_params=pltpu.CompilerParams(vmem_limit_bytes=40 * 2**20),
            cost_estimate=pl.CostEstimate(
                flops=4 * tokens * heads * keys * HD,
                bytes_accessed=2 * tokens * heads * HD,
                transcendentals=tokens * heads * keys,
            ),
            name="attend",
        )(device_id, parents, lengths, *operands)

    output = attend(
        head_cuts[1], 0, [(0, STEMS, 0), (STEMS, blocks - STEMS, kv_width)],
        [second_sums, third_sums], None,
    )
    output = attend(
        head_count - head_cuts[1], head_cuts[1], [(0, blocks, 0)], [fourth_sums], output
    )
    return output.reshape(blocks, block_len, columns)


def solution(mesh):
    return jax.shard_map(
        shards,
        mesh=mesh,
        in_specs=(
            P("branch", None, "fsdp"),
            P(),
            P(),
            P(),
            P("branch", "fsdp"),
            P("branch", "fsdp"),
            P("branch", "fsdp"),
            P("fsdp"),
            P("fsdp"),
            P("fsdp"),
        ),
        out_specs=P("branch", None, "fsdp"),
        check_vma=False,
    )
```

```python
import functools
import math

import jax
import jax.numpy as jnp
from jax import lax
from jax.experimental import pallas as pl
from jax.experimental.pallas import tpu as pltpu
from jax.sharding import PartitionSpec as P

HD = 128
STEMS = 2
THETA = 1000000.0
NEG = -1e30


def bits_of(count):
    return count.bit_length() - 1


def tie(array, *others):
    return lax.optimization_barrier((array,) + others)[0]


def far_chain(parents_ref, first_block, far_slots):
    cursor = parents_ref[first_block]
    ids = []
    total = jnp.int32(0)
    for level in range(far_slots):
        ids.append(cursor)
        total = total + jnp.where(cursor >= 0, 1, 0)
        above = parents_ref[jnp.maximum(cursor, 0)]
        cursor = jnp.where(cursor >= 0, above, -1)
    return ids, total


def add_up(refs, inverse, bias, columns):
    total = refs[0][0, :, columns]
    for ref in refs[1:]:
        total = total + ref[0, :, columns].astype(jnp.float32)
    repeats = total.shape[1] // HD
    inverse = jnp.concatenate([inverse] * repeats, 1)
    return jnp.where(inverse > 0, total * inverse, 0.0) + bias


def turn(vectors, cos, sin):
    half = vectors.shape[-1] // 2
    return vectors * cos + pltpu.roll(vectors, half, 1) * sin


def table_kernel(far_slots, blocks, block_len, device_ref, parents_ref, cos_ref, sin_ref):
    tokens = cos_ref.shape[0]
    unused, far_total = far_chain(parents_ref, device_ref[0] * blocks, far_slots)
    rows = lax.broadcasted_iota(jnp.int32, (tokens, HD), 0)
    lanes = lax.broadcasted_iota(jnp.int32, (tokens, HD), 1)
    front = lanes < HD // 2
    pair = jnp.where(front, lanes, lanes - HD // 2).astype(jnp.float32)
    freqs = jnp.exp(pair * (-2.0 * math.log(THETA) / HD))
    angles = (rows + far_total * block_len).astype(jnp.float32) * freqs
    sin = jnp.sin(angles)
    cos_ref[...] = jnp.cos(angles)
    sin_ref[...] = jnp.where(front, -sin, sin)


def assemble(lines, blocks, place_ref, pieces, held, sems):
    half = lines // 2
    block_len = pieces[0].shape[0]
    copies = []
    for i in range(lines):
        target = lax.bitwise_xor(jnp.int32(i), place_ref[0])
        slot = jnp.where(target % 2 == 0, half, 0) + target // 2
        for block in range(blocks):
            begin = pl.multiple_of((slot * blocks + block) * block_len, block_len)
            n = i * blocks + block
            there = held.at[pl.ds(begin, block_len)]
            copies.append(pltpu.make_async_copy(pieces[n], there, sems.at[n]))
    for copy in copies:
        copy.start()
    return copies


def assemble_kernel(lines, place_ref, *refs):
    pieces, (held, sems) = refs[:lines], refs[lines:]
    for copy in assemble(lines, 1, place_ref, pieces, held, sems):
        copy.wait()


def project_kernel(lines, groups, chunks, counts, fresh, place_ref, *refs):
    fresh_count = lines * counts[-1] if fresh else 0
    whole_count = len(counts) - (1 if fresh else 0)
    wholes = list(refs[:whole_count])
    pieces = refs[whole_count : whole_count + fresh_count]
    refs = refs[whole_count + fresh_count :]
    weights = refs[: groups * chunks]
    outs = refs[groups * chunks :]
    send_ref, keep_ref = outs[:2]
    if fresh:
        held, sems = outs[2:]
        for copy in assemble(lines, counts[-1], place_ref, pieces, held, sems):
            copy.wait()
        wholes.append(held)
    half = lines // 2
    rows = weights[0].shape[0]
    length = send_ref.shape[1]
    begin = 0
    for held, count in zip(wholes, counts):
        share = held.shape[0] // lines
        middle = half * share
        start = 0
        for chunk in range(chunks):
            width = weights[chunk * groups].shape[1]
            for out_ref, low in ((send_ref, 0), (keep_ref, middle)):
                total = None
                for g in range(groups):
                    member = lax.bitwise_xor(place_ref[1], jnp.int32(g))
                    lanes = pl.ds(pl.multiple_of(member * rows, rows), rows)
                    term = jnp.dot(
                        held[low : low + middle, lanes],
                        weights[chunk * groups + g][...],
                        preferred_element_type=jnp.float32,
                    )
                    total = term if total is None else total + term
                total = total.astype(out_ref.dtype).reshape(half, share, width)
                out_ref[:, begin : begin + share, start : start + width] = total
            start += width
        begin += share


def kv_kernel(addends, inverse_ref, bias_ref, cos_ref, sin_ref, *refs):
    kv_ref = refs[-1]
    both = add_up(refs[:addends], inverse_ref[...], bias_ref[...], slice(0, 2 * HD))
    kv_ref[:, :HD] = turn(both[:, :HD], cos_ref[...], sin_ref[...]).astype(jnp.bfloat16)
    kv_ref[:, HD:] = both[:, HD:].astype(jnp.bfloat16)


def attend_kernel(
    far_slots, block_len, blocks, heads, first_head, parts, addends, aliased, tour, device_ref,
    parents_ref, lengths_ref, inverse_ref, bias_ref, cos_ref, sin_ref, stems_ref, *refs,
):
    keys = refs[:2]
    refs = refs[2:]
    sums = [refs[p * addends : (p + 1) * addends] for p in range(len(parts))]
    refs = refs[len(parts) * addends + aliased :]
    out_ref, far_key, far_value, far_mask, held, sems = refs
    device = device_ref[0]
    first_block = device * blocks
    ids, unused = far_chain(parents_ref, first_block, far_slots)
    for level in range(far_slots):
        live = ids[level] >= 0
        safe = jnp.maximum(ids[level], 0)
        owner = lax.div(safe, jnp.int32(blocks))
        inner = lax.rem(safe, jnp.int32(blocks))
        apart = lax.bitwise_xor(owner, device)
        where = jnp.int32(0)
        for step, bit in enumerate(tour):
            where = where + jnp.where(lax.bitwise_and(apart, bit) != 0, 1 << step, 0)
        start = pl.multiple_of(inner * block_len, block_len)
        here = pl.ds(level * block_len, block_len)
        far_key[here, :] = stems_ref[where, pl.ds(start, block_len), :HD]
        far_value[here, :] = stems_ref[where, pl.ds(start, block_len), HD:]
        far_mask[:, here] = jnp.broadcast_to(jnp.where(live, 0.0, NEG), (8, block_len))

    factor = HD ** (-0.5) * math.log2(math.e)
    contract = (((1,), (1,)), ((), ()))
    rows = heads * block_len
    column = lax.broadcasted_iota(jnp.int32, (rows, block_len), 1)
    row = lax.broadcasted_iota(jnp.int32, (rows, block_len), 0) % block_len
    near = [(keys[0], block * block_len) for block in range(STEMS)]
    near += [(keys[1], (block - STEMS) * block_len) for block in range(STEMS, blocks)]
    copies = []
    for p, (first, count, offset) in enumerate(parts):
        for inside in range(count):
            block = first + inside
            here = slice(block * block_len, (block + 1) * block_len)
            mine = slice(inside * block_len, (inside + 1) * block_len)
            total = sums[p][0][0, mine, offset : offset + heads * HD]
            for ref in sums[p][1:]:
                total = total + ref[0, mine, offset : offset + heads * HD].astype(jnp.float32)
            inverse = inverse_ref[here]
            query = []
            for head in range(heads):
                lanes = slice(head * HD, (head + 1) * HD)
                one = jnp.where(inverse > 0, total[:, lanes] * inverse, 0.0)
                one = one + bias_ref[:, lanes]
                query.append(turn(one, cos_ref[here], sin_ref[here]).astype(jnp.bfloat16))
            query = jnp.concatenate(query, 0)
            far = lax.dot_general(
                query, far_key[...], contract, preferred_element_type=jnp.float32
            )
            scores = [far + far_mask[0:1, :]]
            for other in range(block + 1):
                ref, begin = near[other]
                score = lax.dot_general(
                    query,
                    ref[begin : begin + block_len, :HD],
                    contract,
                    preferred_element_type=jnp.float32,
                )
                if other == block or other >= STEMS:
                    seen = column < lengths_ref[first_block + other]
                    if other == block:
                        seen = seen & (column <= row)
                    score = jnp.where(seen, score, NEG)
                scores.append(score)
            peak = functools.reduce(
                jnp.maximum, [jnp.max(score, -1, keepdims=True) for score in scores]
            )
            peak = peak * factor
            exps = [jnp.exp2(score * factor - peak) for score in scores]
            total = functools.reduce(jnp.add, [jnp.sum(e, -1, keepdims=True) for e in exps])
            output = jnp.dot(
                exps[0].astype(jnp.bfloat16), far_value[...], preferred_element_type=jnp.float32
            )
            for other in range(block + 1):
                ref, begin = near[other]
                output += jnp.dot(
                    exps[1 + other].astype(jnp.bfloat16),
                    ref[begin : begin + block_len, HD:],
                    preferred_element_type=jnp.float32,
                )
            output = output / total
            if block >= STEMS:
                output = jnp.where(row < lengths_ref[first_block + block], output, 0.0)
            output = output.astype(jnp.bfloat16)
            for head in range(heads):
                lanes = slice(head * HD, (head + 1) * HD)
                held[here, lanes] = output[head * block_len : (head + 1) * block_len]
            copy = pltpu.make_async_copy(
                held.at[pl.ds(block * block_len, block_len)],
                out_ref.at[pl.ds(block * block_len, block_len), pl.ds(first_head * HD, heads * HD)],
                sems.at[block],
            )
            copy.start()
            copies.append(copy)
    for copy in copies:
        copy.wait()


def shards(
    hidden, parents, lengths, gain, w_query, w_key, w_value, query_bias, key_bias, value_bias
):
    blocks, block_len, feature_part = hidden.shape
    tokens = blocks * block_len
    features = gain.shape[0]
    rows = w_query.shape[0]
    columns = w_query.shape[1]
    head_count = columns // HD
    lines = lax.axis_size("fsdp")
    branches = lax.axis_size("branch")
    groups = branches // lines
    far_slots = STEMS * bits_of(branches)
    part = lax.axis_index("fsdp")
    device = lax.axis_index("branch")
    bf16 = jnp.bfloat16
    f32 = jnp.float32
    half_lines = lines // 2
    top = bits_of(half_lines)
    kv_width = 2 * HD

    def swap(array, axis, bit):
        size = lax.axis_size(axis)
        return lax.ppermute(array, axis, [(i, i ^ bit) for i in range(size)])

    def spread(index):
        return ((index & 1) << top) | (index >> 1)

    smem = pl.BlockSpec(memory_space=pltpu.SMEM)
    vmem = pl.BlockSpec(memory_space=pltpu.VMEM)
    anywhere = pl.BlockSpec(memory_space=pl.ANY)
    device_id = device.astype(jnp.int32)[None]
    place = jnp.stack([spread(part), device % groups]).astype(jnp.int32)

    raw = hidden.reshape(tokens, feature_part)
    gain_part = lax.dynamic_slice_in_dim(gain, part * feature_part, feature_part)

    def column(z, feature):
        return (z ^ feature) & (half_lines - 1)

    def middle(z, feature):
        return (column(z, feature) << 1) | ((feature >> top) ^ (z & 1))

    def landing(z, feature):
        return (column(z, feature) << 1) | ((z ^ feature) >> top)

    first_hop = []
    second_hop = []
    for z in range(lines):
        for g in range(groups):
            for feature in range(lines):
                here = z * groups + g
                there = feature * groups + g
                stop = middle(z, feature) * branches + here
                first_hop.append((feature * branches + here, stop))
                second_hop.append((stop, landing(z, feature) * branches + there))
    axes = ("fsdp", "branch")
    head_cuts = [0, (5 * head_count + 7) // 8, head_count]
    w_chunks = [jnp.concatenate([w_key, w_value], 1)] + [
        lax.slice_in_dim(w_query, low * HD, high * HD, axis=1)
        for low, high in zip(head_cuts, head_cuts[1:])
    ]

    cos, sin = pl.pallas_call(
        functools.partial(table_kernel, far_slots, blocks, block_len),
        in_specs=[smem, smem],
        out_specs=[vmem, vmem],
        out_shape=[jax.ShapeDtypeStruct((tokens, HD), f32)] * 2,
        name="tables",
    )(device_id, parents)

    sent = []
    for block in range(blocks):
        piece = (hidden[block].astype(f32) * gain_part).astype(bf16)
        piece = tie(piece, sent[-1], cos, sin, *w_chunks) if block else piece
        sent.append(lax.ppermute(piece, axes, first_hop))

    w_rows = [None] * len(w_chunks)
    arrived = None
    for c in (1, 0, 2):
        outgoing = w_chunks[c] if arrived is None else tie(w_chunks[c], arrived)
        w_rows[c] = [w_chunks[c]] + [swap(outgoing, "branch", j) for j in range(1, groups)]
        arrived = w_rows[c][-1]

    squares = tie(jnp.sum(jnp.square(raw.astype(f32)), -1).reshape(blocks, block_len), sent[1])
    bit = 1
    while bit < lines:
        squares = squares + swap(squares, "fsdp", bit)
        bit *= 2
    inverse = lax.rsqrt(squares / features + 1e-06).reshape(tokens)
    inverse = jnp.broadcast_to(inverse[:, None], (tokens, HD))

    last_sent = sent[-1]
    sent = [lax.ppermute(piece, axes, second_hop) for piece in sent]
    sent[0] = tie(sent[0], squares, last_sent)
    held = [{0: piece} for piece in sent]
    bit = half_lines
    while bit > 1:
        for piece in held:
            for j in list(piece):
                piece[j | bit] = swap(piece[j], "fsdp", bit)
        bit //= 2

    def last_bit(piece):
        for j in list(piece):
            piece[j | 1] = swap(piece[j], "fsdp", 1)
        return [piece[j] for j in sorted(piece, key=spread)]

    held[0][half_lines] = tie(held[0][half_lines], w_rows[1][-1])
    held[1][half_lines] = tie(held[1][half_lines], w_rows[0][-1])
    held = [last_bit(piece) for piece in held[:STEMS]] + held[STEMS:]

    assembled = {}

    def project(spans, chunks, *after):
        weights = [w for chunk in chunks for w in w_rows[chunk]]
        width = sum(w_chunks[chunk].shape[1] for chunk in chunks)
        fresh = spans[-1] not in assembled
        counts = [high - low for low, high in spans]
        wholes = [assembled[span] for span in spans if span in assembled]
        pieces = []
        if fresh:
            pieces = [held[block][i] for i in range(lines) for block in range(*spans[-1])]
        operands = wholes + pieces
        operands[0] = tie(operands[0], *after) if after else operands[0]
        length = sum(counts) * block_len
        out_specs = [vmem, vmem]
        out_shape = [
            jax.ShapeDtypeStruct((half_lines, length, width), bf16),
            jax.ShapeDtypeStruct((half_lines, length, width), f32),
        ]
        scratch = []
        if fresh:
            out_specs.append(vmem)
            out_shape.append(
                jax.ShapeDtypeStruct((lines * counts[-1] * block_len, feature_part), bf16)
            )
            scratch.append(pltpu.SemaphoreType.DMA((len(pieces),)))
        results = pl.pallas_call(
            functools.partial(project_kernel, lines, groups, len(chunks), counts, fresh),
            in_specs=[smem] + [vmem] * len(wholes) + [anywhere] * len(pieces)
            + [vmem] * len(weights),
            out_specs=out_specs,
            out_shape=out_shape,
            scratch_shapes=scratch,
            compiler_params=pltpu.CompilerParams(vmem_limit_bytes=24 * 2**20),
            cost_estimate=pl.CostEstimate(
                flops=2 * lines * length * feature_part * width,
                bytes_accessed=2 * lines * length * feature_part,
                transcendentals=0,
            ),
            name="project",
        )(place, *operands, *weights)
        if fresh:
            assembled[spans[-1]] = results[2]
        return results[0], results[1]

    class Halving:
        def __init__(self, partial):
            self.send, self.total = partial
            self.addends = [self.total]
            self.bit = 1

        def step(self, *after):
            send = tie(self.send, *after) if after else self.send
            self.came = swap(send, "branch", self.bit * groups)
            self.addends.append(self.came)
            self.bit *= 2

        def add(self, *after):
            self.came = tie(self.came, *after) if after else self.came
            self.addends[-1] = self.came
            total = self.total + self.came.astype(f32)
            self.send = total[1::2].astype(bf16)
            self.total = total[0::2]

        def rest(self, *after):
            while self.bit < lines:
                self.add(*after)
                self.step()

    addend_count = 1 + bits_of(lines)

    def lead(array):
        return pl.BlockSpec((1,) + array.shape[1:], lambda i: (0, 0, 0))

    def whole(array):
        return pl.BlockSpec(array.shape, lambda i: (0,) * array.ndim)

    kv_bias = jnp.concatenate([key_bias, value_bias])[None]

    def finish_kv(addends, first, count):
        low, high = first * block_len, (first + count) * block_len
        operands = [inverse[low:high], kv_bias, cos[low:high], sin[low:high]]
        return pl.pallas_call(
            functools.partial(kv_kernel, addend_count),
            grid=(1,),
            in_specs=[whole(x) for x in operands] + [lead(x) for x in addends],
            out_specs=pl.BlockSpec((high - low, kv_width), lambda i: (0, 0)),
            out_shape=jax.ShapeDtypeStruct((high - low, kv_width), bf16),
            compiler_params=pltpu.CompilerParams(vmem_limit_bytes=16 * 2**20),
            name="finish_kv",
        )(*operands, *addends)

    assembled[(0, 1)] = pl.pallas_call(
        functools.partial(assemble_kernel, lines),
        in_specs=[smem] + [anywhere] * lines,
        out_specs=vmem,
        out_shape=jax.ShapeDtypeStruct((lines * block_len, feature_part), bf16),
        scratch_shapes=[pltpu.SemaphoreType.DMA((lines,))],
        name="assemble",
    )(place, *held[0])

    early = [(0, 1), (1, STEMS)]
    late = [(STEMS, blocks)]
    first = Halving(project(early, [0]))
    first.step()
    second = Halving(project(early, [1], first.send))
    second.step()
    for block in range(STEMS, blocks):
        held[block][0] = tie(held[block][0], second.send)
        held[block] = last_bit(held[block])
    first.rest(second.send)
    stem_kv = finish_kv(first.addends, 0, STEMS)

    tour = [1 << i for i in range(bits_of(groups))]
    tour += [groups << i for i in reversed(range(bits_of(lines)))]
    stems = stem_kv[None]
    came = swap(stems, "branch", tour[0])
    third = Halving(project(late, [0, 1], stem_kv))
    third.step()
    second.add(third.send, w_rows[2][-1])
    for step, bit in enumerate(tour[1:]):
        stems = jnp.concatenate([stems, tie(came, fourth.send if step else second.send)], 0)
        came = swap(stems, "branch", bit)
        if step == 0:
            fourth = Halving(project(early + late, [2], stems))
    second.step(stems)
    fourth.step(stems)
    third.add(stems)
    third.step()
    second.rest()
    third.rest()
    fourth.rest(second.came)
    stems = jnp.concatenate([stems, came], 0)
    third.addends[-1] = tie(third.addends[-1], fourth.send)
    late_kv = finish_kv(third.addends, STEMS, blocks - STEMS)
    second_sums, third_sums, fourth_sums = second.addends, third.addends, fourth.addends

    def attend(heads, first_head, parts, sums, output):
        operands = [
            inverse, query_bias[None, first_head * HD : (first_head + heads) * HD], cos, sin,
            stems, stem_kv, late_kv,
        ]
        in_specs = [smem] * 3 + [whole(x) for x in operands]
        for addends in sums:
            operands += addends
            in_specs += [lead(x) for x in addends]
        aliases = {}
        if output is not None:
            aliases = {3 + len(operands): 0}
            operands.append(output)
            in_specs.append(anywhere)
        kernel = functools.partial(
            attend_kernel, far_slots, block_len, blocks, heads, first_head, parts, addend_count,
            len(aliases), tour,
        )
        keys = (far_slots * len(parts) + blocks) * block_len
        return pl.pallas_call(
            kernel,
            grid=(1,),
            in_specs=in_specs,
            out_specs=anywhere,
            scratch_shapes=[
                pltpu.VMEM((far_slots * block_len, HD), bf16),
                pltpu.VMEM((far_slots * block_len, HD), bf16),
                pltpu.VMEM((8, far_slots * block_len), f32),
                pltpu.VMEM((tokens, heads * HD), bf16),
                pltpu.SemaphoreType.DMA((blocks,)),
            ],
            out_shape=jax.ShapeDtypeStruct((tokens, columns), bf16),
            input_output_aliases=aliases,
            compiler_params=pltpu.CompilerParams(vmem_limit_bytes=40 * 2**20),
            cost_estimate=pl.CostEstimate(
                flops=4 * tokens * heads * keys * HD,
                bytes_accessed=2 * tokens * heads * HD,
                transcendentals=tokens * heads * keys,
            ),
            name="attend",
        )(device_id, parents, lengths, *operands)

    output = attend(
        head_cuts[1], 0, [(0, STEMS, 0), (STEMS, blocks - STEMS, kv_width)],
        [second_sums, third_sums], None,
    )
    output = attend(
        head_count - head_cuts[1], head_cuts[1], [(0, blocks, 0)], [fourth_sums], output
    )
    return output.reshape(blocks, block_len, columns)


def solution(mesh):
    return jax.shard_map(
        shards,
        mesh=mesh,
        in_specs=(
            P("branch", None, "fsdp"),
            P(),
            P(),
            P(),
            P("branch", "fsdp"),
            P("branch", "fsdp"),
            P("branch", "fsdp"),
            P("fsdp"),
            P("fsdp"),
            P("fsdp"),
        ),
        out_specs=P("branch", None, "fsdp"),
        check_vma=False,
    )
```

```python
import functools
import math

import jax
import jax.numpy as jnp
from jax import lax
from jax.experimental import pallas as pl
from jax.experimental.pallas import tpu as pltpu
from jax.sharding import PartitionSpec as P

HD = 128
STEMS = 2
THETA = 1000000.0
NEG = -1e30


def bits_of(count):
    return count.bit_length() - 1


def tie(array, *others):
    return lax.optimization_barrier((array,) + others)[0]


def far_chain(parents_ref, first_block, far_slots):
    cursor = parents_ref[first_block]
    ids = []
    total = jnp.int32(0)
    for level in range(far_slots):
        ids.append(cursor)
        total = total + jnp.where(cursor >= 0, 1, 0)
        above = parents_ref[jnp.maximum(cursor, 0)]
        cursor = jnp.where(cursor >= 0, above, -1)
    return ids, total


def add_up(refs, inverse, bias, columns):
    total = refs[0][0, :, columns]
    for ref in refs[1:]:
        total = total + ref[0, :, columns].astype(jnp.float32)
    repeats = total.shape[1] // HD
    inverse = jnp.concatenate([inverse] * repeats, 1)
    return jnp.where(inverse > 0, total * inverse, 0.0) + bias


def turn(vectors, cos, sin):
    half = vectors.shape[-1] // 2
    return vectors * cos + pltpu.roll(vectors, half, 1) * sin


def table_kernel(far_slots, blocks, block_len, device_ref, parents_ref, cos_ref, sin_ref):
    tokens = cos_ref.shape[0]
    unused, far_total = far_chain(parents_ref, device_ref[0] * blocks, far_slots)
    rows = lax.broadcasted_iota(jnp.int32, (tokens, HD), 0)
    lanes = lax.broadcasted_iota(jnp.int32, (tokens, HD), 1)
    front = lanes < HD // 2
    pair = jnp.where(front, lanes, lanes - HD // 2).astype(jnp.float32)
    freqs = jnp.exp(pair * (-2.0 * math.log(THETA) / HD))
    angles = (rows + far_total * block_len).astype(jnp.float32) * freqs
    sin = jnp.sin(angles)
    cos_ref[...] = jnp.cos(angles)
    sin_ref[...] = jnp.where(front, -sin, sin)


def assemble(lines, blocks, place_ref, pieces, held, sems):
    half = lines // 2
    block_len = pieces[0].shape[0]
    copies = []
    for i in range(lines):
        target = lax.bitwise_xor(jnp.int32(i), place_ref[0])
        slot = jnp.where(target % 2 == 0, half, 0) + target // 2
        for block in range(blocks):
            begin = pl.multiple_of((slot * blocks + block) * block_len, block_len)
            n = i * blocks + block
            there = held.at[pl.ds(begin, block_len)]
            copies.append(pltpu.make_async_copy(pieces[n], there, sems.at[n]))
    for copy in copies:
        copy.start()
    return copies


def assemble_kernel(lines, place_ref, *refs):
    pieces, (held, sems) = refs[:lines], refs[lines:]
    for copy in assemble(lines, 1, place_ref, pieces, held, sems):
        copy.wait()


def project_kernel(lines, groups, chunks, counts, fresh, place_ref, *refs):
    fresh_count = lines * counts[-1] if fresh else 0
    whole_count = len(counts) - (1 if fresh else 0)
    wholes = list(refs[:whole_count])
    pieces = refs[whole_count : whole_count + fresh_count]
    refs = refs[whole_count + fresh_count :]
    weights = refs[: groups * chunks]
    outs = refs[groups * chunks :]
    send_ref, keep_ref = outs[:2]
    if fresh:
        held, sems = outs[2:]
        for copy in assemble(lines, counts[-1], place_ref, pieces, held, sems):
            copy.wait()
        wholes.append(held)
    half = lines // 2
    rows = weights[0].shape[0]
    length = send_ref.shape[1]
    begin = 0
    for held, count in zip(wholes, counts):
        share = held.shape[0] // lines
        middle = half * share
        start = 0
        for chunk in range(chunks):
            width = weights[chunk * groups].shape[1]
            for out_ref, low in ((send_ref, 0), (keep_ref, middle)):
                total = None
                for g in range(groups):
                    member = lax.bitwise_xor(place_ref[1], jnp.int32(g))
                    lanes = pl.ds(pl.multiple_of(member * rows, rows), rows)
                    term = jnp.dot(
                        held[low : low + middle, lanes],
                        weights[chunk * groups + g][...],
                        preferred_element_type=jnp.float32,
                    )
                    total = term if total is None else total + term
                total = total.astype(out_ref.dtype).reshape(half, share, width)
                out_ref[:, begin : begin + share, start : start + width] = total
            start += width
        begin += share


def kv_kernel(addends, inverse_ref, bias_ref, cos_ref, sin_ref, *refs):
    kv_ref = refs[-1]
    both = add_up(refs[:addends], inverse_ref[...], bias_ref[...], slice(0, 2 * HD))
    kv_ref[:, :HD] = turn(both[:, :HD], cos_ref[...], sin_ref[...]).astype(jnp.bfloat16)
    kv_ref[:, HD:] = both[:, HD:].astype(jnp.bfloat16)


def attend_kernel(
    far_slots, block_len, blocks, heads, first_head, parts, addends, aliased, tour, device_ref,
    parents_ref, lengths_ref, inverse_ref, bias_ref, cos_ref, sin_ref, stems_ref, *refs,
):
    keys = refs[:2]
    refs = refs[2:]
    sums = [refs[p * addends : (p + 1) * addends] for p in range(len(parts))]
    refs = refs[len(parts) * addends + aliased :]
    out_ref, far_key, far_value, far_mask, held, sems = refs
    device = device_ref[0]
    first_block = device * blocks
    ids, unused = far_chain(parents_ref, first_block, far_slots)
    for level in range(far_slots):
        live = ids[level] >= 0
        safe = jnp.maximum(ids[level], 0)
        owner = lax.div(safe, jnp.int32(blocks))
        inner = lax.rem(safe, jnp.int32(blocks))
        apart = lax.bitwise_xor(owner, device)
        where = jnp.int32(0)
        for step, bit in enumerate(tour):
            where = where + jnp.where(lax.bitwise_and(apart, bit) != 0, 1 << step, 0)
        start = pl.multiple_of(inner * block_len, block_len)
        here = pl.ds(level * block_len, block_len)
        far_key[here, :] = stems_ref[where, pl.ds(start, block_len), :HD]
        far_value[here, :] = stems_ref[where, pl.ds(start, block_len), HD:]
        far_mask[:, here] = jnp.broadcast_to(jnp.where(live, 0.0, NEG), (8, block_len))

    factor = HD ** (-0.5) * math.log2(math.e)
    contract = (((1,), (1,)), ((), ()))
    rows = heads * block_len
    column = lax.broadcasted_iota(jnp.int32, (rows, block_len), 1)
    row = lax.broadcasted_iota(jnp.int32, (rows, block_len), 0) % block_len
    near = [(keys[0], block * block_len) for block in range(STEMS)]
    near += [(keys[1], (block - STEMS) * block_len) for block in range(STEMS, blocks)]
    copies = []
    for p, (first, count, offset) in enumerate(parts):
        for inside in range(count):
            block = first + inside
            here = slice(block * block_len, (block + 1) * block_len)
            mine = slice(inside * block_len, (inside + 1) * block_len)
            total = sums[p][0][0, mine, offset : offset + heads * HD]
            for ref in sums[p][1:]:
                total = total + ref[0, mine, offset : offset + heads * HD].astype(jnp.float32)
            inverse = inverse_ref[here]
            query = []
            for head in range(heads):
                lanes = slice(head * HD, (head + 1) * HD)
                one = jnp.where(inverse > 0, total[:, lanes] * inverse, 0.0)
                one = one + bias_ref[:, lanes]
                query.append(turn(one, cos_ref[here], sin_ref[here]).astype(jnp.bfloat16))
            query = jnp.concatenate(query, 0)
            far = lax.dot_general(
                query, far_key[...], contract, preferred_element_type=jnp.float32
            )
            scores = [far + far_mask[0:1, :]]
            for other in range(block + 1):
                ref, begin = near[other]
                score = lax.dot_general(
                    query,
                    ref[begin : begin + block_len, :HD],
                    contract,
                    preferred_element_type=jnp.float32,
                )
                if other == block or other >= STEMS:
                    seen = column < lengths_ref[first_block + other]
                    if other == block:
                        seen = seen & (column <= row)
                    score = jnp.where(seen, score, NEG)
                scores.append(score)
            peak = functools.reduce(
                jnp.maximum, [jnp.max(score, -1, keepdims=True) for score in scores]
            )
            peak = peak * factor
            exps = [jnp.exp2(score * factor - peak) for score in scores]
            total = functools.reduce(jnp.add, [jnp.sum(e, -1, keepdims=True) for e in exps])
            output = jnp.dot(
                exps[0].astype(jnp.bfloat16), far_value[...], preferred_element_type=jnp.float32
            )
            for other in range(block + 1):
                ref, begin = near[other]
                output += jnp.dot(
                    exps[1 + other].astype(jnp.bfloat16),
                    ref[begin : begin + block_len, HD:],
                    preferred_element_type=jnp.float32,
                )
            output = output / total
            if block >= STEMS:
                output = jnp.where(row < lengths_ref[first_block + block], output, 0.0)
            output = output.astype(jnp.bfloat16)
            for head in range(heads):
                lanes = slice(head * HD, (head + 1) * HD)
                held[here, lanes] = output[head * block_len : (head + 1) * block_len]
            copy = pltpu.make_async_copy(
                held.at[pl.ds(block * block_len, block_len)],
                out_ref.at[pl.ds(block * block_len, block_len), pl.ds(first_head * HD, heads * HD)],
                sems.at[block],
            )
            copy.start()
            copies.append(copy)
    for copy in copies:
        copy.wait()


def shards(
    hidden, parents, lengths, gain, w_query, w_key, w_value, query_bias, key_bias, value_bias
):
    blocks, block_len, feature_part = hidden.shape
    tokens = blocks * block_len
    features = gain.shape[0]
    rows = w_query.shape[0]
    columns = w_query.shape[1]
    head_count = columns // HD
    lines = lax.axis_size("fsdp")
    branches = lax.axis_size("branch")
    groups = branches // lines
    far_slots = STEMS * bits_of(branches)
    part = lax.axis_index("fsdp")
    device = lax.axis_index("branch")
    bf16 = jnp.bfloat16
    f32 = jnp.float32
    half_lines = lines // 2
    top = bits_of(half_lines)
    kv_width = 2 * HD

    def swap(array, axis, bit):
        size = lax.axis_size(axis)
        return lax.ppermute(array, axis, [(i, i ^ bit) for i in range(size)])

    def spread(index):
        return ((index & 1) << top) | (index >> 1)

    smem = pl.BlockSpec(memory_space=pltpu.SMEM)
    vmem = pl.BlockSpec(memory_space=pltpu.VMEM)
    anywhere = pl.BlockSpec(memory_space=pl.ANY)
    device_id = device.astype(jnp.int32)[None]
    place = jnp.stack([spread(part), device % groups]).astype(jnp.int32)

    raw = hidden.reshape(tokens, feature_part)
    gain_part = lax.dynamic_slice_in_dim(gain, part * feature_part, feature_part)

    def column(z, feature):
        return (z ^ feature) & (half_lines - 1)

    def middle(z, feature):
        return (column(z, feature) << 1) | ((feature >> top) ^ (z & 1))

    def landing(z, feature):
        return (column(z, feature) << 1) | ((z ^ feature) >> top)

    first_hop = []
    second_hop = []
    for z in range(lines):
        for g in range(groups):
            for feature in range(lines):
                here = z * groups + g
                there = feature * groups + g
                stop = middle(z, feature) * branches + here
                first_hop.append((feature * branches + here, stop))
                second_hop.append((stop, landing(z, feature) * branches + there))
    axes = ("fsdp", "branch")
    head_cuts = [0, (5 * head_count + 7) // 8, head_count]
    w_chunks = [jnp.concatenate([w_key, w_value], 1)] + [
        lax.slice_in_dim(w_query, low * HD, high * HD, axis=1)
        for low, high in zip(head_cuts, head_cuts[1:])
    ]

    cos, sin = pl.pallas_call(
        functools.partial(table_kernel, far_slots, blocks, block_len),
        in_specs=[smem, smem],
        out_specs=[vmem, vmem],
        out_shape=[jax.ShapeDtypeStruct((tokens, HD), f32)] * 2,
        name="tables",
    )(device_id, parents)

    sent = []
    for block in range(blocks):
        piece = (hidden[block].astype(f32) * gain_part).astype(bf16)
        piece = tie(piece, sent[-1], cos, sin, *w_chunks) if block else piece
        sent.append(lax.ppermute(piece, axes, first_hop))

    w_rows = [None] * len(w_chunks)
    arrived = None
    for c in (1, 0, 2):
        outgoing = w_chunks[c] if arrived is None else tie(w_chunks[c], arrived)
        w_rows[c] = [w_chunks[c]] + [swap(outgoing, "branch", j) for j in range(1, groups)]
        arrived = w_rows[c][-1]

    last_sent = sent[-1]
    sent = [lax.ppermute(piece, axes, second_hop) for piece in sent]
    sent[0] = tie(sent[0], last_sent, w_rows[1][-1])
    held = [{0: piece} for piece in sent]
    bit = half_lines
    while bit > 1:
        for piece in held:
            for j in list(piece):
                piece[j | bit] = swap(piece[j], "fsdp", bit)
        bit //= 2

    def last_bit(piece):
        for j in list(piece):
            piece[j | 1] = swap(piece[j], "fsdp", 1)
        return [piece[j] for j in sorted(piece, key=spread)]

    held[1][half_lines] = tie(held[1][half_lines], w_rows[0][-1])
    assembled = {}
    held[0] = last_bit(held[0])
    assembled[(0, 1)] = pl.pallas_call(
        functools.partial(assemble_kernel, lines),
        in_specs=[smem] + [anywhere] * lines,
        out_specs=vmem,
        out_shape=jax.ShapeDtypeStruct((lines * block_len, feature_part), bf16),
        scratch_shapes=[pltpu.SemaphoreType.DMA((lines,))],
        name="assemble",
    )(place, *held[0])
    for block in range(1, STEMS):
        held[block][half_lines] = tie(held[block][half_lines], assembled[(0, 1)])
        held[block] = last_bit(held[block])


    def project(spans, chunks, *after):
        weights = [w for chunk in chunks for w in w_rows[chunk]]
        width = sum(w_chunks[chunk].shape[1] for chunk in chunks)
        fresh = spans[-1] not in assembled
        counts = [high - low for low, high in spans]
        wholes = [assembled[span] for span in spans if span in assembled]
        pieces = []
        if fresh:
            pieces = [held[block][i] for i in range(lines) for block in range(*spans[-1])]
        operands = wholes + pieces
        operands[0] = tie(operands[0], *after) if after else operands[0]
        length = sum(counts) * block_len
        out_specs = [vmem, vmem]
        out_shape = [
            jax.ShapeDtypeStruct((half_lines, length, width), bf16),
            jax.ShapeDtypeStruct((half_lines, length, width), f32),
        ]
        scratch = []
        if fresh:
            out_specs.append(vmem)
            out_shape.append(
                jax.ShapeDtypeStruct((lines * counts[-1] * block_len, feature_part), bf16)
            )
            scratch.append(pltpu.SemaphoreType.DMA((len(pieces),)))
        results = pl.pallas_call(
            functools.partial(project_kernel, lines, groups, len(chunks), counts, fresh),
            in_specs=[smem] + [vmem] * len(wholes) + [anywhere] * len(pieces)
            + [vmem] * len(weights),
            out_specs=out_specs,
            out_shape=out_shape,
            scratch_shapes=scratch,
            compiler_params=pltpu.CompilerParams(vmem_limit_bytes=24 * 2**20),
            cost_estimate=pl.CostEstimate(flops=0, bytes_accessed=0, transcendentals=0),
            name="project",
        )(place, *operands, *weights)
        if fresh:
            assembled[spans[-1]] = results[2]
        return results[0], results[1]

    class Halving:
        def __init__(self, partial):
            self.send, self.total = partial
            self.addends = [self.total]
            self.bit = 1

        def step(self, *after):
            send = tie(self.send, *after) if after else self.send
            self.came = swap(send, "branch", self.bit * groups)
            self.addends.append(self.came)
            self.bit *= 2

        def add(self, *after):
            self.came = tie(self.came, *after) if after else self.came
            self.addends[-1] = self.came
            total = self.total + self.came.astype(f32)
            self.send = total[1::2].astype(bf16)
            self.total = total[0::2]

        def rest(self, *after):
            while self.bit < lines:
                self.add(*after)
                self.step()

    addend_count = 1 + bits_of(lines)

    def lead(array):
        return pl.BlockSpec((1,) + array.shape[1:], lambda i: (0, 0, 0))

    def whole(array):
        return pl.BlockSpec(array.shape, lambda i: (0,) * array.ndim)

    kv_bias = jnp.concatenate([key_bias, value_bias])[None]

    def finish_kv(addends, first, count):
        low, high = first * block_len, (first + count) * block_len
        operands = [inverse[low:high], kv_bias, cos[low:high], sin[low:high]]
        return pl.pallas_call(
            functools.partial(kv_kernel, addend_count),
            grid=(1,),
            in_specs=[whole(x) for x in operands] + [lead(x) for x in addends],
            out_specs=pl.BlockSpec((high - low, kv_width), lambda i: (0, 0)),
            out_shape=jax.ShapeDtypeStruct((high - low, kv_width), bf16),
            compiler_params=pltpu.CompilerParams(vmem_limit_bytes=16 * 2**20),
            name="finish_kv",
        )(*operands, *addends)

    early = [(0, 1), (1, STEMS)]
    late = [(STEMS, blocks)]
    first = Halving(project(early, [0]))
    first.step()

    second = Halving(project(early, [1], first.send))
    second.step()
    first.rest(second.send)

    squares = jnp.sum(jnp.square(raw.astype(f32)), -1).reshape(blocks, block_len)
    squares = tie(squares, first.send)
    bit = 1
    while bit < lines:
        squares = squares + swap(squares, "fsdp", bit)
        bit *= 2
    inverse = lax.rsqrt(squares / features + 1e-06).reshape(tokens)
    inverse = jnp.broadcast_to(inverse[:, None], (tokens, HD))

    for block in range(STEMS, blocks):
        held[block] = {j: tie(piece, first.send) for j, piece in held[block].items()}
        held[block] = last_bit(held[block])
    third = Halving(project(late, [0, 1], first.send))
    first.addends[-1] = tie(first.addends[-1], third.send)
    stem_kv = finish_kv(first.addends, 0, STEMS)

    tour = [groups << i for i in reversed(range(bits_of(lines)))]
    tour += [1 << i for i in range(bits_of(groups))]
    stems = stem_kv[None]
    came = swap(stems, "branch", tour[0])
    third.step(stem_kv)
    second.add(stem_kv, w_rows[2][-1])
    second.step()
    fourth = Halving(project(early + late, [2], second.send))
    for step, bit in enumerate(tour[1:]):
        stems = jnp.concatenate([stems, tie(came, third.send if step else fourth.send)], 0)
        came = swap(stems, "branch", bit)
        if step == 0:
            fourth.step(stems)
            third.add(stems, second.came)
            third.step()
    second.rest()
    third.rest()
    fourth.rest(stems, second.came)
    stems = jnp.concatenate([stems, came], 0)
    third.addends[-1] = tie(third.addends[-1], fourth.send)
    late_kv = finish_kv(third.addends, STEMS, blocks - STEMS)
    second_sums, third_sums, fourth_sums = second.addends, third.addends, fourth.addends

    def attend(heads, first_head, parts, sums, output):
        operands = [
            inverse, query_bias[None, first_head * HD : (first_head + heads) * HD], cos, sin,
            stems, stem_kv, late_kv,
        ]
        in_specs = [smem] * 3 + [whole(x) for x in operands]
        for addends in sums:
            operands += addends
            in_specs += [lead(x) for x in addends]
        aliases = {}
        if output is not None:
            aliases = {3 + len(operands): 0}
            operands.append(output)
            in_specs.append(anywhere)
        kernel = functools.partial(
            attend_kernel, far_slots, block_len, blocks, heads, first_head, parts, addend_count,
            len(aliases), tour,
        )
        keys = (far_slots * len(parts) + blocks) * block_len
        return pl.pallas_call(
            kernel,
            grid=(1,),
            in_specs=in_specs,
            out_specs=anywhere,
            scratch_shapes=[
                pltpu.VMEM((far_slots * block_len, HD), bf16),
                pltpu.VMEM((far_slots * block_len, HD), bf16),
                pltpu.VMEM((8, far_slots * block_len), f32),
                pltpu.VMEM((tokens, heads * HD), bf16),
                pltpu.SemaphoreType.DMA((blocks,)),
            ],
            out_shape=jax.ShapeDtypeStruct((tokens, columns), bf16),
            input_output_aliases=aliases,
            compiler_params=pltpu.CompilerParams(vmem_limit_bytes=40 * 2**20),
            cost_estimate=pl.CostEstimate(
                flops=4 * tokens * heads * keys * HD,
                bytes_accessed=2 * tokens * heads * HD,
                transcendentals=tokens * heads * keys,
            ),
            name="attend",
        )(device_id, parents, lengths, *operands)

    output = attend(
        head_cuts[1], 0, [(0, STEMS, 0), (STEMS, blocks - STEMS, kv_width)],
        [second_sums, third_sums], None,
    )
    output = attend(
        head_count - head_cuts[1], head_cuts[1], [(0, blocks, 0)], [fourth_sums], output
    )
    return output.reshape(blocks, block_len, columns)


def solution(mesh):
    return jax.shard_map(
        shards,
        mesh=mesh,
        in_specs=(
            P("branch", None, "fsdp"),
            P(),
            P(),
            P(),
            P("branch", "fsdp"),
            P("branch", "fsdp"),
            P("branch", "fsdp"),
            P("fsdp"),
            P("fsdp"),
            P("fsdp"),
        ),
        out_specs=P("branch", None, "fsdp"),
        check_vma=False,
    )
```

```python
import functools
import math

import jax
import jax.numpy as jnp
from jax import lax
from jax.experimental import pallas as pl
from jax.experimental.pallas import tpu as pltpu
from jax.sharding import PartitionSpec as P

HD = 128
STEMS = 2
THETA = 1000000.0
NEG = -1e30


def bits_of(count):
    return count.bit_length() - 1


def tie(array, *others):
    return lax.optimization_barrier((array,) + others)[0]


def far_chain(parents_ref, first_block, far_slots):
    cursor = parents_ref[first_block]
    ids = []
    total = jnp.int32(0)
    for level in range(far_slots):
        ids.append(cursor)
        total = total + jnp.where(cursor >= 0, 1, 0)
        above = parents_ref[jnp.maximum(cursor, 0)]
        cursor = jnp.where(cursor >= 0, above, -1)
    return ids, total


def add_up(refs, inverse, bias, columns):
    total = refs[0][0, :, columns]
    for ref in refs[1:]:
        total = total + ref[0, :, columns].astype(jnp.float32)
    repeats = total.shape[1] // HD
    inverse = jnp.concatenate([inverse] * repeats, 1)
    return jnp.where(inverse > 0, total * inverse, 0.0) + bias


def turn(vectors, cos, sin):
    half = vectors.shape[-1] // 2
    return vectors * cos + pltpu.roll(vectors, half, 1) * sin


def table_kernel(far_slots, blocks, block_len, device_ref, parents_ref, cos_ref, sin_ref):
    tokens = cos_ref.shape[0]
    unused, far_total = far_chain(parents_ref, device_ref[0] * blocks, far_slots)
    rows = lax.broadcasted_iota(jnp.int32, (tokens, HD), 0)
    lanes = lax.broadcasted_iota(jnp.int32, (tokens, HD), 1)
    front = lanes < HD // 2
    pair = jnp.where(front, lanes, lanes - HD // 2).astype(jnp.float32)
    freqs = jnp.exp(pair * (-2.0 * math.log(THETA) / HD))
    angles = (rows + far_total * block_len).astype(jnp.float32) * freqs
    sin = jnp.sin(angles)
    cos_ref[...] = jnp.cos(angles)
    sin_ref[...] = jnp.where(front, -sin, sin)


def assemble(lines, blocks, place_ref, pieces, held, sems):
    half = lines // 2
    block_len = pieces[0].shape[0]
    copies = []
    for i in range(lines):
        target = lax.bitwise_xor(jnp.int32(i), place_ref[0])
        slot = jnp.where(target % 2 == 0, half, 0) + target // 2
        for block in range(blocks):
            begin = pl.multiple_of((slot * blocks + block) * block_len, block_len)
            n = i * blocks + block
            there = held.at[pl.ds(begin, block_len)]
            copies.append(pltpu.make_async_copy(pieces[n], there, sems.at[n]))
    for copy in copies:
        copy.start()
    return copies


def project_kernel(lines, groups, chunks, counts, fresh, place_ref, *refs):
    fresh_count = lines * counts[-1] if fresh else 0
    whole_count = len(counts) - (1 if fresh else 0)
    wholes = list(refs[:whole_count])
    pieces = refs[whole_count : whole_count + fresh_count]
    refs = refs[whole_count + fresh_count :]
    weights = refs[: groups * chunks]
    outs = refs[groups * chunks :]
    send_ref, keep_ref = outs[:2]
    if fresh:
        held, sems = outs[2:]
        for copy in assemble(lines, counts[-1], place_ref, pieces, held, sems):
            copy.wait()
        wholes.append(held)
    half = lines // 2
    rows = weights[0].shape[0]
    length = send_ref.shape[1]
    begin = 0
    for held, count in zip(wholes, counts):
        share = held.shape[0] // lines
        middle = half * share
        start = 0
        for chunk in range(chunks):
            width = weights[chunk * groups].shape[1]
            for out_ref, low in ((send_ref, 0), (keep_ref, middle)):
                total = None
                for g in range(groups):
                    member = lax.bitwise_xor(place_ref[1], jnp.int32(g))
                    lanes = pl.ds(pl.multiple_of(member * rows, rows), rows)
                    term = jnp.dot(
                        held[low : low + middle, lanes],
                        weights[chunk * groups + g][...],
                        preferred_element_type=jnp.float32,
                    )
                    total = term if total is None else total + term
                total = total.astype(out_ref.dtype).reshape(half, share, width)
                out_ref[:, begin : begin + share, start : start + width] = total
            start += width
        begin += share


def kv_kernel(addends, inverse_ref, bias_ref, cos_ref, sin_ref, *refs):
    kv_ref = refs[-1]
    both = add_up(refs[:addends], inverse_ref[...], bias_ref[...], slice(0, 2 * HD))
    kv_ref[:, :HD] = turn(both[:, :HD], cos_ref[...], sin_ref[...]).astype(jnp.bfloat16)
    kv_ref[:, HD:] = both[:, HD:].astype(jnp.bfloat16)


def attend_kernel(
    far_slots, block_len, blocks, heads, first_head, parts, addends, aliased, tour, device_ref,
    parents_ref, lengths_ref, inverse_ref, bias_ref, cos_ref, sin_ref, stems_ref, *refs,
):
    near = refs[:blocks]
    refs = refs[blocks:]
    sums = [refs[p * addends : (p + 1) * addends] for p in range(len(parts))]
    refs = refs[len(parts) * addends + aliased :]
    out_ref, far_key, far_value, far_mask, held, sems = refs
    device = device_ref[0]
    first_block = device * blocks
    ids, unused = far_chain(parents_ref, first_block, far_slots)
    for level in range(far_slots):
        live = ids[level] >= 0
        safe = jnp.maximum(ids[level], 0)
        owner = lax.div(safe, jnp.int32(blocks))
        inner = lax.rem(safe, jnp.int32(blocks))
        apart = lax.bitwise_xor(owner, device)
        where = jnp.int32(0)
        for step, bit in enumerate(tour):
            where = where + jnp.where(lax.bitwise_and(apart, bit) != 0, 1 << step, 0)
        start = pl.multiple_of(inner * block_len, block_len)
        here = pl.ds(level * block_len, block_len)
        far_key[here, :] = stems_ref[where, pl.ds(start, block_len), :HD]
        far_value[here, :] = stems_ref[where, pl.ds(start, block_len), HD:]
        far_mask[:, here] = jnp.broadcast_to(jnp.where(live, 0.0, NEG), (8, block_len))

    factor = HD ** (-0.5) * math.log2(math.e)
    contract = (((1,), (1,)), ((), ()))
    rows = heads * block_len
    column = lax.broadcasted_iota(jnp.int32, (rows, block_len), 1)
    row = lax.broadcasted_iota(jnp.int32, (rows, block_len), 0) % block_len
    copies = []
    for p, (first, count, offset) in enumerate(parts):
        for inside in range(count):
            block = first + inside
            here = slice(block * block_len, (block + 1) * block_len)
            mine = slice(inside * block_len, (inside + 1) * block_len)
            total = sums[p][0][0, mine, offset : offset + heads * HD]
            for ref in sums[p][1:]:
                total = total + ref[0, mine, offset : offset + heads * HD].astype(jnp.float32)
            inverse = inverse_ref[here]
            query = []
            for head in range(heads):
                lanes = slice(head * HD, (head + 1) * HD)
                one = jnp.where(inverse > 0, total[:, lanes] * inverse, 0.0)
                one = one + bias_ref[:, lanes]
                query.append(turn(one, cos_ref[here], sin_ref[here]).astype(jnp.bfloat16))
            query = jnp.concatenate(query, 0)
            far = lax.dot_general(
                query, far_key[...], contract, preferred_element_type=jnp.float32
            )
            scores = [far + far_mask[0:1, :]]
            for other in range(block + 1):
                score = lax.dot_general(
                    query, near[other][:, :HD], contract, preferred_element_type=jnp.float32
                )
                if other == block or other >= STEMS:
                    seen = column < lengths_ref[first_block + other]
                    if other == block:
                        seen = seen & (column <= row)
                    score = jnp.where(seen, score, NEG)
                scores.append(score)
            peak = functools.reduce(
                jnp.maximum, [jnp.max(score, -1, keepdims=True) for score in scores]
            )
            peak = peak * factor
            exps = [jnp.exp2(score * factor - peak) for score in scores]
            total = functools.reduce(jnp.add, [jnp.sum(e, -1, keepdims=True) for e in exps])
            output = jnp.dot(
                exps[0].astype(jnp.bfloat16), far_value[...], preferred_element_type=jnp.float32
            )
            for other in range(block + 1):
                output += jnp.dot(
                    exps[1 + other].astype(jnp.bfloat16),
                    near[other][:, HD:],
                    preferred_element_type=jnp.float32,
                )
            output = output / total
            if block >= STEMS:
                output = jnp.where(row < lengths_ref[first_block + block], output, 0.0)
            output = output.astype(jnp.bfloat16)
            for head in range(heads):
                lanes = slice(head * HD, (head + 1) * HD)
                held[here, lanes] = output[head * block_len : (head + 1) * block_len]
            copy = pltpu.make_async_copy(
                held.at[pl.ds(block * block_len, block_len)],
                out_ref.at[pl.ds(block * block_len, block_len), pl.ds(first_head * HD, heads * HD)],
                sems.at[block],
            )
            copy.start()
            copies.append(copy)
    for copy in copies:
        copy.wait()


def shards(
    hidden, parents, lengths, gain, w_query, w_key, w_value, query_bias, key_bias, value_bias
):
    blocks, block_len, feature_part = hidden.shape
    tokens = blocks * block_len
    features = gain.shape[0]
    rows = w_query.shape[0]
    columns = w_query.shape[1]
    head_count = columns // HD
    lines = lax.axis_size("fsdp")
    branches = lax.axis_size("branch")
    groups = branches // lines
    far_slots = STEMS * bits_of(branches)
    part = lax.axis_index("fsdp")
    device = lax.axis_index("branch")
    bf16 = jnp.bfloat16
    f32 = jnp.float32
    half_lines = lines // 2
    top = bits_of(half_lines)
    kv_width = 2 * HD

    def swap(array, axis, bit):
        size = lax.axis_size(axis)
        return lax.ppermute(array, axis, [(i, i ^ bit) for i in range(size)])

    def spread(index):
        return ((index & 1) << top) | (index >> 1)

    smem = pl.BlockSpec(memory_space=pltpu.SMEM)
    vmem = pl.BlockSpec(memory_space=pltpu.VMEM)
    anywhere = pl.BlockSpec(memory_space=pl.ANY)
    device_id = device.astype(jnp.int32)[None]
    place = jnp.stack([spread(part), device % groups]).astype(jnp.int32)

    raw = hidden.reshape(tokens, feature_part)
    gain_part = lax.dynamic_slice_in_dim(gain, part * feature_part, feature_part)

    def column(z, feature):
        return (z ^ feature) & (half_lines - 1)

    def middle(z, feature):
        return (column(z, feature) << 1) | ((feature >> top) ^ (z & 1))

    def landing(z, feature):
        return (column(z, feature) << 1) | ((z ^ feature) >> top)

    first_hop = []
    second_hop = []
    for z in range(lines):
        for g in range(groups):
            for feature in range(lines):
                here = z * groups + g
                there = feature * groups + g
                stop = middle(z, feature) * branches + here
                first_hop.append((feature * branches + here, stop))
                second_hop.append((stop, landing(z, feature) * branches + there))
    axes = ("fsdp", "branch")
    head_cuts = [0, (5 * head_count + 7) // 8, head_count]
    w_chunks = [jnp.concatenate([w_key, w_value], 1)] + [
        lax.slice_in_dim(w_query, low * HD, high * HD, axis=1)
        for low, high in zip(head_cuts, head_cuts[1:])
    ]

    cos, sin = pl.pallas_call(
        functools.partial(table_kernel, far_slots, blocks, block_len),
        in_specs=[smem, smem],
        out_specs=[vmem, vmem],
        out_shape=[jax.ShapeDtypeStruct((tokens, HD), f32)] * 2,
        name="tables",
    )(device_id, parents)

    sent = []
    for block in range(blocks):
        piece = (hidden[block].astype(f32) * gain_part).astype(bf16)
        piece = tie(piece, sent[-1], cos, sin, *w_chunks) if block else piece
        sent.append(lax.ppermute(piece, axes, first_hop))

    last_sent = sent[-1]
    sent = [lax.ppermute(piece, axes, second_hop) for piece in sent]
    w_rows = [None] * len(w_chunks)
    arrived = None
    for c in (1, 0, 2):
        outgoing = w_chunks[c] if arrived is None else tie(w_chunks[c], arrived, sent[0])
        w_rows[c] = [w_chunks[c]] + [swap(outgoing, "branch", j) for j in range(1, groups)]
        arrived = w_rows[c][-1]

    sent[0] = tie(sent[0], last_sent)
    last_sent = sent[-1]
    held = [{0: piece} for piece in sent]
    bit = half_lines
    while bit > 1:
        for piece in held:
            for j in list(piece):
                piece[j | bit] = swap(piece[j], "fsdp", bit)
        bit //= 2

    def last_bit(piece):
        for j in list(piece):
            piece[j | 1] = swap(piece[j], "fsdp", 1)
        return [piece[j] for j in sorted(piece, key=spread)]

    assembled = {}
    held[0] = last_bit(held[0])
    held[1] = last_bit(held[1])

    def project(spans, chunks, *after):
        weights = [w for chunk in chunks for w in w_rows[chunk]]
        width = sum(w_chunks[chunk].shape[1] for chunk in chunks)
        fresh = spans[-1] not in assembled
        counts = [high - low for low, high in spans]
        wholes = [assembled[span] for span in spans if span in assembled]
        pieces = []
        if fresh:
            pieces = [held[block][i] for i in range(lines) for block in range(*spans[-1])]
        operands = wholes + pieces
        operands[0] = tie(operands[0], *after) if after else operands[0]
        length = sum(counts) * block_len
        out_specs = [vmem, vmem]
        out_shape = [
            jax.ShapeDtypeStruct((half_lines, length, width), bf16),
            jax.ShapeDtypeStruct((half_lines, length, width), f32),
        ]
        scratch = []
        if fresh:
            out_specs.append(vmem)
            out_shape.append(
                jax.ShapeDtypeStruct((lines * counts[-1] * block_len, feature_part), bf16)
            )
            scratch.append(pltpu.SemaphoreType.DMA((len(pieces),)))
        results = pl.pallas_call(
            functools.partial(project_kernel, lines, groups, len(chunks), counts, fresh),
            in_specs=[smem] + [vmem] * len(wholes) + [anywhere] * len(pieces)
            + [vmem] * len(weights),
            out_specs=out_specs,
            out_shape=out_shape,
            scratch_shapes=scratch,
            compiler_params=pltpu.CompilerParams(vmem_limit_bytes=24 * 2**20),
            cost_estimate=pl.CostEstimate(flops=0, bytes_accessed=0, transcendentals=0),
            name="project",
        )(place, *operands, *weights)
        if fresh:
            assembled[spans[-1]] = results[2]
        return results[0], results[1]

    class Halving:
        def __init__(self, partial):
            self.send, self.total = partial
            self.addends = [self.total]
            self.bit = 1

        def step(self, *after):
            send = tie(self.send, *after) if after else self.send
            self.came = swap(send, "branch", self.bit * groups)
            self.addends.append(self.came)
            self.bit *= 2

        def add(self, *after):
            self.came = tie(self.came, *after) if after else self.came
            self.addends[-1] = self.came
            total = self.total + self.came.astype(f32)
            self.send = total[1::2].astype(bf16)
            self.total = total[0::2]

        def rest(self, *after):
            while self.bit < lines:
                self.add(*after)
                self.step()

    addend_count = 1 + bits_of(lines)

    def lead(array):
        return pl.BlockSpec((1,) + array.shape[1:], lambda i: (0, 0, 0))

    def whole(array):
        return pl.BlockSpec(array.shape, lambda i: (0,) * array.ndim)

    kv_bias = jnp.concatenate([key_bias, value_bias])[None]

    def finish_kv(addends, first, count):
        low, high = first * block_len, (first + count) * block_len
        operands = [inverse[low:high], kv_bias, cos[low:high], sin[low:high]]
        return pl.pallas_call(
            functools.partial(kv_kernel, addend_count),
            grid=(1,),
            in_specs=[whole(x) for x in operands] + [lead(x) for x in addends],
            out_specs=pl.BlockSpec((high - low, kv_width), lambda i: (0, 0)),
            out_shape=jax.ShapeDtypeStruct((high - low, kv_width), bf16),
            compiler_params=pltpu.CompilerParams(vmem_limit_bytes=16 * 2**20),
            name="finish_kv",
        )(*operands, *addends)

    units = [Halving(project([(0, 1)], [0, 1], last_sent))]
    units[0].step()
    for block in range(1, blocks):
        before = units[-1]
        if block > 1:
            held[block] = {j: tie(piece, gate) for j, piece in held[block].items()}
            held[block] = last_bit(held[block])
        units.append(Halving(project([(block, block + 1)], [0, 1], before.send)))
        before.rest(units[-1].send)
        gate = before.send
        units[-1].step(gate)

    squares = jnp.sum(jnp.square(raw.astype(f32)), -1).reshape(blocks, block_len)
    squares = tie(squares, units[STEMS - 1].send)
    bit = 1
    while bit < lines:
        squares = squares + swap(squares, "fsdp", bit)
        bit *= 2
    inverse = lax.rsqrt(squares / features + 1e-06).reshape(tokens)
    inverse = jnp.broadcast_to(inverse[:, None], (tokens, HD))

    last = Halving(project([(b, b + 1) for b in range(blocks)], [2], units[STEMS - 1].send))
    stem_kv = []
    for block in range(STEMS):
        unit = units[block]
        unit.addends[-1] = tie(unit.addends[-1], last.send)
        stem_kv.append(finish_kv(unit.addends, block, 1))

    tour = [groups << i for i in reversed(range(bits_of(lines)))]
    tour += [1 << i for i in range(bits_of(groups))]
    stems = jnp.concatenate(stem_kv, 0)[None]
    came = swap(stems, "branch", tour[0])
    units[-1].rest(stems)
    last.step(units[-1].send)
    for step, bit in enumerate(tour[1:]):
        stems = jnp.concatenate([stems, tie(came, units[-1].send)], 0)
        came = swap(stems, "branch", bit)
    last.rest(stems)
    stems = jnp.concatenate([stems, came], 0)
    late_kv = []
    for block in range(STEMS, blocks):
        unit = units[block]
        unit.addends[-1] = tie(unit.addends[-1], last.send)
        late_kv.append(finish_kv(unit.addends, block, 1))
    keys = stem_kv + late_kv

    def attend(heads, first_head, parts, sums, output):
        operands = [
            inverse, query_bias[None, first_head * HD : (first_head + heads) * HD], cos, sin,
            stems, *keys,
        ]
        in_specs = [smem] * 3 + [whole(x) for x in operands]
        for addends in sums:
            operands += addends
            in_specs += [lead(x) for x in addends]
        aliases = {}
        if output is not None:
            aliases = {3 + len(operands): 0}
            operands.append(output)
            in_specs.append(anywhere)
        kernel = functools.partial(
            attend_kernel, far_slots, block_len, blocks, heads, first_head, parts, addend_count,
            len(aliases), tour,
        )
        length = (far_slots + blocks) * block_len
        return pl.pallas_call(
            kernel,
            grid=(1,),
            in_specs=in_specs,
            out_specs=anywhere,
            scratch_shapes=[
                pltpu.VMEM((far_slots * block_len, HD), bf16),
                pltpu.VMEM((far_slots * block_len, HD), bf16),
                pltpu.VMEM((8, far_slots * block_len), f32),
                pltpu.VMEM((tokens, heads * HD), bf16),
                pltpu.SemaphoreType.DMA((blocks,)),
            ],
            out_shape=jax.ShapeDtypeStruct((tokens, columns), bf16),
            input_output_aliases=aliases,
            compiler_params=pltpu.CompilerParams(vmem_limit_bytes=40 * 2**20),
            cost_estimate=pl.CostEstimate(
                flops=4 * tokens * heads * length * HD,
                bytes_accessed=2 * tokens * heads * HD,
                transcendentals=tokens * heads * length,
            ),
            name="attend",
        )(device_id, parents, lengths, *operands)

    parts = [(block, 1, kv_width) for block in range(blocks)]
    output = attend(head_cuts[1], 0, parts, [unit.addends for unit in units], None)
    output = attend(
        head_count - head_cuts[1], head_cuts[1], [(0, blocks, 0)], [last.addends], output
    )
    return output.reshape(blocks, block_len, columns)


def solution(mesh):
    return jax.shard_map(
        shards,
        mesh=mesh,
        in_specs=(
            P("branch", None, "fsdp"),
            P(),
            P(),
            P(),
            P("branch", "fsdp"),
            P("branch", "fsdp"),
            P("branch", "fsdp"),
            P("fsdp"),
            P("fsdp"),
            P("fsdp"),
        ),
        out_specs=P("branch", None, "fsdp"),
        check_vma=False,
    )
```

```python
import functools
import math

import jax
import jax.numpy as jnp
from jax import lax
from jax.experimental import pallas as pl
from jax.experimental.pallas import tpu as pltpu
from jax.sharding import PartitionSpec as P

HD = 128
STEMS = 2
THETA = 1000000.0
NEG = -1e30


def bits_of(count):
    return count.bit_length() - 1


def tie(array, *others):
    return lax.optimization_barrier((array,) + others)[0]


def far_chain(parents_ref, first_block, far_slots):
    cursor = parents_ref[first_block]
    ids = []
    total = jnp.int32(0)
    for level in range(far_slots):
        ids.append(cursor)
        total = total + jnp.where(cursor >= 0, 1, 0)
        above = parents_ref[jnp.maximum(cursor, 0)]
        cursor = jnp.where(cursor >= 0, above, -1)
    return ids, total


def add_up(refs, inverse, bias, columns):
    total = refs[0][0, :, columns]
    for ref in refs[1:]:
        total = total + ref[0, :, columns].astype(jnp.float32)
    repeats = total.shape[1] // HD
    inverse = jnp.concatenate([inverse] * repeats, 1)
    return jnp.where(inverse > 0, total * inverse, 0.0) + bias


def turn(vectors, cos, sin):
    half = vectors.shape[-1] // 2
    return vectors * cos + pltpu.roll(vectors, half, 1) * sin


def table_kernel(far_slots, blocks, block_len, device_ref, parents_ref, cos_ref, sin_ref):
    tokens = cos_ref.shape[0]
    unused, far_total = far_chain(parents_ref, device_ref[0] * blocks, far_slots)
    rows = lax.broadcasted_iota(jnp.int32, (tokens, HD), 0)
    lanes = lax.broadcasted_iota(jnp.int32, (tokens, HD), 1)
    front = lanes < HD // 2
    pair = jnp.where(front, lanes, lanes - HD // 2).astype(jnp.float32)
    freqs = jnp.exp(pair * (-2.0 * math.log(THETA) / HD))
    angles = (rows + far_total * block_len).astype(jnp.float32) * freqs
    sin = jnp.sin(angles)
    cos_ref[...] = jnp.cos(angles)
    sin_ref[...] = jnp.where(front, -sin, sin)


def assemble(lines, blocks, place_ref, pieces, held, sems):
    half = lines // 2
    block_len = pieces[0].shape[0]
    copies = []
    for i in range(lines):
        target = lax.bitwise_xor(jnp.int32(i), place_ref[0])
        slot = jnp.where(target % 2 == 0, half, 0) + target // 2
        for block in range(blocks):
            begin = pl.multiple_of((slot * blocks + block) * block_len, block_len)
            n = i * blocks + block
            there = held.at[pl.ds(begin, block_len)]
            copies.append(pltpu.make_async_copy(pieces[n], there, sems.at[n]))
    for copy in copies:
        copy.start()
    return copies


def project_kernel(lines, groups, chunks, counts, fresh, place_ref, *refs):
    fresh_count = lines * counts[-1] if fresh else 0
    whole_count = len(counts) - (1 if fresh else 0)
    wholes = list(refs[:whole_count])
    pieces = refs[whole_count : whole_count + fresh_count]
    refs = refs[whole_count + fresh_count :]
    weights = refs[: groups * chunks]
    outs = refs[groups * chunks :]
    send_ref, keep_ref = outs[:2]
    if fresh:
        held, sems = outs[2:]
        for copy in assemble(lines, counts[-1], place_ref, pieces, held, sems):
            copy.wait()
        wholes.append(held)
    half = lines // 2
    rows = weights[0].shape[0]
    length = send_ref.shape[1]
    begin = 0
    for held, count in zip(wholes, counts):
        share = held.shape[0] // lines
        middle = half * share
        start = 0
        for chunk in range(chunks):
            width = weights[chunk * groups].shape[1]
            for out_ref, low in ((send_ref, 0), (keep_ref, middle)):
                total = None
                for g in range(groups):
                    member = lax.bitwise_xor(place_ref[1], jnp.int32(g))
                    lanes = pl.ds(pl.multiple_of(member * rows, rows), rows)
                    term = jnp.dot(
                        held[low : low + middle, lanes],
                        weights[chunk * groups + g][...],
                        preferred_element_type=jnp.float32,
                    )
                    total = term if total is None else total + term
                total = total.astype(out_ref.dtype).reshape(half, share, width)
                out_ref[:, begin : begin + share, start : start + width] = total
            start += width
        begin += share


def kv_kernel(addends, inverse_ref, bias_ref, cos_ref, sin_ref, *refs):
    kv_ref = refs[-1]
    both = add_up(refs[:addends], inverse_ref[...], bias_ref[...], slice(0, 2 * HD))
    kv_ref[:, :HD] = turn(both[:, :HD], cos_ref[...], sin_ref[...]).astype(jnp.bfloat16)
    kv_ref[:, HD:] = both[:, HD:].astype(jnp.bfloat16)


def attend_kernel(
    far_slots, block_len, blocks, heads, first_head, parts, addends, aliased, tour, device_ref,
    parents_ref, lengths_ref, inverse_ref, bias_ref, cos_ref, sin_ref, stems_ref, *refs,
):
    near = refs[:blocks]
    refs = refs[blocks:]
    sums = [refs[p * addends : (p + 1) * addends] for p in range(len(parts))]
    refs = refs[len(parts) * addends + aliased :]
    out_ref, far_key, far_value, far_mask, held, sems = refs
    device = device_ref[0]
    first_block = device * blocks
    ids, unused = far_chain(parents_ref, first_block, far_slots)
    for level in range(far_slots):
        live = ids[level] >= 0
        safe = jnp.maximum(ids[level], 0)
        owner = lax.div(safe, jnp.int32(blocks))
        inner = lax.rem(safe, jnp.int32(blocks))
        apart = lax.bitwise_xor(owner, device)
        where = jnp.int32(0)
        for step, bit in enumerate(tour):
            where = where + jnp.where(lax.bitwise_and(apart, bit) != 0, 1 << step, 0)
        start = pl.multiple_of(inner * block_len, block_len)
        here = pl.ds(level * block_len, block_len)
        far_key[here, :] = stems_ref[where, pl.ds(start, block_len), :HD]
        far_value[here, :] = stems_ref[where, pl.ds(start, block_len), HD:]
        far_mask[:, here] = jnp.broadcast_to(jnp.where(live, 0.0, NEG), (8, block_len))

    factor = HD ** (-0.5) * math.log2(math.e)
    contract = (((1,), (1,)), ((), ()))
    rows = heads * block_len
    column = lax.broadcasted_iota(jnp.int32, (rows, block_len), 1)
    row = lax.broadcasted_iota(jnp.int32, (rows, block_len), 0) % block_len
    copies = []
    for p, (first, count, offset) in enumerate(parts):
        for inside in range(count):
            block = first + inside
            here = slice(block * block_len, (block + 1) * block_len)
            mine = slice(inside * block_len, (inside + 1) * block_len)
            total = sums[p][0][0, mine, offset : offset + heads * HD]
            for ref in sums[p][1:]:
                total = total + ref[0, mine, offset : offset + heads * HD].astype(jnp.float32)
            inverse = inverse_ref[here]
            query = []
            for head in range(heads):
                lanes = slice(head * HD, (head + 1) * HD)
                one = jnp.where(inverse > 0, total[:, lanes] * inverse, 0.0)
                one = one + bias_ref[:, lanes]
                query.append(turn(one, cos_ref[here], sin_ref[here]).astype(jnp.bfloat16))
            query = jnp.concatenate(query, 0)
            far = lax.dot_general(
                query, far_key[...], contract, preferred_element_type=jnp.float32
            )
            scores = [far + far_mask[0:1, :]]
            for other in range(block + 1):
                score = lax.dot_general(
                    query, near[other][:, :HD], contract, preferred_element_type=jnp.float32
                )
                if other == block or other >= STEMS:
                    seen = column < lengths_ref[first_block + other]
                    if other == block:
                        seen = seen & (column <= row)
                    score = jnp.where(seen, score, NEG)
                scores.append(score)
            peak = functools.reduce(
                jnp.maximum, [jnp.max(score, -1, keepdims=True) for score in scores]
            )
            peak = peak * factor
            exps = [jnp.exp2(score * factor - peak) for score in scores]
            total = functools.reduce(jnp.add, [jnp.sum(e, -1, keepdims=True) for e in exps])
            output = jnp.dot(
                exps[0].astype(jnp.bfloat16), far_value[...], preferred_element_type=jnp.float32
            )
            for other in range(block + 1):
                output += jnp.dot(
                    exps[1 + other].astype(jnp.bfloat16),
                    near[other][:, HD:],
                    preferred_element_type=jnp.float32,
                )
            output = output / total
            if block >= STEMS:
                output = jnp.where(row < lengths_ref[first_block + block], output, 0.0)
            output = output.astype(jnp.bfloat16)
            for head in range(heads):
                lanes = slice(head * HD, (head + 1) * HD)
                held[here, lanes] = output[head * block_len : (head + 1) * block_len]
            copy = pltpu.make_async_copy(
                held.at[pl.ds(block * block_len, block_len)],
                out_ref.at[pl.ds(block * block_len, block_len), pl.ds(first_head * HD, heads * HD)],
                sems.at[block],
            )
            copy.start()
            copies.append(copy)
    for copy in copies:
        copy.wait()


def shards(
    hidden, parents, lengths, gain, w_query, w_key, w_value, query_bias, key_bias, value_bias
):
    blocks, block_len, feature_part = hidden.shape
    tokens = blocks * block_len
    features = gain.shape[0]
    rows = w_query.shape[0]
    columns = w_query.shape[1]
    head_count = columns // HD
    lines = lax.axis_size("fsdp")
    branches = lax.axis_size("branch")
    groups = branches // lines
    far_slots = STEMS * bits_of(branches)
    part = lax.axis_index("fsdp")
    device = lax.axis_index("branch")
    bf16 = jnp.bfloat16
    f32 = jnp.float32
    half_lines = lines // 2
    top = bits_of(half_lines)
    kv_width = 2 * HD

    def swap(array, axis, bit):
        size = lax.axis_size(axis)
        return lax.ppermute(array, axis, [(i, i ^ bit) for i in range(size)])

    def spread(index):
        return ((index & 1) << top) | (index >> 1)

    smem = pl.BlockSpec(memory_space=pltpu.SMEM)
    vmem = pl.BlockSpec(memory_space=pltpu.VMEM)
    anywhere = pl.BlockSpec(memory_space=pl.ANY)
    device_id = device.astype(jnp.int32)[None]
    place = jnp.stack([spread(part), device % groups]).astype(jnp.int32)

    raw = hidden.reshape(tokens, feature_part)
    gain_part = lax.dynamic_slice_in_dim(gain, part * feature_part, feature_part)

    def column(z, feature):
        return (z ^ feature) & (half_lines - 1)

    def middle(z, feature):
        return (column(z, feature) << 1) | ((feature >> top) ^ (z & 1))

    def landing(z, feature):
        return (column(z, feature) << 1) | ((z ^ feature) >> top)

    first_hop = []
    second_hop = []
    both_hops = []
    for z in range(lines):
        for g in range(groups):
            for feature in range(lines):
                here = z * groups + g
                there = feature * groups + g
                stop = middle(z, feature) * branches + here
                first_hop.append((feature * branches + here, stop))
                end = landing(z, feature) * branches + there
                second_hop.append((stop, end))
                both_hops.append((feature * branches + here, end))
    axes = ("fsdp", "branch")
    head_cuts = [0, (5 * head_count + 7) // 8, head_count]
    w_chunks = [jnp.concatenate([w_key, w_value], 1)] + [
        lax.slice_in_dim(w_query, low * HD, high * HD, axis=1)
        for low, high in zip(head_cuts, head_cuts[1:])
    ]

    cos, sin = pl.pallas_call(
        functools.partial(table_kernel, far_slots, blocks, block_len),
        in_specs=[smem, smem],
        out_specs=[vmem, vmem],
        out_shape=[jax.ShapeDtypeStruct((tokens, HD), f32)] * 2,
        name="tables",
    )(device_id, parents)

    scaled = [(hidden[block].astype(f32) * gain_part).astype(bf16) for block in range(blocks)]
    sent = [lax.ppermute(scaled[0], axes, both_hops)]
    for block in range(1, blocks):
        piece = tie(scaled[block], sent[-1], cos, sin, *w_chunks) if block > 1 else scaled[block]
        sent.append(lax.ppermute(piece, axes, first_hop))
    last_sent = sent[-1]
    sent = sent[:1] + [lax.ppermute(piece, axes, second_hop) for piece in sent[1:]]
    w_rows = [None] * len(w_chunks)
    arrived = None
    for c in (1, 0, 2):
        outgoing = w_chunks[c] if arrived is None else tie(w_chunks[c], arrived, sent[0])
        w_rows[c] = [w_chunks[c]] + [swap(outgoing, "branch", j) for j in range(1, groups)]
        arrived = w_rows[c][-1]

    sent[0] = tie(sent[0], last_sent)
    sent[1] = tie(sent[1], w_rows[1][-1])
    last_sent = sent[-1]
    held = [{0: piece} for piece in sent]
    bit = half_lines
    while bit > 1:
        for piece in held:
            for j in list(piece):
                piece[j | bit] = swap(piece[j], "fsdp", bit)
        bit //= 2

    def last_bit(piece):
        for j in list(piece):
            piece[j | 1] = swap(piece[j], "fsdp", 1)
        return [piece[j] for j in sorted(piece, key=spread)]

    assembled = {}
    held[0] = last_bit(held[0])
    held[1] = last_bit(held[1])

    def project(spans, chunks, *after):
        weights = [w for chunk in chunks for w in w_rows[chunk]]
        width = sum(w_chunks[chunk].shape[1] for chunk in chunks)
        fresh = spans[-1] not in assembled
        counts = [high - low for low, high in spans]
        wholes = [assembled[span] for span in spans if span in assembled]
        pieces = []
        if fresh:
            pieces = [held[block][i] for i in range(lines) for block in range(*spans[-1])]
        operands = wholes + pieces
        operands[0] = tie(operands[0], *after) if after else operands[0]
        length = sum(counts) * block_len
        out_specs = [vmem, vmem]
        out_shape = [
            jax.ShapeDtypeStruct((half_lines, length, width), bf16),
            jax.ShapeDtypeStruct((half_lines, length, width), f32),
        ]
        scratch = []
        if fresh:
            out_specs.append(vmem)
            out_shape.append(
                jax.ShapeDtypeStruct((lines * counts[-1] * block_len, feature_part), bf16)
            )
            scratch.append(pltpu.SemaphoreType.DMA((len(pieces),)))
        results = pl.pallas_call(
            functools.partial(project_kernel, lines, groups, len(chunks), counts, fresh),
            in_specs=[smem] + [vmem] * len(wholes) + [anywhere] * len(pieces)
            + [vmem] * len(weights),
            out_specs=out_specs,
            out_shape=out_shape,
            scratch_shapes=scratch,
            compiler_params=pltpu.CompilerParams(vmem_limit_bytes=24 * 2**20),
            cost_estimate=pl.CostEstimate(flops=0, bytes_accessed=0, transcendentals=0),
            name="project",
        )(place, *operands, *weights)
        if fresh:
            assembled[spans[-1]] = results[2]
        return results[0], results[1]

    class Halving:
        def __init__(self, partial):
            self.send, self.total = partial
            self.addends = [self.total]
            self.bit = 1

        def step(self, *after):
            send = tie(self.send, *after) if after else self.send
            self.came = swap(send, "branch", self.bit * groups)
            self.addends.append(self.came)
            self.bit *= 2

        def add(self, *after):
            self.came = tie(self.came, *after) if after else self.came
            self.addends[-1] = self.came
            total = self.total + self.came.astype(f32)
            self.send = total[1::2].astype(bf16)
            self.total = total[0::2]

        def rest(self, *after):
            while self.bit < lines:
                self.add(*after)
                self.step()

    addend_count = 1 + bits_of(lines)

    def lead(array):
        return pl.BlockSpec((1,) + array.shape[1:], lambda i: (0, 0, 0))

    def whole(array):
        return pl.BlockSpec(array.shape, lambda i: (0,) * array.ndim)

    kv_bias = jnp.concatenate([key_bias, value_bias])[None]

    def finish_kv(addends, first, count):
        low, high = first * block_len, (first + count) * block_len
        operands = [inverse[low:high], kv_bias, cos[low:high], sin[low:high]]
        return pl.pallas_call(
            functools.partial(kv_kernel, addend_count),
            grid=(1,),
            in_specs=[whole(x) for x in operands] + [lead(x) for x in addends],
            out_specs=pl.BlockSpec((high - low, kv_width), lambda i: (0, 0)),
            out_shape=jax.ShapeDtypeStruct((high - low, kv_width), bf16),
            compiler_params=pltpu.CompilerParams(vmem_limit_bytes=16 * 2**20),
            name="finish_kv",
        )(*operands, *addends)

    units = [Halving(project([(0, 1)], [0, 1], last_sent))]
    units[0].step()
    for block in range(1, blocks):
        before = units[-1]
        gate = before.came
        before.rest()
        if block > 1:
            held[block] = {j: tie(piece, gate) for j, piece in held[block].items()}
            held[block] = last_bit(held[block])
        units.append(Halving(project([(block, block + 1)], [0, 1], before.send)))
        units[-1].step()

    squares = jnp.sum(jnp.square(raw.astype(f32)), -1).reshape(blocks, block_len)
    squares = tie(squares, units[STEMS - 1].send)
    bit = 1
    while bit < lines:
        squares = squares + swap(squares, "fsdp", bit)
        bit *= 2
    inverse = lax.rsqrt(squares / features + 1e-06).reshape(tokens)
    inverse = jnp.broadcast_to(inverse[:, None], (tokens, HD))

    stem_kv = []
    for block in range(STEMS):
        unit = units[block]
        unit.addends[-1] = tie(unit.addends[-1], units[-1].send)
        stem_kv.append(finish_kv(unit.addends, block, 1))

    tour = [groups << i for i in reversed(range(bits_of(lines)))]
    tour += [1 << i for i in range(bits_of(groups))]
    stems = jnp.concatenate(stem_kv, 0)[None]
    came = swap(stems, "branch", tour[0])
    last = Halving(project([(b, b + 1) for b in range(blocks)], [2], stems))
    last.step()
    units[-1].rest(last.send)
    for step, bit in enumerate(tour[1:]):
        stems = jnp.concatenate([stems, tie(came, units[-1].send)], 0)
        came = swap(stems, "branch", bit)
    last.rest(stems)
    stems = jnp.concatenate([stems, came], 0)
    late_kv = []
    for block in range(STEMS, blocks):
        unit = units[block]
        unit.addends[-1] = tie(unit.addends[-1], last.send)
        late_kv.append(finish_kv(unit.addends, block, 1))
    keys = stem_kv + late_kv

    def attend(heads, first_head, parts, sums, output):
        operands = [
            inverse, query_bias[None, first_head * HD : (first_head + heads) * HD], cos, sin,
            stems, *keys,
        ]
        in_specs = [smem] * 3 + [whole(x) for x in operands]
        for addends in sums:
            operands += addends
            in_specs += [lead(x) for x in addends]
        aliases = {}
        if output is not None:
            aliases = {3 + len(operands): 0}
            operands.append(output)
            in_specs.append(anywhere)
        kernel = functools.partial(
            attend_kernel, far_slots, block_len, blocks, heads, first_head, parts, addend_count,
            len(aliases), tour,
        )
        length = (far_slots + blocks) * block_len
        return pl.pallas_call(
            kernel,
            grid=(1,),
            in_specs=in_specs,
            out_specs=anywhere,
            scratch_shapes=[
                pltpu.VMEM((far_slots * block_len, HD), bf16),
                pltpu.VMEM((far_slots * block_len, HD), bf16),
                pltpu.VMEM((8, far_slots * block_len), f32),
                pltpu.VMEM((tokens, heads * HD), bf16),
                pltpu.SemaphoreType.DMA((blocks,)),
            ],
            out_shape=jax.ShapeDtypeStruct((tokens, columns), bf16),
            input_output_aliases=aliases,
            compiler_params=pltpu.CompilerParams(vmem_limit_bytes=40 * 2**20),
            cost_estimate=pl.CostEstimate(
                flops=4 * tokens * heads * length * HD,
                bytes_accessed=2 * tokens * heads * HD,
                transcendentals=tokens * heads * length,
            ),
            name="attend",
        )(device_id, parents, lengths, *operands)

    parts = [(block, 1, kv_width) for block in range(blocks)]
    output = attend(head_cuts[1], 0, parts, [unit.addends for unit in units], None)
    output = attend(
        head_count - head_cuts[1], head_cuts[1], [(0, blocks, 0)], [last.addends], output
    )
    return output.reshape(blocks, block_len, columns)


def solution(mesh):
    return jax.shard_map(
        shards,
        mesh=mesh,
        in_specs=(
            P("branch", None, "fsdp"),
            P(),
            P(),
            P(),
            P("branch", "fsdp"),
            P("branch", "fsdp"),
            P("branch", "fsdp"),
            P("fsdp"),
            P("fsdp"),
            P("fsdp"),
        ),
        out_specs=P("branch", None, "fsdp"),
        check_vma=False,
    )
```

```python
import functools
import math

import jax
import jax.numpy as jnp
from jax import lax
from jax.experimental import pallas as pl
from jax.experimental.pallas import tpu as pltpu
from jax.sharding import PartitionSpec as P

HD = 128
STEMS = 2
THETA = 1000000.0
NEG = -1e30


def bits_of(count):
    return count.bit_length() - 1


def tie(array, *others):
    return lax.optimization_barrier((array,) + others)[0]


def far_chain(parents_ref, first_block, far_slots):
    cursor = parents_ref[first_block]
    ids = []
    total = jnp.int32(0)
    for level in range(far_slots):
        ids.append(cursor)
        total = total + jnp.where(cursor >= 0, 1, 0)
        above = parents_ref[jnp.maximum(cursor, 0)]
        cursor = jnp.where(cursor >= 0, above, -1)
    return ids, total


def add_up(refs, inverse, bias, columns):
    total = refs[0][0, :, columns]
    for ref in refs[1:]:
        total = total + ref[0, :, columns].astype(jnp.float32)
    repeats = total.shape[1] // HD
    inverse = jnp.concatenate([inverse] * repeats, 1)
    return jnp.where(inverse > 0, total * inverse, 0.0) + bias


def turn(vectors, cos, sin):
    half = vectors.shape[-1] // 2
    return vectors * cos + pltpu.roll(vectors, half, 1) * sin


def table_kernel(far_slots, blocks, block_len, device_ref, parents_ref, cos_ref, sin_ref):
    tokens = cos_ref.shape[0]
    unused, far_total = far_chain(parents_ref, device_ref[0] * blocks, far_slots)
    rows = lax.broadcasted_iota(jnp.int32, (tokens, HD), 0)
    lanes = lax.broadcasted_iota(jnp.int32, (tokens, HD), 1)
    front = lanes < HD // 2
    pair = jnp.where(front, lanes, lanes - HD // 2).astype(jnp.float32)
    freqs = jnp.exp(pair * (-2.0 * math.log(THETA) / HD))
    angles = (rows + far_total * block_len).astype(jnp.float32) * freqs
    sin = jnp.sin(angles)
    cos_ref[...] = jnp.cos(angles)
    sin_ref[...] = jnp.where(front, -sin, sin)


def assemble(lines, blocks, place_ref, pieces, held, sems):
    half = lines // 2
    block_len = pieces[0].shape[0]
    copies = []
    for i in range(lines):
        target = lax.bitwise_xor(jnp.int32(i), place_ref[0])
        slot = jnp.where(target % 2 == 0, half, 0) + target // 2
        for block in range(blocks):
            begin = pl.multiple_of((slot * blocks + block) * block_len, block_len)
            n = i * blocks + block
            there = held.at[pl.ds(begin, block_len)]
            copies.append(pltpu.make_async_copy(pieces[n], there, sems.at[n]))
    for copy in copies:
        copy.start()
    return copies


def project_kernel(lines, groups, chunks, counts, fresh, place_ref, *refs):
    fresh_count = lines * counts[-1] if fresh else 0
    whole_count = len(counts) - (1 if fresh else 0)
    wholes = list(refs[:whole_count])
    pieces = refs[whole_count : whole_count + fresh_count]
    refs = refs[whole_count + fresh_count :]
    weights = refs[: groups * chunks]
    outs = refs[groups * chunks :]
    send_ref, keep_ref = outs[:2]
    if fresh:
        held, sems = outs[2:]
        for copy in assemble(lines, counts[-1], place_ref, pieces, held, sems):
            copy.wait()
        wholes.append(held)
    half = lines // 2
    rows = weights[0].shape[0]
    length = send_ref.shape[1]
    begin = 0
    for held, count in zip(wholes, counts):
        share = held.shape[0] // lines
        middle = half * share
        start = 0
        for chunk in range(chunks):
            width = weights[chunk * groups].shape[1]
            for out_ref, low in ((send_ref, 0), (keep_ref, middle)):
                total = None
                for g in range(groups):
                    member = lax.bitwise_xor(place_ref[1], jnp.int32(g))
                    lanes = pl.ds(pl.multiple_of(member * rows, rows), rows)
                    term = jnp.dot(
                        held[low : low + middle, lanes],
                        weights[chunk * groups + g][...],
                        preferred_element_type=jnp.float32,
                    )
                    total = term if total is None else total + term
                total = total.astype(out_ref.dtype).reshape(half, share, width)
                out_ref[:, begin : begin + share, start : start + width] = total
            start += width
        begin += share


def kv_kernel(addends, inverse_ref, bias_ref, cos_ref, sin_ref, *refs):
    kv_ref = refs[-1]
    both = add_up(refs[:addends], inverse_ref[...], bias_ref[...], slice(0, 2 * HD))
    kv_ref[:, :HD] = turn(both[:, :HD], cos_ref[...], sin_ref[...]).astype(jnp.bfloat16)
    kv_ref[:, HD:] = both[:, HD:].astype(jnp.bfloat16)


def attend_kernel(
    far_slots, block_len, blocks, heads, first_head, parts, addends, aliased, tour, device_ref,
    parents_ref, lengths_ref, inverse_ref, bias_ref, cos_ref, sin_ref, stems_ref, *refs,
):
    keys = refs[:2]
    refs = refs[2:]
    sums = [refs[p * addends : (p + 1) * addends] for p in range(len(parts))]
    refs = refs[len(parts) * addends + aliased :]
    out_ref, far_key, far_value, far_mask, held, sems = refs
    device = device_ref[0]
    first_block = device * blocks
    ids, unused = far_chain(parents_ref, first_block, far_slots)
    for level in range(far_slots):
        live = ids[level] >= 0
        safe = jnp.maximum(ids[level], 0)
        owner = lax.div(safe, jnp.int32(blocks))
        inner = lax.rem(safe, jnp.int32(blocks))
        apart = lax.bitwise_xor(owner, device)
        where = jnp.int32(0)
        for step, bit in enumerate(tour):
            where = where + jnp.where(lax.bitwise_and(apart, bit) != 0, 1 << step, 0)
        start = pl.multiple_of(inner * block_len, block_len)
        here = pl.ds(level * block_len, block_len)
        far_key[here, :] = stems_ref[where, pl.ds(start, block_len), :HD]
        far_value[here, :] = stems_ref[where, pl.ds(start, block_len), HD:]
        far_mask[:, here] = jnp.broadcast_to(jnp.where(live, 0.0, NEG), (8, block_len))

    factor = HD ** (-0.5) * math.log2(math.e)
    contract = (((1,), (1,)), ((), ()))
    rows = heads * block_len
    column = lax.broadcasted_iota(jnp.int32, (rows, block_len), 1)
    row = lax.broadcasted_iota(jnp.int32, (rows, block_len), 0) % block_len
    near = [(keys[0], block * block_len) for block in range(STEMS)]
    near += [(keys[1], (block - STEMS) * block_len) for block in range(STEMS, blocks)]
    copies = []
    for p, (first, count, offset) in enumerate(parts):
        for inside in range(count):
            block = first + inside
            here = slice(block * block_len, (block + 1) * block_len)
            mine = slice(inside * block_len, (inside + 1) * block_len)
            total = sums[p][0][0, mine, offset : offset + heads * HD]
            for ref in sums[p][1:]:
                total = total + ref[0, mine, offset : offset + heads * HD].astype(jnp.float32)
            inverse = inverse_ref[here]
            query = []
            for head in range(heads):
                lanes = slice(head * HD, (head + 1) * HD)
                one = jnp.where(inverse > 0, total[:, lanes] * inverse, 0.0)
                one = one + bias_ref[:, lanes]
                query.append(turn(one, cos_ref[here], sin_ref[here]).astype(jnp.bfloat16))
            query = jnp.concatenate(query, 0)
            far = lax.dot_general(
                query, far_key[...], contract, preferred_element_type=jnp.float32
            )
            scores = [far + far_mask[0:1, :]]
            for other in range(block + 1):
                ref, begin = near[other]
                score = lax.dot_general(
                    query,
                    ref[begin : begin + block_len, :HD],
                    contract,
                    preferred_element_type=jnp.float32,
                )
                if other == block or other >= STEMS:
                    seen = column < lengths_ref[first_block + other]
                    if other == block:
                        seen = seen & (column <= row)
                    score = jnp.where(seen, score, NEG)
                scores.append(score)
            peak = functools.reduce(
                jnp.maximum, [jnp.max(score, -1, keepdims=True) for score in scores]
            )
            peak = peak * factor
            exps = [jnp.exp2(score * factor - peak) for score in scores]
            total = functools.reduce(jnp.add, [jnp.sum(e, -1, keepdims=True) for e in exps])
            output = jnp.dot(
                exps[0].astype(jnp.bfloat16), far_value[...], preferred_element_type=jnp.float32
            )
            for other in range(block + 1):
                ref, begin = near[other]
                output += jnp.dot(
                    exps[1 + other].astype(jnp.bfloat16),
                    ref[begin : begin + block_len, HD:],
                    preferred_element_type=jnp.float32,
                )
            output = output / total
            if block >= STEMS:
                output = jnp.where(row < lengths_ref[first_block + block], output, 0.0)
            output = output.astype(jnp.bfloat16)
            for head in range(heads):
                lanes = slice(head * HD, (head + 1) * HD)
                held[here, lanes] = output[head * block_len : (head + 1) * block_len]
            copy = pltpu.make_async_copy(
                held.at[pl.ds(block * block_len, block_len)],
                out_ref.at[pl.ds(block * block_len, block_len), pl.ds(first_head * HD, heads * HD)],
                sems.at[block],
            )
            copy.start()
            copies.append(copy)
    for copy in copies:
        copy.wait()


def shards(
    hidden, parents, lengths, gain, w_query, w_key, w_value, query_bias, key_bias, value_bias
):
    blocks, block_len, feature_part = hidden.shape
    tokens = blocks * block_len
    features = gain.shape[0]
    rows = w_query.shape[0]
    columns = w_query.shape[1]
    head_count = columns // HD
    lines = lax.axis_size("fsdp")
    branches = lax.axis_size("branch")
    groups = branches // lines
    far_slots = STEMS * bits_of(branches)
    part = lax.axis_index("fsdp")
    device = lax.axis_index("branch")
    bf16 = jnp.bfloat16
    f32 = jnp.float32
    half_lines = lines // 2
    top = bits_of(half_lines)
    kv_width = 2 * HD

    def swap(array, axis, bit):
        size = lax.axis_size(axis)
        return lax.ppermute(array, axis, [(i, i ^ bit) for i in range(size)])

    def spread(index):
        return ((index & 1) << top) | (index >> 1)

    smem = pl.BlockSpec(memory_space=pltpu.SMEM)
    vmem = pl.BlockSpec(memory_space=pltpu.VMEM)
    anywhere = pl.BlockSpec(memory_space=pl.ANY)
    device_id = device.astype(jnp.int32)[None]
    place = jnp.stack([spread(part), device % groups]).astype(jnp.int32)

    raw = hidden.reshape(tokens, feature_part)
    gain_part = lax.dynamic_slice_in_dim(gain, part * feature_part, feature_part)

    def column(z, feature):
        return (z ^ feature) & (half_lines - 1)

    def middle(z, feature):
        return (column(z, feature) << 1) | ((feature >> top) ^ (z & 1))

    def landing(z, feature):
        return (column(z, feature) << 1) | ((z ^ feature) >> top)

    first_hop = []
    second_hop = []
    for z in range(lines):
        for g in range(groups):
            for feature in range(lines):
                here = z * groups + g
                there = feature * groups + g
                stop = middle(z, feature) * branches + here
                first_hop.append((feature * branches + here, stop))
                second_hop.append((stop, landing(z, feature) * branches + there))
    axes = ("fsdp", "branch")
    head_cuts = [0, (5 * head_count + 7) // 8, head_count]
    w_chunks = [jnp.concatenate([w_key, w_value], 1)] + [
        lax.slice_in_dim(w_query, low * HD, high * HD, axis=1)
        for low, high in zip(head_cuts, head_cuts[1:])
    ]

    cos, sin = pl.pallas_call(
        functools.partial(table_kernel, far_slots, blocks, block_len),
        in_specs=[smem, smem],
        out_specs=[vmem, vmem],
        out_shape=[jax.ShapeDtypeStruct((tokens, HD), f32)] * 2,
        name="tables",
    )(device_id, parents)

    sent = []
    for block in range(blocks):
        piece = (hidden[block].astype(f32) * gain_part).astype(bf16)
        piece = tie(piece, sent[-1], cos, sin, *w_chunks) if block else piece
        sent.append(lax.ppermute(piece, axes, first_hop))

    last_sent = sent[-1]
    sent = [lax.ppermute(piece, axes, second_hop) for piece in sent]
    w_rows = [None] * len(w_chunks)
    arrived = None
    for c in (1, 0, 2):
        outgoing = w_chunks[c] if arrived is None else tie(w_chunks[c], arrived, sent[1])
        w_rows[c] = [w_chunks[c]] + [swap(outgoing, "branch", j) for j in range(1, groups)]
        arrived = w_rows[c][-1]

    sent[0] = tie(sent[0], last_sent)
    sent[1] = tie(sent[1], w_rows[1][-1])
    last_sent = sent[-1]
    held = [{0: piece} for piece in sent]
    bit = half_lines
    while bit > 1:
        for piece in held:
            for j in list(piece):
                piece[j | bit] = swap(piece[j], "fsdp", bit)
        bit //= 2

    def last_bit(piece):
        for j in list(piece):
            piece[j | 1] = swap(piece[j], "fsdp", 1)
        return [piece[j] for j in sorted(piece, key=spread)]

    assembled = {}
    held[0] = last_bit(held[0])
    held[1] = last_bit(held[1])

    def project(spans, chunks, *after):
        weights = [w for chunk in chunks for w in w_rows[chunk]]
        width = sum(w_chunks[chunk].shape[1] for chunk in chunks)
        fresh = spans[-1] not in assembled
        counts = [high - low for low, high in spans]
        wholes = [assembled[span] for span in spans if span in assembled]
        pieces = []
        if fresh:
            pieces = [held[block][i] for i in range(lines) for block in range(*spans[-1])]
        operands = wholes + pieces
        operands[0] = tie(operands[0], *after) if after else operands[0]
        length = sum(counts) * block_len
        out_specs = [vmem, vmem]
        out_shape = [
            jax.ShapeDtypeStruct((half_lines, length, width), bf16),
            jax.ShapeDtypeStruct((half_lines, length, width), f32),
        ]
        scratch = []
        if fresh:
            out_specs.append(vmem)
            out_shape.append(
                jax.ShapeDtypeStruct((lines * counts[-1] * block_len, feature_part), bf16)
            )
            scratch.append(pltpu.SemaphoreType.DMA((len(pieces),)))
        results = pl.pallas_call(
            functools.partial(project_kernel, lines, groups, len(chunks), counts, fresh),
            in_specs=[smem] + [vmem] * len(wholes) + [anywhere] * len(pieces)
            + [vmem] * len(weights),
            out_specs=out_specs,
            out_shape=out_shape,
            scratch_shapes=scratch,
            compiler_params=pltpu.CompilerParams(vmem_limit_bytes=24 * 2**20),
            cost_estimate=pl.CostEstimate(flops=0, bytes_accessed=0, transcendentals=0),
            name="project",
        )(place, *operands, *weights)
        if fresh:
            assembled[spans[-1]] = results[2]
        return results[0], results[1]

    class Halving:
        def __init__(self, partial):
            self.send, self.total = partial
            self.addends = [self.total]
            self.bit = 1

        def step(self, *after):
            send = tie(self.send, *after) if after else self.send
            self.came = swap(send, "branch", self.bit * groups)
            self.addends.append(self.came)
            self.bit *= 2

        def add(self, *after):
            self.came = tie(self.came, *after) if after else self.came
            self.addends[-1] = self.came
            total = self.total + self.came.astype(f32)
            self.send = total[1::2].astype(bf16)
            self.total = total[0::2]

        def rest(self, *after):
            while self.bit < lines:
                self.add(*after)
                self.step()

    addend_count = 1 + bits_of(lines)

    def lead(array):
        return pl.BlockSpec((1,) + array.shape[1:], lambda i: (0, 0, 0))

    def whole(array):
        return pl.BlockSpec(array.shape, lambda i: (0,) * array.ndim)

    kv_bias = jnp.concatenate([key_bias, value_bias])[None]

    def finish_kv(addends, first, count):
        low, high = first * block_len, (first + count) * block_len
        operands = [inverse[low:high], kv_bias, cos[low:high], sin[low:high]]
        return pl.pallas_call(
            functools.partial(kv_kernel, addend_count),
            grid=(1,),
            in_specs=[whole(x) for x in operands] + [lead(x) for x in addends],
            out_specs=pl.BlockSpec((high - low, kv_width), lambda i: (0, 0)),
            out_shape=jax.ShapeDtypeStruct((high - low, kv_width), bf16),
            compiler_params=pltpu.CompilerParams(vmem_limit_bytes=16 * 2**20),
            name="finish_kv",
        )(*operands, *addends)

    early = [(0, STEMS)]
    late = [(STEMS, blocks)]
    first = Halving(project(early, [0]))
    first.step()
    second = Halving(project(early, [1], first.send))
    second.step()
    first.rest(second.send)

    squares = jnp.sum(jnp.square(raw.astype(f32)), -1).reshape(blocks, block_len)
    squares = tie(squares, first.send)
    bit = 1
    while bit < lines:
        squares = squares + swap(squares, "fsdp", bit)
        bit *= 2
    inverse = lax.rsqrt(squares / features + 1e-06).reshape(tokens)
    inverse = jnp.broadcast_to(inverse[:, None], (tokens, HD))

    for block in range(STEMS, blocks):
        held[block] = {j: tie(piece, second.send) for j, piece in held[block].items()}
        held[block] = last_bit(held[block])
    third = Halving(project(late, [0, 1], first.send))
    third.step()
    first.addends[-1] = tie(first.addends[-1], third.send)
    stem_kv = finish_kv(first.addends, 0, STEMS)

    tour = [groups << i for i in reversed(range(bits_of(lines)))]
    tour += [1 << i for i in range(bits_of(groups))]
    stems = stem_kv[None]
    came = swap(stems, "branch", tour[0])
    second.add(stem_kv, w_rows[2][-1])
    fourth = Halving(project(early + late, [2], second.send))
    for step, bit in enumerate(tour[1:]):
        stems = jnp.concatenate([stems, tie(came, third.send if step else fourth.send)], 0)
        came = swap(stems, "branch", bit)
        if step == 0:
            second.step(stems)
            fourth.step(stems)
            third.add(stems)
            third.step()
    second.rest()
    third.rest()
    fourth.rest(stems, second.came)
    stems = jnp.concatenate([stems, came], 0)
    third.addends[-1] = tie(third.addends[-1], fourth.send)
    late_kv = finish_kv(third.addends, STEMS, blocks - STEMS)
    second_sums, third_sums, fourth_sums = second.addends, third.addends, fourth.addends

    def attend(heads, first_head, parts, sums, output):
        operands = [
            inverse, query_bias[None, first_head * HD : (first_head + heads) * HD], cos, sin,
            stems, stem_kv, late_kv,
        ]
        in_specs = [smem] * 3 + [whole(x) for x in operands]
        for addends in sums:
            operands += addends
            in_specs += [lead(x) for x in addends]
        aliases = {}
        if output is not None:
            aliases = {3 + len(operands): 0}
            operands.append(output)
            in_specs.append(anywhere)
        kernel = functools.partial(
            attend_kernel, far_slots, block_len, blocks, heads, first_head, parts, addend_count,
            len(aliases), tour,
        )
        keys = (far_slots * len(parts) + blocks) * block_len
        return pl.pallas_call(
            kernel,
            grid=(1,),
            in_specs=in_specs,
            out_specs=anywhere,
            scratch_shapes=[
                pltpu.VMEM((far_slots * block_len, HD), bf16),
                pltpu.VMEM((far_slots * block_len, HD), bf16),
                pltpu.VMEM((8, far_slots * block_len), f32),
                pltpu.VMEM((tokens, heads * HD), bf16),
                pltpu.SemaphoreType.DMA((blocks,)),
            ],
            out_shape=jax.ShapeDtypeStruct((tokens, columns), bf16),
            input_output_aliases=aliases,
            compiler_params=pltpu.CompilerParams(vmem_limit_bytes=40 * 2**20),
            cost_estimate=pl.CostEstimate(
                flops=4 * tokens * heads * keys * HD,
                bytes_accessed=2 * tokens * heads * HD,
                transcendentals=tokens * heads * keys,
            ),
            name="attend",
        )(device_id, parents, lengths, *operands)

    output = attend(
        head_cuts[1], 0, [(0, STEMS, 0), (STEMS, blocks - STEMS, kv_width)],
        [second_sums, third_sums], None,
    )
    output = attend(
        head_count - head_cuts[1], head_cuts[1], [(0, blocks, 0)], [fourth_sums], output
    )
    return output.reshape(blocks, block_len, columns)


def solution(mesh):
    return jax.shard_map(
        shards,
        mesh=mesh,
        in_specs=(
            P("branch", None, "fsdp"),
            P(),
            P(),
            P(),
            P("branch", "fsdp"),
            P("branch", "fsdp"),
            P("branch", "fsdp"),
            P("fsdp"),
            P("fsdp"),
            P("fsdp"),
        ),
        out_specs=P("branch", None, "fsdp"),
        check_vma=False,
    )
```

```python
import functools
import math

import jax
import jax.numpy as jnp
from jax import lax
from jax.experimental import pallas as pl
from jax.experimental.pallas import tpu as pltpu
from jax.sharding import PartitionSpec as P

HD = 128
STEMS = 2
THETA = 1000000.0
NEG = -1e30


def bits_of(count):
    return count.bit_length() - 1


def tie(array, *others):
    return lax.optimization_barrier((array,) + others)[0]


def far_chain(parents_ref, first_block, far_slots):
    cursor = parents_ref[first_block]
    ids = []
    total = jnp.int32(0)
    for level in range(far_slots):
        ids.append(cursor)
        total = total + jnp.where(cursor >= 0, 1, 0)
        above = parents_ref[jnp.maximum(cursor, 0)]
        cursor = jnp.where(cursor >= 0, above, -1)
    return ids, total


def add_up(refs, inverse, bias, columns):
    total = refs[0][0, :, columns]
    for ref in refs[1:]:
        total = total + ref[0, :, columns].astype(jnp.float32)
    repeats = total.shape[1] // HD
    inverse = jnp.concatenate([inverse] * repeats, 1)
    return jnp.where(inverse > 0, total * inverse, 0.0) + bias


def turn(vectors, cos, sin):
    half = vectors.shape[-1] // 2
    return vectors * cos + pltpu.roll(vectors, half, 1) * sin


def table_kernel(far_slots, blocks, block_len, device_ref, parents_ref, cos_ref, sin_ref):
    tokens = cos_ref.shape[0]
    unused, far_total = far_chain(parents_ref, device_ref[0] * blocks, far_slots)
    rows = lax.broadcasted_iota(jnp.int32, (tokens, HD), 0)
    lanes = lax.broadcasted_iota(jnp.int32, (tokens, HD), 1)
    front = lanes < HD // 2
    pair = jnp.where(front, lanes, lanes - HD // 2).astype(jnp.float32)
    freqs = jnp.exp(pair * (-2.0 * math.log(THETA) / HD))
    angles = (rows + far_total * block_len).astype(jnp.float32) * freqs
    sin = jnp.sin(angles)
    cos_ref[...] = jnp.cos(angles)
    sin_ref[...] = jnp.where(front, -sin, sin)


def assemble(lines, blocks, place_ref, pieces, held, sems):
    half = lines // 2
    block_len = pieces[0].shape[0]
    copies = []
    for i in range(lines):
        target = lax.bitwise_xor(jnp.int32(i), place_ref[0])
        slot = jnp.where(target % 2 == 0, half, 0) + target // 2
        for block in range(blocks):
            begin = pl.multiple_of((slot * blocks + block) * block_len, block_len)
            n = i * blocks + block
            there = held.at[pl.ds(begin, block_len)]
            copies.append(pltpu.make_async_copy(pieces[n], there, sems.at[n]))
    for copy in copies:
        copy.start()
    return copies


def project_kernel(lines, groups, chunks, counts, fresh, place_ref, *refs):
    fresh_count = lines * counts[-1] if fresh else 0
    whole_count = len(counts) - (1 if fresh else 0)
    wholes = list(refs[:whole_count])
    pieces = refs[whole_count : whole_count + fresh_count]
    refs = refs[whole_count + fresh_count :]
    weights = refs[: groups * chunks]
    outs = refs[groups * chunks :]
    send_ref, keep_ref = outs[:2]
    if fresh:
        held, sems = outs[2:]
        for copy in assemble(lines, counts[-1], place_ref, pieces, held, sems):
            copy.wait()
        wholes.append(held)
    half = lines // 2
    rows = weights[0].shape[0]
    length = send_ref.shape[1]
    begin = 0
    for held, count in zip(wholes, counts):
        share = held.shape[0] // lines
        middle = half * share
        start = 0
        for chunk in range(chunks):
            width = weights[chunk * groups].shape[1]
            for out_ref, low in ((send_ref, 0), (keep_ref, middle)):
                total = None
                for g in range(groups):
                    member = lax.bitwise_xor(place_ref[1], jnp.int32(g))
                    lanes = pl.ds(pl.multiple_of(member * rows, rows), rows)
                    term = jnp.dot(
                        held[low : low + middle, lanes],
                        weights[chunk * groups + g][...],
                        preferred_element_type=jnp.float32,
                    )
                    total = term if total is None else total + term
                total = total.astype(out_ref.dtype).reshape(half, share, width)
                out_ref[:, begin : begin + share, start : start + width] = total
            start += width
        begin += share


def kv_kernel(addends, inverse_ref, bias_ref, cos_ref, sin_ref, *refs):
    kv_ref = refs[-1]
    both = add_up(refs[:addends], inverse_ref[...], bias_ref[...], slice(0, 2 * HD))
    kv_ref[:, :HD] = turn(both[:, :HD], cos_ref[...], sin_ref[...]).astype(jnp.bfloat16)
    kv_ref[:, HD:] = both[:, HD:].astype(jnp.bfloat16)


def attend_kernel(
    far_slots, block_len, blocks, heads, first_head, parts, addends, aliased, tour, device_ref,
    parents_ref, lengths_ref, inverse_ref, bias_ref, cos_ref, sin_ref, stems_ref, *refs,
):
    keys = refs[:2]
    refs = refs[2:]
    sums = [refs[p * addends : (p + 1) * addends] for p in range(len(parts))]
    refs = refs[len(parts) * addends + aliased :]
    out_ref, far_key, far_value, far_mask, held, sems = refs
    device = device_ref[0]
    first_block = device * blocks
    ids, unused = far_chain(parents_ref, first_block, far_slots)
    for level in range(far_slots):
        live = ids[level] >= 0
        safe = jnp.maximum(ids[level], 0)
        owner = lax.div(safe, jnp.int32(blocks))
        inner = lax.rem(safe, jnp.int32(blocks))
        apart = lax.bitwise_xor(owner, device)
        where = jnp.int32(0)
        for step, bit in enumerate(tour):
            where = where + jnp.where(lax.bitwise_and(apart, bit) != 0, 1 << step, 0)
        start = pl.multiple_of(inner * block_len, block_len)
        here = pl.ds(level * block_len, block_len)
        far_key[here, :] = stems_ref[where, pl.ds(start, block_len), :HD]
        far_value[here, :] = stems_ref[where, pl.ds(start, block_len), HD:]
        far_mask[:, here] = jnp.broadcast_to(jnp.where(live, 0.0, NEG), (8, block_len))

    factor = HD ** (-0.5) * math.log2(math.e)
    contract = (((1,), (1,)), ((), ()))
    rows = heads * block_len
    column = lax.broadcasted_iota(jnp.int32, (rows, block_len), 1)
    row = lax.broadcasted_iota(jnp.int32, (rows, block_len), 0) % block_len
    near = [(keys[0], block * block_len) for block in range(STEMS)]
    near += [(keys[1], (block - STEMS) * block_len) for block in range(STEMS, blocks)]
    copies = []
    for p, (first, count, offset) in enumerate(parts):
        for inside in range(count):
            block = first + inside
            here = slice(block * block_len, (block + 1) * block_len)
            mine = slice(inside * block_len, (inside + 1) * block_len)
            total = sums[p][0][0, mine, offset : offset + heads * HD]
            for ref in sums[p][1:]:
                total = total + ref[0, mine, offset : offset + heads * HD].astype(jnp.float32)
            inverse = inverse_ref[here]
            query = []
            for head in range(heads):
                lanes = slice(head * HD, (head + 1) * HD)
                one = jnp.where(inverse > 0, total[:, lanes] * inverse, 0.0)
                one = one + bias_ref[:, lanes]
                query.append(turn(one, cos_ref[here], sin_ref[here]).astype(jnp.bfloat16))
            query = jnp.concatenate(query, 0)
            far = lax.dot_general(
                query, far_key[...], contract, preferred_element_type=jnp.float32
            )
            scores = [far + far_mask[0:1, :]]
            for other in range(block + 1):
                ref, begin = near[other]
                score = lax.dot_general(
                    query,
                    ref[begin : begin + block_len, :HD],
                    contract,
                    preferred_element_type=jnp.float32,
                )
                if other == block or other >= STEMS:
                    seen = column < lengths_ref[first_block + other]
                    if other == block:
                        seen = seen & (column <= row)
                    score = jnp.where(seen, score, NEG)
                scores.append(score)
            peak = functools.reduce(
                jnp.maximum, [jnp.max(score, -1, keepdims=True) for score in scores]
            )
            peak = peak * factor
            exps = [jnp.exp2(score * factor - peak) for score in scores]
            total = functools.reduce(jnp.add, [jnp.sum(e, -1, keepdims=True) for e in exps])
            output = jnp.dot(
                exps[0].astype(jnp.bfloat16), far_value[...], preferred_element_type=jnp.float32
            )
            for other in range(block + 1):
                ref, begin = near[other]
                output += jnp.dot(
                    exps[1 + other].astype(jnp.bfloat16),
                    ref[begin : begin + block_len, HD:],
                    preferred_element_type=jnp.float32,
                )
            output = output / total
            if block >= STEMS:
                output = jnp.where(row < lengths_ref[first_block + block], output, 0.0)
            output = output.astype(jnp.bfloat16)
            for head in range(heads):
                lanes = slice(head * HD, (head + 1) * HD)
                held[here, lanes] = output[head * block_len : (head + 1) * block_len]
            copy = pltpu.make_async_copy(
                held.at[pl.ds(block * block_len, block_len)],
                out_ref.at[pl.ds(block * block_len, block_len), pl.ds(first_head * HD, heads * HD)],
                sems.at[block],
            )
            copy.start()
            copies.append(copy)
    for copy in copies:
        copy.wait()


def shards(
    hidden, parents, lengths, gain, w_query, w_key, w_value, query_bias, key_bias, value_bias
):
    blocks, block_len, feature_part = hidden.shape
    tokens = blocks * block_len
    features = gain.shape[0]
    rows = w_query.shape[0]
    columns = w_query.shape[1]
    head_count = columns // HD
    lines = lax.axis_size("fsdp")
    branches = lax.axis_size("branch")
    groups = branches // lines
    far_slots = STEMS * bits_of(branches)
    part = lax.axis_index("fsdp")
    device = lax.axis_index("branch")
    bf16 = jnp.bfloat16
    f32 = jnp.float32
    half_lines = lines // 2
    top = bits_of(half_lines)
    kv_width = 2 * HD

    def swap(array, axis, bit):
        size = lax.axis_size(axis)
        return lax.ppermute(array, axis, [(i, i ^ bit) for i in range(size)])

    def spread(index):
        return ((index & 1) << top) | (index >> 1)

    smem = pl.BlockSpec(memory_space=pltpu.SMEM)
    vmem = pl.BlockSpec(memory_space=pltpu.VMEM)
    anywhere = pl.BlockSpec(memory_space=pl.ANY)
    device_id = device.astype(jnp.int32)[None]
    place = jnp.stack([spread(part), device % groups]).astype(jnp.int32)

    raw = hidden.reshape(tokens, feature_part)
    gain_part = lax.dynamic_slice_in_dim(gain, part * feature_part, feature_part)

    def column(z, feature):
        return (z ^ feature) & (half_lines - 1)

    def middle(z, feature):
        return (column(z, feature) << 1) | ((feature >> top) ^ (z & 1))

    def landing(z, feature):
        return (column(z, feature) << 1) | ((z ^ feature) >> top)

    first_hop = []
    second_hop = []
    for z in range(lines):
        for g in range(groups):
            for feature in range(lines):
                here = z * groups + g
                there = feature * groups + g
                stop = middle(z, feature) * branches + here
                first_hop.append((feature * branches + here, stop))
                second_hop.append((stop, landing(z, feature) * branches + there))
    axes = ("fsdp", "branch")
    head_cuts = [0, (3 * head_count + 3) // 4, head_count]
    w_chunks = [jnp.concatenate([w_key, w_value], 1)] + [
        lax.slice_in_dim(w_query, low * HD, high * HD, axis=1)
        for low, high in zip(head_cuts, head_cuts[1:])
    ]

    cos, sin = pl.pallas_call(
        functools.partial(table_kernel, far_slots, blocks, block_len),
        in_specs=[smem, smem],
        out_specs=[vmem, vmem],
        out_shape=[jax.ShapeDtypeStruct((tokens, HD), f32)] * 2,
        name="tables",
    )(device_id, parents)

    sent = []
    for block in range(blocks):
        piece = (hidden[block].astype(f32) * gain_part).astype(bf16)
        piece = tie(piece, sent[-1], cos, sin, *w_chunks) if block else piece
        sent.append(lax.ppermute(piece, axes, first_hop))

    last_sent = sent[-1]
    sent = [lax.ppermute(piece, axes, second_hop) for piece in sent]
    w_rows = [None] * len(w_chunks)
    arrived = None
    for c in (1, 0, 2):
        outgoing = w_chunks[c] if arrived is None else tie(w_chunks[c], arrived, sent[1])
        w_rows[c] = [w_chunks[c]] + [swap(outgoing, "branch", j) for j in range(1, groups)]
        arrived = w_rows[c][-1]

    sent[0] = tie(sent[0], last_sent)
    sent[1] = tie(sent[1], w_rows[1][-1])
    last_sent = sent[-1]
    held = [{0: piece} for piece in sent]
    bit = half_lines
    while bit > 1:
        for piece in held:
            for j in list(piece):
                piece[j | bit] = swap(piece[j], "fsdp", bit)
        bit //= 2

    squares = jnp.sum(jnp.square(raw.astype(f32)), -1).reshape(blocks, block_len)
    squares = tie(squares, held[0][half_lines])
    bit = 1
    while bit < lines:
        squares = squares + swap(squares, "fsdp", bit)
        bit *= 2
    inverse = lax.rsqrt(squares / features + 1e-06).reshape(tokens)
    inverse = jnp.broadcast_to(inverse[:, None], (tokens, HD))

    def last_bit(piece):
        for j in list(piece):
            piece[j | 1] = swap(piece[j], "fsdp", 1)
        return [piece[j] for j in sorted(piece, key=spread)]

    assembled = {}
    held[0] = last_bit(held[0])
    held[1][half_lines] = tie(held[1][half_lines], w_rows[0][-1])
    held[1] = last_bit(held[1])

    def project(spans, chunks, *after):
        weights = [w for chunk in chunks for w in w_rows[chunk]]
        width = sum(w_chunks[chunk].shape[1] for chunk in chunks)
        fresh = spans[-1] not in assembled
        counts = [high - low for low, high in spans]
        wholes = [assembled[span] for span in spans if span in assembled]
        pieces = []
        if fresh:
            pieces = [held[block][i] for i in range(lines) for block in range(*spans[-1])]
        operands = wholes + pieces
        operands[0] = tie(operands[0], *after) if after else operands[0]
        length = sum(counts) * block_len
        out_specs = [vmem, vmem]
        out_shape = [
            jax.ShapeDtypeStruct((half_lines, length, width), bf16),
            jax.ShapeDtypeStruct((half_lines, length, width), f32),
        ]
        scratch = []
        if fresh:
            out_specs.append(vmem)
            out_shape.append(
                jax.ShapeDtypeStruct((lines * counts[-1] * block_len, feature_part), bf16)
            )
            scratch.append(pltpu.SemaphoreType.DMA((len(pieces),)))
        results = pl.pallas_call(
            functools.partial(project_kernel, lines, groups, len(chunks), counts, fresh),
            in_specs=[smem] + [vmem] * len(wholes) + [anywhere] * len(pieces)
            + [vmem] * len(weights),
            out_specs=out_specs,
            out_shape=out_shape,
            scratch_shapes=scratch,
            compiler_params=pltpu.CompilerParams(vmem_limit_bytes=24 * 2**20),
            cost_estimate=pl.CostEstimate(flops=0, bytes_accessed=0, transcendentals=0),
            name="project",
        )(place, *operands, *weights)
        if fresh:
            assembled[spans[-1]] = results[2]
        return results[0], results[1]

    class Halving:
        def __init__(self, partial):
            self.send, self.total = partial
            self.addends = [self.total]
            self.bit = 1

        def step(self, *after):
            send = tie(self.send, *after) if after else self.send
            self.came = swap(send, "branch", self.bit * groups)
            self.addends.append(self.came)
            self.bit *= 2

        def add(self, *after):
            self.came = tie(self.came, *after) if after else self.came
            self.addends[-1] = self.came
            total = self.total + self.came.astype(f32)
            self.send = total[1::2].astype(bf16)
            self.total = total[0::2]

        def rest(self, *after):
            while self.bit < lines:
                self.add(*after)
                self.step()

    addend_count = 1 + bits_of(lines)

    def lead(array):
        return pl.BlockSpec((1,) + array.shape[1:], lambda i: (0, 0, 0))

    def whole(array):
        return pl.BlockSpec(array.shape, lambda i: (0,) * array.ndim)

    kv_bias = jnp.concatenate([key_bias, value_bias])[None]

    def finish_kv(addends, first, count):
        low, high = first * block_len, (first + count) * block_len
        operands = [inverse[low:high], kv_bias, cos[low:high], sin[low:high]]
        return pl.pallas_call(
            functools.partial(kv_kernel, addend_count),
            grid=(1,),
            in_specs=[whole(x) for x in operands] + [lead(x) for x in addends],
            out_specs=pl.BlockSpec((high - low, kv_width), lambda i: (0, 0)),
            out_shape=jax.ShapeDtypeStruct((high - low, kv_width), bf16),
            compiler_params=pltpu.CompilerParams(vmem_limit_bytes=16 * 2**20),
            name="finish_kv",
        )(*operands, *addends)

    early = [(0, STEMS)]
    late = [(STEMS, blocks)]
    first = Halving(project(early, [0], squares, last_sent))
    first.step()
    second = Halving(project(early, [1], first.send))
    first.rest(second.send)
    second.step(first.send)

    for block in range(STEMS, blocks):
        held[block] = {j: tie(piece, second.send) for j, piece in held[block].items()}
        held[block] = last_bit(held[block])
    third = Halving(project(late, [0, 1], first.send))
    third.step()
    first.addends[-1] = tie(first.addends[-1], third.send)
    stem_kv = finish_kv(first.addends, 0, STEMS)

    tour = [groups << i for i in reversed(range(bits_of(lines)))]
    tour += [1 << i for i in range(bits_of(groups))]
    stems = stem_kv[None]
    came = swap(stems, "branch", tour[0])
    second.add(stem_kv, w_rows[2][-1])
    fourth = Halving(project(early + late, [2], second.send))
    second.step(fourth.send)
    for step, bit in enumerate(tour[1:]):
        stems = jnp.concatenate([stems, tie(came, third.send if step else fourth.send)], 0)
        came = swap(stems, "branch", bit)
        if step == 0:
            fourth.step(stems)
            third.add(stems)
            third.step()
    second.rest()
    third.rest()
    fourth.rest(stems, second.came)
    stems = jnp.concatenate([stems, came], 0)
    third.addends[-1] = tie(third.addends[-1], fourth.send)
    late_kv = finish_kv(third.addends, STEMS, blocks - STEMS)
    second_sums, third_sums, fourth_sums = second.addends, third.addends, fourth.addends

    def attend(heads, first_head, parts, sums, output):
        operands = [
            inverse, query_bias[None, first_head * HD : (first_head + heads) * HD], cos, sin,
            stems, stem_kv, late_kv,
        ]
        in_specs = [smem] * 3 + [whole(x) for x in operands]
        for addends in sums:
            operands += addends
            in_specs += [lead(x) for x in addends]
        aliases = {}
        if output is not None:
            aliases = {3 + len(operands): 0}
            operands.append(output)
            in_specs.append(anywhere)
        kernel = functools.partial(
            attend_kernel, far_slots, block_len, blocks, heads, first_head, parts, addend_count,
            len(aliases), tour,
        )
        keys = (far_slots * len(parts) + blocks) * block_len
        return pl.pallas_call(
            kernel,
            grid=(1,),
            in_specs=in_specs,
            out_specs=anywhere,
            scratch_shapes=[
                pltpu.VMEM((far_slots * block_len, HD), bf16),
                pltpu.VMEM((far_slots * block_len, HD), bf16),
                pltpu.VMEM((8, far_slots * block_len), f32),
                pltpu.VMEM((tokens, heads * HD), bf16),
                pltpu.SemaphoreType.DMA((blocks,)),
            ],
            out_shape=jax.ShapeDtypeStruct((tokens, columns), bf16),
            input_output_aliases=aliases,
            compiler_params=pltpu.CompilerParams(vmem_limit_bytes=40 * 2**20),
            cost_estimate=pl.CostEstimate(
                flops=4 * tokens * heads * keys * HD,
                bytes_accessed=2 * tokens * heads * HD,
                transcendentals=tokens * heads * keys,
            ),
            name="attend",
        )(device_id, parents, lengths, *operands)

    output = attend(
        head_cuts[1], 0, [(0, STEMS, 0), (STEMS, blocks - STEMS, kv_width)],
        [second_sums, third_sums], None,
    )
    output = attend(
        head_count - head_cuts[1], head_cuts[1], [(0, blocks, 0)], [fourth_sums], output
    )
    return output.reshape(blocks, block_len, columns)


def solution(mesh):
    return jax.shard_map(
        shards,
        mesh=mesh,
        in_specs=(
            P("branch", None, "fsdp"),
            P(),
            P(),
            P(),
            P("branch", "fsdp"),
            P("branch", "fsdp"),
            P("branch", "fsdp"),
            P("fsdp"),
            P("fsdp"),
            P("fsdp"),
        ),
        out_specs=P("branch", None, "fsdp"),
        check_vma=False,
    )
```

```python
import functools
import math

import jax
import jax.numpy as jnp
from jax import lax
from jax.experimental import pallas as pl
from jax.experimental.pallas import tpu as pltpu
from jax.sharding import PartitionSpec as P

HD = 128
STEMS = 2
THETA = 1000000.0
NEG = -1e30


def bits_of(count):
    return count.bit_length() - 1


def tie(array, *others):
    return lax.optimization_barrier((array,) + others)[0]


def far_chain(parents_ref, first_block, far_slots):
    cursor = parents_ref[first_block]
    ids = []
    total = jnp.int32(0)
    for level in range(far_slots):
        ids.append(cursor)
        total = total + jnp.where(cursor >= 0, 1, 0)
        above = parents_ref[jnp.maximum(cursor, 0)]
        cursor = jnp.where(cursor >= 0, above, -1)
    return ids, total


def add_up(refs, inverse, bias, columns):
    total = refs[0][0, :, columns]
    for ref in refs[1:]:
        total = total + ref[0, :, columns].astype(jnp.float32)
    repeats = total.shape[1] // HD
    inverse = jnp.concatenate([inverse] * repeats, 1)
    return jnp.where(inverse > 0, total * inverse, 0.0) + bias


def turn(vectors, cos, sin):
    half = vectors.shape[-1] // 2
    return vectors * cos + pltpu.roll(vectors, half, 1) * sin


def table_kernel(far_slots, blocks, block_len, device_ref, parents_ref, cos_ref, sin_ref):
    tokens = cos_ref.shape[0]
    unused, far_total = far_chain(parents_ref, device_ref[0] * blocks, far_slots)
    rows = lax.broadcasted_iota(jnp.int32, (tokens, HD), 0)
    lanes = lax.broadcasted_iota(jnp.int32, (tokens, HD), 1)
    front = lanes < HD // 2
    pair = jnp.where(front, lanes, lanes - HD // 2).astype(jnp.float32)
    freqs = jnp.exp(pair * (-2.0 * math.log(THETA) / HD))
    angles = (rows + far_total * block_len).astype(jnp.float32) * freqs
    sin = jnp.sin(angles)
    cos_ref[...] = jnp.cos(angles)
    sin_ref[...] = jnp.where(front, -sin, sin)


def assemble(lines, blocks, place_ref, pieces, held, sems):
    half = lines // 2
    block_len = pieces[0].shape[0]
    copies = []
    for i in range(lines):
        target = lax.bitwise_xor(jnp.int32(i), place_ref[0])
        slot = jnp.where(target % 2 == 0, half, 0) + target // 2
        for block in range(blocks):
            begin = pl.multiple_of((slot * blocks + block) * block_len, block_len)
            n = i * blocks + block
            there = held.at[pl.ds(begin, block_len)]
            copies.append(pltpu.make_async_copy(pieces[n], there, sems.at[n]))
    for copy in copies:
        copy.start()
    return copies


def project_kernel(lines, groups, chunks, counts, fresh, place_ref, *refs):
    fresh_count = lines * counts[-1] if fresh else 0
    whole_count = len(counts) - (1 if fresh else 0)
    wholes = list(refs[:whole_count])
    pieces = refs[whole_count : whole_count + fresh_count]
    refs = refs[whole_count + fresh_count :]
    weights = refs[: groups * chunks]
    outs = refs[groups * chunks :]
    send_ref, keep_ref = outs[:2]
    if fresh:
        held, sems = outs[2:]
        for copy in assemble(lines, counts[-1], place_ref, pieces, held, sems):
            copy.wait()
        wholes.append(held)
    half = lines // 2
    rows = weights[0].shape[0]
    length = send_ref.shape[1]
    begin = 0
    for held, count in zip(wholes, counts):
        share = held.shape[0] // lines
        middle = half * share
        start = 0
        for chunk in range(chunks):
            width = weights[chunk * groups].shape[1]
            for out_ref, low in ((send_ref, 0), (keep_ref, middle)):
                total = None
                for g in range(groups):
                    member = lax.bitwise_xor(place_ref[1], jnp.int32(g))
                    lanes = pl.ds(pl.multiple_of(member * rows, rows), rows)
                    term = jnp.dot(
                        held[low : low + middle, lanes],
                        weights[chunk * groups + g][...],
                        preferred_element_type=jnp.float32,
                    )
                    total = term if total is None else total + term
                total = total.astype(out_ref.dtype).reshape(half, share, width)
                out_ref[:, begin : begin + share, start : start + width] = total
            start += width
        begin += share


def kv_kernel(addends, inverse_ref, bias_ref, cos_ref, sin_ref, *refs):
    kv_ref = refs[-1]
    both = add_up(refs[:addends], inverse_ref[...], bias_ref[...], slice(0, 2 * HD))
    kv_ref[:, :HD] = turn(both[:, :HD], cos_ref[...], sin_ref[...]).astype(jnp.bfloat16)
    kv_ref[:, HD:] = both[:, HD:].astype(jnp.bfloat16)


def attend_kernel(
    far_slots, block_len, blocks, heads, first_head, parts, addends, aliased, tour, device_ref,
    parents_ref, lengths_ref, inverse_ref, bias_ref, cos_ref, sin_ref, stems_ref, *refs,
):
    keys = refs[:2]
    refs = refs[2:]
    sums = [refs[p * addends : (p + 1) * addends] for p in range(len(parts))]
    refs = refs[len(parts) * addends + aliased :]
    out_ref, far_key, far_value, far_mask, held, sems = refs
    device = device_ref[0]
    first_block = device * blocks
    ids, unused = far_chain(parents_ref, first_block, far_slots)
    for level in range(far_slots):
        live = ids[level] >= 0
        safe = jnp.maximum(ids[level], 0)
        owner = lax.div(safe, jnp.int32(blocks))
        inner = lax.rem(safe, jnp.int32(blocks))
        apart = lax.bitwise_xor(owner, device)
        where = jnp.int32(0)
        for step, bit in enumerate(tour):
            where = where + jnp.where(lax.bitwise_and(apart, bit) != 0, 1 << step, 0)
        start = pl.multiple_of(inner * block_len, block_len)
        here = pl.ds(level * block_len, block_len)
        far_key[here, :] = stems_ref[where, pl.ds(start, block_len), :HD]
        far_value[here, :] = stems_ref[where, pl.ds(start, block_len), HD:]
        far_mask[:, here] = jnp.broadcast_to(jnp.where(live, 0.0, NEG), (8, block_len))

    factor = HD ** (-0.5) * math.log2(math.e)
    contract = (((1,), (1,)), ((), ()))
    rows = heads * block_len
    column = lax.broadcasted_iota(jnp.int32, (rows, block_len), 1)
    row = lax.broadcasted_iota(jnp.int32, (rows, block_len), 0) % block_len
    near = [(keys[0], block * block_len) for block in range(STEMS)]
    near += [(keys[1], (block - STEMS) * block_len) for block in range(STEMS, blocks)]
    copies = []
    for p, (first, count, offset) in enumerate(parts):
        for inside in range(count):
            block = first + inside
            here = slice(block * block_len, (block + 1) * block_len)
            mine = slice(inside * block_len, (inside + 1) * block_len)
            total = sums[p][0][0, mine, offset : offset + heads * HD]
            for ref in sums[p][1:]:
                total = total + ref[0, mine, offset : offset + heads * HD].astype(jnp.float32)
            inverse = inverse_ref[here]
            query = []
            for head in range(heads):
                lanes = slice(head * HD, (head + 1) * HD)
                one = jnp.where(inverse > 0, total[:, lanes] * inverse, 0.0)
                one = one + bias_ref[:, lanes]
                query.append(turn(one, cos_ref[here], sin_ref[here]).astype(jnp.bfloat16))
            query = jnp.concatenate(query, 0)
            far = lax.dot_general(
                query, far_key[...], contract, preferred_element_type=jnp.float32
            )
            scores = [far + far_mask[0:1, :]]
            for other in range(block + 1):
                ref, begin = near[other]
                score = lax.dot_general(
                    query,
                    ref[begin : begin + block_len, :HD],
                    contract,
                    preferred_element_type=jnp.float32,
                )
                if other == block or other >= STEMS:
                    seen = column < lengths_ref[first_block + other]
                    if other == block:
                        seen = seen & (column <= row)
                    score = jnp.where(seen, score, NEG)
                scores.append(score)
            peak = functools.reduce(
                jnp.maximum, [jnp.max(score, -1, keepdims=True) for score in scores]
            )
            peak = peak * factor
            exps = [jnp.exp2(score * factor - peak) for score in scores]
            total = functools.reduce(jnp.add, [jnp.sum(e, -1, keepdims=True) for e in exps])
            output = jnp.dot(
                exps[0].astype(jnp.bfloat16), far_value[...], preferred_element_type=jnp.float32
            )
            for other in range(block + 1):
                ref, begin = near[other]
                output += jnp.dot(
                    exps[1 + other].astype(jnp.bfloat16),
                    ref[begin : begin + block_len, HD:],
                    preferred_element_type=jnp.float32,
                )
            output = output / total
            if block >= STEMS:
                output = jnp.where(row < lengths_ref[first_block + block], output, 0.0)
            output = output.astype(jnp.bfloat16)
            for head in range(heads):
                lanes = slice(head * HD, (head + 1) * HD)
                held[here, lanes] = output[head * block_len : (head + 1) * block_len]
            copy = pltpu.make_async_copy(
                held.at[pl.ds(block * block_len, block_len)],
                out_ref.at[pl.ds(block * block_len, block_len), pl.ds(first_head * HD, heads * HD)],
                sems.at[block],
            )
            copy.start()
            copies.append(copy)
    for copy in copies:
        copy.wait()


def shards(
    hidden, parents, lengths, gain, w_query, w_key, w_value, query_bias, key_bias, value_bias
):
    blocks, block_len, feature_part = hidden.shape
    tokens = blocks * block_len
    features = gain.shape[0]
    rows = w_query.shape[0]
    columns = w_query.shape[1]
    head_count = columns // HD
    lines = lax.axis_size("fsdp")
    branches = lax.axis_size("branch")
    groups = branches // lines
    far_slots = STEMS * bits_of(branches)
    part = lax.axis_index("fsdp")
    device = lax.axis_index("branch")
    bf16 = jnp.bfloat16
    f32 = jnp.float32
    half_lines = lines // 2
    top = bits_of(half_lines)
    kv_width = 2 * HD

    def swap(array, axis, bit):
        size = lax.axis_size(axis)
        return lax.ppermute(array, axis, [(i, i ^ bit) for i in range(size)])

    def spread(index):
        return ((index & 1) << top) | (index >> 1)

    smem = pl.BlockSpec(memory_space=pltpu.SMEM)
    vmem = pl.BlockSpec(memory_space=pltpu.VMEM)
    anywhere = pl.BlockSpec(memory_space=pl.ANY)
    device_id = device.astype(jnp.int32)[None]
    place = jnp.stack([spread(part), device % groups]).astype(jnp.int32)

    raw = hidden.reshape(tokens, feature_part)
    gain_part = lax.dynamic_slice_in_dim(gain, part * feature_part, feature_part)

    def column(z, feature):
        return (z ^ feature) & (half_lines - 1)

    def middle(z, feature):
        return (column(z, feature) << 1) | ((feature >> top) ^ (z & 1))

    def landing(z, feature):
        return (column(z, feature) << 1) | ((z ^ feature) >> top)

    first_hop = []
    second_hop = []
    for z in range(lines):
        for g in range(groups):
            for feature in range(lines):
                here = z * groups + g
                there = feature * groups + g
                stop = middle(z, feature) * branches + here
                first_hop.append((feature * branches + here, stop))
                second_hop.append((stop, landing(z, feature) * branches + there))
    axes = ("fsdp", "branch")
    head_cuts = [0, (5 * head_count + 7) // 8, head_count]
    w_chunks = [jnp.concatenate([w_key, w_value], 1)] + [
        lax.slice_in_dim(w_query, low * HD, high * HD, axis=1)
        for low, high in zip(head_cuts, head_cuts[1:])
    ]

    cos, sin = pl.pallas_call(
        functools.partial(table_kernel, far_slots, blocks, block_len),
        in_specs=[smem, smem],
        out_specs=[vmem, vmem],
        out_shape=[jax.ShapeDtypeStruct((tokens, HD), f32)] * 2,
        name="tables",
    )(device_id, parents)

    sent = []
    for block in range(blocks):
        piece = (hidden[block].astype(f32) * gain_part).astype(bf16)
        piece = tie(piece, sent[-1], cos, sin, *w_chunks) if block else piece
        sent.append(lax.ppermute(piece, axes, first_hop))

    last_sent = sent[-1]
    sent = [lax.ppermute(piece, axes, second_hop) for piece in sent]
    w_rows = [None] * len(w_chunks)
    arrived = None
    for c in (1, 0, 2):
        outgoing = w_chunks[c] if arrived is None else tie(w_chunks[c], arrived, sent[1])
        w_rows[c] = [w_chunks[c]] + [swap(outgoing, "branch", j) for j in range(1, groups)]
        arrived = w_rows[c][-1]

    sent[0] = tie(sent[0], last_sent)
    sent[1] = tie(sent[1], w_rows[1][-1])
    last_sent = sent[-1]
    held = [{0: piece} for piece in sent]
    bit = half_lines
    while bit > 1:
        for piece in held:
            for j in list(piece):
                piece[j | bit] = swap(piece[j], "fsdp", bit)
        bit //= 2

    def last_bit(piece):
        for j in list(piece):
            piece[j | 1] = swap(piece[j], "fsdp", 1)
        return [piece[j] for j in sorted(piece, key=spread)]

    assembled = {}
    held[0] = last_bit(held[0])
    held[1] = last_bit(held[1])

    def project(spans, chunks, *after):
        weights = [w for chunk in chunks for w in w_rows[chunk]]
        width = sum(w_chunks[chunk].shape[1] for chunk in chunks)
        fresh = spans[-1] not in assembled
        counts = [high - low for low, high in spans]
        wholes = [assembled[span] for span in spans if span in assembled]
        pieces = []
        if fresh:
            pieces = [held[block][i] for i in range(lines) for block in range(*spans[-1])]
        operands = wholes + pieces
        operands[0] = tie(operands[0], *after) if after else operands[0]
        length = sum(counts) * block_len
        out_specs = [vmem, vmem]
        out_shape = [
            jax.ShapeDtypeStruct((half_lines, length, width), bf16),
            jax.ShapeDtypeStruct((half_lines, length, width), f32),
        ]
        scratch = []
        if fresh:
            out_specs.append(vmem)
            out_shape.append(
                jax.ShapeDtypeStruct((lines * counts[-1] * block_len, feature_part), bf16)
            )
            scratch.append(pltpu.SemaphoreType.DMA((len(pieces),)))
        results = pl.pallas_call(
            functools.partial(project_kernel, lines, groups, len(chunks), counts, fresh),
            in_specs=[smem] + [vmem] * len(wholes) + [anywhere] * len(pieces)
            + [vmem] * len(weights),
            out_specs=out_specs,
            out_shape=out_shape,
            scratch_shapes=scratch,
            compiler_params=pltpu.CompilerParams(vmem_limit_bytes=24 * 2**20),
            cost_estimate=pl.CostEstimate(
                flops=0,
                bytes_accessed=0,
                transcendentals=0,
            ),
            name="project",
        )(place, *operands, *weights)
        if fresh:
            assembled[spans[-1]] = results[2]
        return results[0], results[1]

    class Halving:
        def __init__(self, partial):
            self.send, self.total = partial
            self.addends = [self.total]
            self.bit = 1

        def step(self, *after):
            send = tie(self.send, *after) if after else self.send
            self.came = swap(send, "branch", self.bit * groups)
            self.addends.append(self.came)
            self.bit *= 2

        def add(self, *after):
            self.came = tie(self.came, *after) if after else self.came
            self.addends[-1] = self.came
            total = self.total + self.came.astype(f32)
            self.send = total[1::2].astype(bf16)
            self.total = total[0::2]

        def rest(self, *after):
            while self.bit < lines:
                self.add(*after)
                self.step()

    addend_count = 1 + bits_of(lines)

    def lead(array):
        return pl.BlockSpec((1,) + array.shape[1:], lambda i: (0, 0, 0))

    def whole(array):
        return pl.BlockSpec(array.shape, lambda i: (0,) * array.ndim)

    kv_bias = jnp.concatenate([key_bias, value_bias])[None]

    def finish_kv(addends, first, count):
        low, high = first * block_len, (first + count) * block_len
        operands = [inverse[low:high], kv_bias, cos[low:high], sin[low:high]]
        return pl.pallas_call(
            functools.partial(kv_kernel, addend_count),
            grid=(1,),
            in_specs=[whole(x) for x in operands] + [lead(x) for x in addends],
            out_specs=pl.BlockSpec((high - low, kv_width), lambda i: (0, 0)),
            out_shape=jax.ShapeDtypeStruct((high - low, kv_width), bf16),
            compiler_params=pltpu.CompilerParams(vmem_limit_bytes=16 * 2**20),
            name="finish_kv",
        )(*operands, *addends)

    early = [(0, STEMS)]
    late = [(STEMS, blocks)]
    first = Halving(project(early, [0]))
    first.step()
    second = Halving(project(early, [1], first.send))
    second.step()
    first.rest(second.send)

    squares = jnp.sum(jnp.square(raw.astype(f32)), -1).reshape(blocks, block_len)
    squares = tie(squares, first.send)
    bit = 1
    while bit < lines:
        squares = squares + swap(squares, "fsdp", bit)
        bit *= 2
    inverse = lax.rsqrt(squares / features + 1e-06).reshape(tokens)
    inverse = jnp.broadcast_to(inverse[:, None], (tokens, HD))

    for block in range(STEMS, blocks):
        held[block] = {j: tie(piece, second.send) for j, piece in held[block].items()}
        held[block] = last_bit(held[block])
    third = Halving(project(late, [0, 1], first.send))
    third.step()
    first.addends[-1] = tie(first.addends[-1], third.send)
    stem_kv = finish_kv(first.addends, 0, STEMS)

    tour = [groups << i for i in reversed(range(bits_of(lines)))]
    tour += [1 << i for i in range(bits_of(groups))]
    stems = stem_kv[None]
    came = swap(stems, "branch", tour[0])
    second.add(stem_kv, w_rows[2][-1])
    fourth = Halving(project(early + late, [2], second.send, came))
    second.step(came)
    for step, bit in enumerate(tour[1:]):
        stems = jnp.concatenate([stems, tie(came, third.send if step else second.send)], 0)
        came = swap(stems, "branch", bit)
        if step == 0:
            fourth.step(stems)
            third.add(stems, second.came)
            third.step()
    second.rest()
    third.rest()
    fourth.rest(stems, second.came)
    stems = jnp.concatenate([stems, came], 0)
    third.addends[-1] = tie(third.addends[-1], fourth.send)
    late_kv = finish_kv(third.addends, STEMS, blocks - STEMS)
    second_sums, third_sums, fourth_sums = second.addends, third.addends, fourth.addends

    def attend(heads, first_head, parts, sums, output):
        operands = [
            inverse, query_bias[None, first_head * HD : (first_head + heads) * HD], cos, sin,
            stems, stem_kv, late_kv,
        ]
        in_specs = [smem] * 3 + [whole(x) for x in operands]
        for addends in sums:
            operands += addends
            in_specs += [lead(x) for x in addends]
        aliases = {}
        if output is not None:
            aliases = {3 + len(operands): 0}
            operands.append(output)
            in_specs.append(anywhere)
        kernel = functools.partial(
            attend_kernel, far_slots, block_len, blocks, heads, first_head, parts, addend_count,
            len(aliases), tour,
        )
        keys = (far_slots * len(parts) + blocks) * block_len
        return pl.pallas_call(
            kernel,
            grid=(1,),
            in_specs=in_specs,
            out_specs=anywhere,
            scratch_shapes=[
                pltpu.VMEM((far_slots * block_len, HD), bf16),
                pltpu.VMEM((far_slots * block_len, HD), bf16),
                pltpu.VMEM((8, far_slots * block_len), f32),
                pltpu.VMEM((tokens, heads * HD), bf16),
                pltpu.SemaphoreType.DMA((blocks,)),
            ],
            out_shape=jax.ShapeDtypeStruct((tokens, columns), bf16),
            input_output_aliases=aliases,
            compiler_params=pltpu.CompilerParams(vmem_limit_bytes=40 * 2**20),
            cost_estimate=pl.CostEstimate(
                flops=4 * tokens * heads * keys * HD,
                bytes_accessed=2 * tokens * heads * HD,
                transcendentals=tokens * heads * keys,
            ),
            name="attend",
        )(device_id, parents, lengths, *operands)

    output = attend(
        head_cuts[1], 0, [(0, STEMS, 0), (STEMS, blocks - STEMS, kv_width)],
        [second_sums, third_sums], None,
    )
    output = attend(
        head_count - head_cuts[1], head_cuts[1], [(0, blocks, 0)], [fourth_sums], output
    )
    return output.reshape(blocks, block_len, columns)


def solution(mesh):
    return jax.shard_map(
        shards,
        mesh=mesh,
        in_specs=(
            P("branch", None, "fsdp"),
            P(),
            P(),
            P(),
            P("branch", "fsdp"),
            P("branch", "fsdp"),
            P("branch", "fsdp"),
            P("fsdp"),
            P("fsdp"),
            P("fsdp"),
        ),
        out_specs=P("branch", None, "fsdp"),
        check_vma=False,
    )
```
